32 devices in a mesh: fsdp: 8 (over z, x), tp: 4 (over y, core).
Axes of the slice: x: 2, y: 2, z: 4, core: 2. Of those that a mesh axis runs over, the one named last changes fastest.
Arguments:
- layer_input: bfloat16 [32768, 768], P(('fsdp', 'tp')), may hold values from -6 to 6
- w_qkv: bfloat16 [768, 3, 768], P('fsdp', None, 'tp'), may hold values from -0.21875 to 0.21875
- bias_qv: bfloat16 [2, 768], P(None, 'tp'), may hold values from -3 to 3
- w_out: bfloat16 [768, 768], P('tp', 'fsdp'), may hold values from -0.875 to 0.875
- bias_out: bfloat16 [768], replicated, may hold values from -2 to 2
- gain_attn: bfloat16 [768], replicated, may hold values from 0.25 to 1.75
- shift_attn: bfloat16 [768], replicated, may hold values from -2 to 2
- gain_mlp: bfloat16 [768], replicated, may hold values from 0.25 to 1.75
- shift_mlp: bfloat16 [768], replicated, may hold values from -2 to 2
- w_up: bfloat16 [768, 3072], P('fsdp', 'tp'), may hold values from -0.21875 to 0.21875
- bias_up: bfloat16 [3072], P('tp'), may hold values from -3 to 3
- w_down: bfloat16 [3072, 768], P('tp', 'fsdp'), may hold values from -0.109375 to 0.109375
- bias_down: bfloat16 [768], replicated, may hold values from -2 to 2
- cotangent: bfloat16 [32768, 768], P(('fsdp', 'tp')), may hold values from -18 to 18
Outputs:
- layer_output: bfloat16 [32768, 768], P(('fsdp', 'tp'))
- grad_input: bfloat16 [32768, 768], P(('fsdp', 'tp'))
- grad_w_qkv: float32 [768, 3, 768], P('fsdp', None, 'tp')
- grad_bias_qv: float32 [2, 768], P(None, 'tp')
- grad_w_out: float32 [768, 768], P('tp', 'fsdp')
- grad_bias_out: float32 [768], replicated
- grad_gain_attn: float32 [768], replicated
- grad_shift_attn: float32 [768], replicated
- grad_gain_mlp: float32 [768], replicated
- grad_shift_mlp: float32 [768], replicated
- grad_w_up: float32 [768, 3072], P('fsdp', 'tp')
- grad_bias_up: float32 [3072], P('tp')
- grad_w_down: float32 [3072, 768], P('tp', 'fsdp')
- grad_bias_down: float32 [768], replicated
The draws below stay inside these ranges and needn't reach their ends.
All inputs are finite; a program needn't handle non-finite values.
Results may differ from the reference program's by a relative error of at most 0.017.
Values may be sent and summed in bfloat16 or wider, within the bound.
No kernel may reach another device: no remote copies, remote signals or barrier semaphores. Data moves between devices by JAX's collectives and lax.ppermute only.
A program may use at most 192 MiB of HBM per device.

```python
import jax
import jax.numpy as jnp
from jax import lax

D = 768
HEADS = 12
HEAD_DIM = 64
FF = 3072
SEQ_LEN = 512
TOKENS = 32768


def draw_cotangent(key, part):
    ramp = jnp.arange(TOKENS, dtype=jnp.float32) / max(TOKENS - 1, 1)
    values = jnp.clip(jax.random.normal(key, (TOKENS, D), jnp.float32), -6.0, 6.0)
    return (values * jnp.power(3.0, ramp)[:, None]).astype(jnp.bfloat16)


def shard_levels(stream_key, extent, shards, least, high):
    level = 1.0
    for dim, blocks in shards:
        draws = jax.random.uniform(jax.random.fold_in(jax.random.fold_in(stream_key, 6), dim), (blocks,), jnp.float32, least / len(shards), high / len(shards))
        level = level * jnp.repeat(jnp.exp(draws), extent[dim] // blocks).reshape((-1,) + (1,) * (len(extent) - 1 - dim))
    return level


def gaussian(rng, shape, scale, limit, pieces=(), held_as=jnp.bfloat16):
    drawn = jax.random.normal(rng, shape, jnp.float32) * scale
    if len(pieces) > 0:
        drawn = shard_levels(rng, shape, pieces, -0.22, 0.18) * drawn
    return jnp.clip(drawn, min=-limit, max=limit).astype(held_as)


def setup_inputs(seed: int = 0) -> dict:
    key_list = jax.random.split(jax.random.key(seed), 15)
    return {
        "layer_input": gaussian(key_list[0], (TOKENS, D), 1.0, 6.0, ((0, 32),)),
        "w_qkv": gaussian(key_list[1], (D, 3, D), D ** -0.5, 0.21875, ((0, 8), (2, 4))),
        "bias_qv": gaussian(key_list[2], (2, D), 0.5, 3.0, ((1, 4),)),
        "w_out": gaussian(key_list[3], (D, D), (D // 16) ** -0.5, 0.875, ((0, 4), (1, 8))),
        "bias_out": gaussian(key_list[4], (D,), 0.3, 2.0),
        "gain_attn": jnp.clip(1.0 + 0.15 * jax.random.normal(key_list[5], (D,), jnp.float32), 0.25, 1.75).astype(jnp.bfloat16),
        "shift_attn": gaussian(key_list[6], (D,), 0.3, 2.0),
        "gain_mlp": jnp.clip(1.0 + 0.15 * jax.random.normal(key_list[7], (D,), jnp.float32), 0.25, 1.75).astype(jnp.bfloat16),
        "shift_mlp": gaussian(key_list[8], (D,), 0.3, 2.0),
        "w_up": gaussian(key_list[9], (D, FF), D ** -0.5, 0.21875, ((0, 8), (1, 4))),
        "bias_up": gaussian(key_list[10], (FF,), 0.5, 3.0, ((0, 4),)),
        "w_down": gaussian(key_list[11], (FF, D), FF ** -0.5, 0.109375, ((0, 4), (1, 8))),
        "bias_down": gaussian(key_list[12], (D,), 0.3, 2.0),
        "cotangent": draw_cotangent(jax.random.fold_in(key_list[14], 71), 0),
    }


@jax.custom_vjp
def low(v):
    return lax.optimization_barrier(v.astype(jnp.bfloat16)).astype(jnp.float32)

@jax.custom_vjp
def low_back(v):
    return v

def low_keep(v):
    return (low(v), None)

def low_pass(kept, grad):
    return (grad,)

def back_keep(v):
    return (v, None)

def back_low(kept, grad):
    return (low(grad),)
low.defvjp(low_keep, low_pass)
low_back.defvjp(back_keep, back_low)
HIGH = lax.Precision.HIGHEST

def normalize(rows, gain, shift):
    centre = rows - lax.optimization_barrier(jnp.mean(rows, axis=-1, keepdims=True))
    spread = lax.rsqrt(lax.optimization_barrier(jnp.mean(centre * centre, axis=-1, keepdims=True)) + 1e-05)
    return centre * spread * gain + shift

def gelu_exact(value):
    return 0.5 * value * (1.0 + lax.erf(value * 2.0 ** (-0.5)))

def attend(block):
    query, keys, values = block
    scores = jnp.einsum('qhe,khe->hqk', query, keys, precision=HIGH) * HEAD_DIM ** (-0.5)
    scores = low_back(scores)
    rows_idx = lax.broadcasted_iota(jnp.int32, (SEQ_LEN, SEQ_LEN), 0)
    cols_idx = lax.broadcasted_iota(jnp.int32, (SEQ_LEN, SEQ_LEN), 1)
    scores = jnp.where((rows_idx >= cols_idx)[None], scores, -1e+30)
    probs = low(jax.nn.softmax(scores, axis=-1))
    return jnp.einsum('hqk,khe->qhe', probs, values, precision=HIGH)

def forward(layer_input, w_qkv, bias_qv, w_out, bias_out, gain_attn, shift_attn, gain_mlp, shift_mlp, w_up, bias_up, w_down, bias_down):
    normed_one = low(normalize(layer_input, gain_attn, shift_attn))
    bias_three = jnp.stack([bias_qv[0], jnp.zeros_like(bias_qv[0]), bias_qv[1]])
    projected = jnp.einsum('td,dcf->tcf', normed_one, w_qkv, precision=HIGH) + bias_three
    projected = low(low_back(projected))
    shaped = projected.reshape(TOKENS // SEQ_LEN, SEQ_LEN, 3, HEADS, HEAD_DIM)
    mixed = lax.map(jax.checkpoint(attend), (shaped[:, :, 0], shaped[:, :, 1], shaped[:, :, 2]))
    mixed = low(low_back(mixed.reshape(TOKENS, D)))
    attended = low_back(jnp.dot(mixed, w_out, precision=HIGH) + bias_out)
    middle = layer_input + attended
    normed_two = low(normalize(middle, gain_mlp, shift_mlp))
    hidden = low(gelu_exact(low_back(jnp.dot(normed_two, w_up, precision=HIGH) + bias_up)))
    return middle + (jnp.dot(hidden, w_down, precision=HIGH) + bias_down)

def reference(layer_input, w_qkv, bias_qv, w_out, bias_out, gain_attn, shift_attn, gain_mlp, shift_mlp, w_up, bias_up, w_down, bias_down, cotangent):
    inputs = [a.astype(jnp.float32) for a in (layer_input, w_qkv, bias_qv, w_out, bias_out, gain_attn, shift_attn, gain_mlp, shift_mlp, w_up, bias_up, w_down, bias_down)]
    result, pullback = jax.vjp(forward, *inputs)
    grads = pullback(cotangent.astype(jnp.float32))
    return (result.astype(jnp.bfloat16), grads[0].astype(jnp.bfloat16), grads[1], grads[2], grads[3], grads[4], grads[5], grads[6], grads[7], grads[8], grads[9], grads[10], grads[11], grads[12])
```

```python
import functools

import jax
import jax.numpy as jnp
from jax import lax
from jax.experimental import pallas as pl
from jax.experimental.pallas import tpu as pltpu
from jax.sharding import PartitionSpec as P

HEAD_DIM = 64
SEQ_LEN = 512
HALF = 256
EPS = 1e-05
AXES = ("fsdp", "tp")
BF = jnp.bfloat16
F32 = jnp.float32
MB = 1 << 20


def dot(left, right):
    return lax.dot_general(left, right, (((1,), (0,)), ((), ())), preferred_element_type=F32)


def dot_nt(left, right):
    return lax.dot_general(left, right, (((1,), (1,)), ((), ())), preferred_element_type=F32)


def dot_tn(left, right):
    return lax.dot_general(left, right, (((0,), (0,)), ((), ())), preferred_element_type=F32)


def whole(shape):
    zeros = (0,) * len(shape)
    return pl.BlockSpec(shape, lambda *_: zeros)


def params(limit_mb):
    return pltpu.CompilerParams(vmem_limit_bytes=limit_mb * MB)


def cost(flops, nbytes, trans=0):
    return pl.CostEstimate(flops=int(flops), bytes_accessed=int(nbytes), transcendentals=int(trans))


def unit_rows(rows):
    centre = rows - jnp.mean(rows, axis=-1, keepdims=True)
    spread = lax.rsqrt(jnp.mean(centre * centre, axis=-1, keepdims=True) + EPS)
    return centre * spread, spread


def norm_back(grad_out, unit, spread, gain):
    scaled = grad_out * gain
    inner = jnp.mean(scaled * unit, axis=-1, keepdims=True)
    return spread * (scaled - jnp.mean(scaled, axis=-1, keepdims=True) - unit * inner)


def add_sum(ref, value):
    @pl.when(pl.program_id(0) == 0)
    def _():
        ref[...] = jnp.zeros_like(ref)

    ref[...] += jnp.sum(value, axis=0, keepdims=True)


def start_kernel(x_ref, cot_ref, gain_ref, shift_ref, n1_ref, n1t_ref, cott_ref, sum_ref):
    unit, _ = unit_rows(x_ref[...].astype(F32))
    normed = unit * gain_ref[...].astype(F32) + shift_ref[...].astype(F32)
    n1_ref[...] = normed.astype(BF)
    n1t_ref[...] = normed.T.astype(BF)
    cot = cot_ref[...].astype(F32)
    cott_ref[...] = cot.T.astype(BF)
    add_sum(sum_ref, cot)


def start_call(x, cot, gain, shift):
    rows, d = x.shape
    tile = 256
    by_rows = pl.BlockSpec((tile, d), lambda i: (i, 0))
    by_cols = pl.BlockSpec((d, tile), lambda i: (0, i))
    return pl.pallas_call(
        start_kernel,
        grid=(rows // tile,),
        in_specs=[by_rows, by_rows, whole((1, d)), whole((1, d))],
        out_specs=[by_rows, by_cols, by_cols, whole((1, d))],
        out_shape=[
            jax.ShapeDtypeStruct((rows, d), BF),
            jax.ShapeDtypeStruct((d, rows), BF),
            jax.ShapeDtypeStruct((d, rows), BF),
            jax.ShapeDtypeStruct((1, d), F32),
        ],
        compiler_params=params(24),
        cost_estimate=cost(0, 10 * rows * d),
        name="start",
    )(x, cot, gain, shift)


def assemble_kernel(count, place_ref, *refs):
    pieces, out_ref, sems = refs[: 2 * count], refs[2 * count], refs[2 * count + 1]
    z, x = place_ref[0], place_ref[1]
    copies = []
    for k in range(count):
        for dx in range(2):
            slot = lax.rem(z - k + count, count) * 2 + lax.rem(x + dx, 2)
            copies.append(
                pltpu.make_async_copy(
                    pieces[dx * count + k], out_ref.at[slot], sems.at[dx * count + k]
                )
            )
    for copy in copies:
        copy.start()
    for copy in copies:
        copy.wait()


def assemble(place, near, far):
    count = len(near)
    rows, cols = near[0].shape
    out = pl.pallas_call(
        functools.partial(assemble_kernel, count),
        in_specs=[pl.BlockSpec(memory_space=pltpu.SMEM)]
        + [pl.BlockSpec(memory_space=pl.ANY)] * (2 * count),
        out_specs=pl.BlockSpec(memory_space=pl.ANY),
        out_shape=jax.ShapeDtypeStruct((2 * count, rows, cols), BF),
        scratch_shapes=[pltpu.SemaphoreType.DMA((2 * count,))],
        cost_estimate=cost(0, 8 * count * rows * cols),
        name="assemble",
    )(place, *near, *far)
    return out.reshape(2 * count * rows, cols)


HEAD_PLACES = ((0, 1, 2, 0, 0), (0, 1, 2, 64, 64), (3, 4, 3, 0, 64))


def lane_keep(tile, first):
    lanes = lax.broadcasted_iota(jnp.int32, tile.shape, 1)
    keep = (lanes >= first) & (lanes < first + HEAD_DIM)
    return jnp.where(keep, tile, jnp.zeros_like(tile))


def score_block(keys, query, start, stop, first_query):
    scores = dot_nt(keys[start:stop], query)
    if stop - 1 > first_query:
        key_idx = lax.broadcasted_iota(jnp.int32, scores.shape, 0) + start
        query_idx = lax.broadcasted_iota(jnp.int32, scores.shape, 1) + first_query
        scores = jnp.where(key_idx <= query_idx, scores, -1e30)
    return scores


def attend_kernel(n1_ref, w_ref, bias_ref, proj_ref, mixed_ref, lse_ref):
    projected = (dot(n1_ref[...], w_ref[...]) + bias_ref[...]).astype(BF)
    proj_ref[...] = projected
    outs = {}
    for head, (qt, kt, vt, qk_lane, v_lane) in enumerate(HEAD_PLACES):
        query = lane_keep(projected[:, qt * 128 : qt * 128 + 128], qk_lane) * BF(0.125)
        keys = projected[:, kt * 128 : kt * 128 + 128]
        values = projected[:, vt * 128 : vt * 128 + 128]
        for block in range(2):
            first = block * HALF
            last = first + HALF
            scores = score_block(keys, query[first:last], 0, last, first)
            top = jnp.max(scores, axis=0, keepdims=True)
            weight = jnp.exp(scores - top)
            total = jnp.sum(weight, axis=0, keepdims=True)
            mixed = dot_tn(values[0:last], weight.astype(BF)) * (1.0 / total)
            outs[head, block] = mixed[v_lane : v_lane + HEAD_DIM]
            lse_ref[0, head : head + 1, first:last] = top + jnp.log(total)
    for block in range(2):
        first = block * HALF
        rows = slice(first, first + HALF)
        single = jnp.concatenate([jnp.zeros_like(outs[2, block]), outs[2, block]], axis=0)
        pair = jnp.concatenate([outs[0, block], outs[1, block]], axis=0)
        mixed_ref[rows, 0:128] = single.T.astype(BF)
        mixed_ref[rows, 128:256] = pair.T.astype(BF)


def attend_call(n1, w, bias):
    rows, d = n1.shape
    seqs = rows // SEQ_LEN
    return pl.pallas_call(
        attend_kernel,
        grid=(seqs,),
        in_specs=[
            pl.BlockSpec((SEQ_LEN, d), lambda i: (i, 0)),
            pl.BlockSpec((d, 640), lambda i: (0, 0)),
            whole((1, 640)),
        ],
        out_specs=[
            pl.BlockSpec((SEQ_LEN, 640), lambda i: (i, 0)),
            pl.BlockSpec((SEQ_LEN, 256), lambda i: (i, 0)),
            pl.BlockSpec((1, 8, SEQ_LEN), lambda i: (i, 0, 0)),
        ],
        out_shape=[
            jax.ShapeDtypeStruct((rows, 640), BF),
            jax.ShapeDtypeStruct((rows, 256), BF),
            jax.ShapeDtypeStruct((seqs, 8, SEQ_LEN), F32),
        ],
        compiler_params=params(32),
        cost_estimate=cost(6e9, 8e6),
        name="attend",
    )(n1, w, bias)


def middle_kernel(x_ref, bias_ref, gain_ref, shift_ref, *refs):
    mixed, weights, (mid_ref, n2_ref, n2t_ref) = refs[0:4], refs[4:8], refs[8:]
    attended = bias_ref[...].astype(F32)
    for m, w in zip(mixed, weights):
        attended = attended + dot_nt(m[...], w[...])
    middle = x_ref[...].astype(F32) + attended
    mid_ref[...] = middle
    unit, _ = unit_rows(middle)
    normed = unit * gain_ref[...].astype(F32) + shift_ref[...].astype(F32)
    n2_ref[...] = normed.astype(BF)
    n2t_ref[...] = normed.T.astype(BF)


def middle_call(x, bias, gain, shift, mixed, weights):
    rows, d = x.shape
    tile = 256
    by_rows = pl.BlockSpec((tile, d), lambda i: (i, 0))
    return pl.pallas_call(
        middle_kernel,
        grid=(rows // tile,),
        in_specs=[by_rows, whole((1, d)), whole((1, d)), whole((1, d))]
        + [pl.BlockSpec((tile, 256), lambda i: (i, 0))] * 4
        + [pl.BlockSpec((d, 256), lambda i: (0, 2))] * 4,
        out_specs=[by_rows, by_rows, pl.BlockSpec((d, tile), lambda i: (0, i))],
        out_shape=[
            jax.ShapeDtypeStruct((rows, d), F32),
            jax.ShapeDtypeStruct((rows, d), BF),
            jax.ShapeDtypeStruct((d, rows), BF),
        ],
        compiler_params=params(24),
        cost_estimate=cost(2 * rows * d * 1024, 16e6),
        name="middle",
    )(x, bias, gain, shift, *mixed, *weights)


def gelu_both(value):
    size = jnp.abs(value)
    frac = 1.0 / (1.0 + (0.3275911 * 2.0**-0.5) * size)
    bell = jnp.exp(-0.5 * value * value)
    series = 0.5 * 1.061405429 * frac - 0.5 * 1.453152027
    series = series * frac + 0.5 * 1.421413741
    series = series * frac - 0.5 * 0.284496736
    series = series * frac + 0.5 * 0.254829592
    tail = series * frac * bell
    cumulative = jnp.where(value < 0, tail, 1.0 - tail)
    return value * cumulative, cumulative + value * bell * (2.0 * 3.141592653589793) ** -0.5


def store_blocks(ref, place_ref, value, count):
    z, x = place_ref[0], place_ref[1]
    size = value.shape[0] // (2 * count)
    for block in range(2 * count):
        slot = lax.rem(x + block % 2, 2) * count + lax.rem(block // 2 - z + count, count)
        ref[slot] = value[block * size : (block + 1) * size].astype(BF)


def feed_kernel(count, tokens, place_ref, n2_ref, n2t_ref, cot_ref, cott_ref, *refs):
    ups, downs, biases = refs[0:2], refs[2:4], refs[4:6]
    hidden_refs, pre_refs, gup_refs, gdown_refs, sum_refs = (
        refs[6:8],
        refs[8:10],
        refs[10:12],
        refs[12:14],
        refs[14:16],
    )
    rows = n2_ref.shape[0]
    for c in range(2):
        up, down, bias = ups[c][...], downs[c][...], biases[c][...]
        total = jnp.zeros_like(bias)
        for first in range(0, rows, tokens):
            here = slice(first, first + tokens)
            pre = dot(n2_ref[here], up) + bias
            grad_hidden = dot(cot_ref[here], down)
            hidden, slope = gelu_both(pre)
            hidden_refs[c][here] = hidden.astype(BF)
            grad_pre = (grad_hidden * slope).astype(BF)
            pre_refs[c][here] = grad_pre
            total = total + jnp.sum(grad_pre.astype(F32), axis=0, keepdims=True)
        sum_refs[c][...] = total
        store_blocks(gup_refs[c], place_ref, dot(n2t_ref[...], pre_refs[c][...]), count)
        store_blocks(gdown_refs[c], place_ref, dot(cott_ref[...], hidden_refs[c][...]), count)


def feed_call(place, count, n2, n2t, cot, cott, ups, downs, biases):
    rows, d = n2.shape
    units = ups[0].shape[1]
    tile = 256
    shard = d // (2 * count)
    cols = lambda n: pl.BlockSpec((n, tile), lambda i: (0, i))
    blocks = pl.BlockSpec((2 * count, shard, tile), lambda i: (0, 0, i))
    hid = jax.ShapeDtypeStruct((rows, units), BF)
    grad = jax.ShapeDtypeStruct((2 * count, shard, units), BF)
    total = jax.ShapeDtypeStruct((1, units), F32)
    return pl.pallas_call(
        functools.partial(feed_kernel, count, 256),
        grid=(units // tile,),
        in_specs=[
            pl.BlockSpec(memory_space=pltpu.SMEM),
            whole((rows, d)),
            whole((d, rows)),
            whole((rows, d)),
            whole((d, rows)),
        ]
        + [cols(d)] * 4
        + [cols(1)] * 2,
        out_specs=[cols(rows)] * 4 + [blocks] * 4 + [cols(1)] * 2,
        out_shape=[hid] * 4 + [grad] * 4 + [total] * 2,
        compiler_params=params(48),
        cost_estimate=cost(2 * 4 * 2 * rows * d * units, 20e6, 2 * rows * units),
        name="feed",
    )(place, n2, n2t, cot, cott, *ups, *downs, *biases)


def output_kernel(mid_ref, cot_ref, bias_ref, gain_ref, *refs):
    hidden, pre, ups, downs = refs[0:4], refs[4:8], refs[8:12], refs[12:16]
    out_ref, gmid_ref, grows_ref, growst_ref, gain_sum, shift_sum, bias_sum = refs[16:]
    mlp = bias_ref[...].astype(F32)
    grad = None
    for h, w in zip(hidden, downs):
        mlp = mlp + dot_nt(h[...], w[...])
    for g, w in zip(pre, ups):
        term = dot_nt(g[...], w[...])
        grad = term if grad is None else grad + term
    middle = mid_ref[...]
    out_ref[...] = (middle + mlp).astype(BF)
    unit, spread = unit_rows(middle)
    add_sum(gain_sum, grad * unit)
    add_sum(shift_sum, grad)
    back = norm_back(grad, unit, spread, gain_ref[...].astype(F32))
    grad_middle = cot_ref[...].astype(F32) + back
    gmid_ref[...] = grad_middle
    rows = grad_middle.astype(BF)
    grows_ref[...] = rows
    growst_ref[...] = grad_middle.T.astype(BF)
    add_sum(bias_sum, rows.astype(F32))


def output_call(middle, cot, bias, gain, hidden, pre, ups, downs):
    rows, d = middle.shape
    units = ups[0].shape[1]
    tile = 256
    by_rows = pl.BlockSpec((tile, d), lambda i: (i, 0))
    kept = pl.BlockSpec((d, units), lambda i: (0, 0), pipeline_mode=pl.Buffered(1))
    total = jax.ShapeDtypeStruct((1, d), F32)
    return pl.pallas_call(
        output_kernel,
        grid=(rows // tile,),
        in_specs=[by_rows, by_rows, whole((1, d)), whole((1, d))]
        + [pl.BlockSpec((tile, units), lambda i: (i, 0))] * 8
        + [kept] * 8,
        out_specs=[by_rows] * 3 + [pl.BlockSpec((d, tile), lambda i: (0, i))] + [whole((1, d))] * 3,
        out_shape=[
            jax.ShapeDtypeStruct((rows, d), BF),
            jax.ShapeDtypeStruct((rows, d), F32),
            jax.ShapeDtypeStruct((rows, d), BF),
            jax.ShapeDtypeStruct((d, rows), BF),
            total,
            total,
            total,
        ],
        compiler_params=params(48),
        cost_estimate=cost(2 * 8 * rows * d * units, 34e6),
        name="output",
    )(middle, cot, bias, gain, *hidden, *pre, *ups, *downs)


def attend_back_kernel(
    count,
    place_ref,
    grows_ref,
    growst_ref,
    n1t_ref,
    w_ref,
    proj_ref,
    mixed_ref,
    lse_ref,
    gproj_ref,
    gw_ref,
    sum_ref,
    total,
):
    step = pl.program_id(0)
    projected = proj_ref[...]
    grad_mixed = dot(grows_ref[...], w_ref[...]).astype(BF)
    parts = {}
    for head, (qt, kt, vt, qk_lane, v_lane) in enumerate(HEAD_PLACES):
        mt = 0 if head == 2 else 1
        query = lane_keep(projected[:, qt * 128 : qt * 128 + 128], qk_lane) * BF(0.125)
        keys = projected[:, kt * 128 : kt * 128 + 128]
        values = projected[:, vt * 128 : vt * 128 + 128]
        grads = lane_keep(grad_mixed[:, mt * 128 : mt * 128 + 128], v_lane)
        gkeys, gvalues = [None, None], [None, None]
        for block in range(2):
            first = block * HALF
            last = first + HALF
            qb, gb = query[first:last], grads[first:last]
            scores = score_block(keys, qb, 0, last, first)
            probs = jnp.exp(scores - lse_ref[0, head : head + 1, first:last])
            gprobs = dot_nt(values[0:last], gb)
            both = probs * gprobs
            delta = jnp.sum(both, axis=0, keepdims=True)
            gscores = (both - probs * delta).astype(BF)
            gq = dot_tn(keys[0:last], gscores) * 0.125
            parts["q", head, block] = gq[qk_lane : qk_lane + HEAD_DIM]
            gk = dot(gscores, qb)
            gv = dot(probs.astype(BF), gb)
            for b in range(block + 1):
                part = slice(b * HALF, b * HALF + HALF)
                gkeys[b] = gk[part] if gkeys[b] is None else gkeys[b] + gk[part]
                gvalues[b] = gv[part] if gvalues[b] is None else gvalues[b] + gv[part]
        parts["k", head] = gkeys
        parts["v", head] = gvalues
    for block in range(2):
        rows = slice(block * HALF, block * HALF + HALF)
        pair = jnp.concatenate([parts["q", 0, block], parts["q", 1, block]], axis=0).T
        lone = parts["q", 2, block]
        lone = jnp.concatenate([lone, jnp.zeros_like(lone)], axis=0).T
        gproj_ref[rows, 0:128] = pair.astype(BF)
        gproj_ref[rows, 128:256] = (parts["k", 0][block] + parts["k", 1][block]).astype(BF)
        gproj_ref[rows, 256:384] = (parts["v", 0][block] + parts["v", 1][block]).astype(BF)
        gproj_ref[rows, 384:512] = (lone + parts["v", 2][block]).astype(BF)
        gproj_ref[rows, 512:640] = parts["k", 2][block].astype(BF)
    gproj = gproj_ref[...]
    add_sum(sum_ref, gproj.astype(F32))
    grad_a = dot(n1t_ref[...], gproj)
    grad_b = dot(growst_ref[...], mixed_ref[...])
    grad = jnp.concatenate(
        [grad_a[:, 0:512], grad_a[:, 512:640] + grad_b[:, 0:128], grad_b[:, 128:256]], axis=1
    )

    @pl.when(step == 0)
    def _():
        total[...] = grad

    @pl.when(step > 0)
    def _():
        total[...] += grad

    @pl.when(step == pl.num_programs(0) - 1)
    def _():
        store_blocks(gw_ref, place_ref, total[...], count)


def attend_back_call(place, count, grows, growst, n1t, w, proj, mixed, lse):
    rows, d = grows.shape
    seqs = rows // SEQ_LEN
    shard = d // (2 * count)
    by_rows = lambda n: pl.BlockSpec((SEQ_LEN, n), lambda i: (i, 0))
    by_cols = pl.BlockSpec((d, SEQ_LEN), lambda i: (0, i))
    return pl.pallas_call(
        functools.partial(attend_back_kernel, count),
        grid=(seqs,),
        in_specs=[
            pl.BlockSpec(memory_space=pltpu.SMEM),
            by_rows(d),
            by_cols,
            by_cols,
            pl.BlockSpec((d, 256), lambda i: (0, 2)),
            by_rows(640),
            by_rows(256),
            pl.BlockSpec((1, 8, SEQ_LEN), lambda i: (i, 0, 0)),
        ],
        out_specs=[by_rows(640), whole((2 * count, shard, 768)), whole((1, 640))],
        out_shape=[
            jax.ShapeDtypeStruct((rows, 640), BF),
            jax.ShapeDtypeStruct((2 * count, shard, 768), BF),
            jax.ShapeDtypeStruct((1, 640), F32),
        ],
        scratch_shapes=[pltpu.VMEM((d, 768), F32)],
        compiler_params=params(40),
        cost_estimate=cost(10e9, 12e6),
        name="attend_back",
    )(place, grows, growst, n1t, w, proj, mixed, lse)


def finish_kernel(x_ref, gmid_ref, gain_ref, *refs):
    gproj, weights, (out_ref, gain_sum, shift_sum) = refs[0:4], refs[4:8], refs[8:]
    grad = None
    for g, w in zip(gproj, weights):
        term = dot_nt(g[...], w[...])
        grad = term if grad is None else grad + term
    unit, spread = unit_rows(x_ref[...].astype(F32))
    add_sum(gain_sum, grad * unit)
    add_sum(shift_sum, grad)
    back = norm_back(grad, unit, spread, gain_ref[...].astype(F32))
    out_ref[...] = (gmid_ref[...] + back).astype(BF)


def finish_call(x, gmid, gain, gproj, weights):
    rows, d = x.shape
    tile = 256
    by_rows = pl.BlockSpec((tile, d), lambda i: (i, 0))
    total = jax.ShapeDtypeStruct((1, d), F32)
    return pl.pallas_call(
        finish_kernel,
        grid=(rows // tile,),
        in_specs=[by_rows, by_rows, whole((1, d))]
        + [pl.BlockSpec((tile, 640), lambda i: (i, 0))] * 4
        + [pl.BlockSpec((d, 640), lambda i: (0, 0))] * 4,
        out_specs=[by_rows, whole((1, d)), whole((1, d))],
        out_shape=[jax.ShapeDtypeStruct((rows, d), BF), total, total],
        compiler_params=params(32),
        cost_estimate=cost(2 * 4 * rows * d * 640, 16e6),
        name="finish",
    )(x, gmid, gain, *gproj, *weights)


class Links:
    def __init__(self, mesh):
        self.count = mesh.shape["fsdp"] // 2
        places = [
            (z, x, y, c)
            for z in range(self.count)
            for x in range(2)
            for y in range(2)
            for c in range(2)
        ]

        def index(z, x, y, c):
            return ((z * 2 + x) * 2 + y) * 2 + c

        def pairs(move):
            return [(index(*p), index(*move(*p))) for p in places]

        self.core = pairs(lambda z, x, y, c: (z, x, y, 1 - c))
        self.y = pairs(lambda z, x, y, c: (z, x, 1 - y, c))
        self.x = pairs(lambda z, x, y, c: (z, 1 - x, y, c))
        self.ring = pairs(lambda z, x, y, c: ((z + 1) % self.count, x, y, c))
        self.bits = []
        bit = 1
        while bit < self.count:
            self.bits.append(pairs(lambda z, x, y, c, b=bit: (z ^ b, x, y, c)))
            bit *= 2

    @staticmethod
    def send(value, pairs):
        return lax.ppermute(value, AXES, pairs)


def gather(links, place, shard):
    near = [shard]
    for _ in range(links.count - 1):
        near.append(links.send(near[-1], links.ring))
    far = [links.send(v, links.x) for v in near]
    own = assemble(place, near, far)
    over = links.send(own, links.y)
    return [own, links.send(own, links.core), over, links.send(over, links.core)]


def plus(a, b, kind=BF):
    return (a.astype(F32) + b.astype(F32)).astype(kind)


def scatter_pair(links, own, other):
    return plus(own, links.send(other, links.core))


def scatter_rest(links, here, there):
    n = links.count
    both = links.send(there, links.y)
    away = plus(here[n:], both[n:])
    home = plus(here[:n], both[:n])
    home = plus(home, links.send(away, links.x))
    held = home[n - 1]
    for k in range(n - 2, -1, -1):
        held = plus(home[k], links.send(held, links.ring), F32 if k == 0 else BF)
    return held


def sum_all(links, rep, groups):
    n = rep.shape[0]
    got = links.send(jnp.concatenate([rep, groups[1], groups[3]]), links.core)
    width = groups.shape[1]
    rep = rep + got[:n]
    here = groups[0] + got[n : n + width]
    there = groups[2] + got[n + width :]
    got = links.send(jnp.concatenate([rep, there]), links.y)
    vec = jnp.concatenate([rep, here]) + got
    vec = vec + links.send(vec, links.x)
    for pairs in links.bits:
        vec = vec + links.send(vec, pairs)
    return vec[:n], vec[n:]


def pack_attn(w_qkv, w_out):
    q, k, v, o = w_qkv[:, 0], w_qkv[:, 1], w_qkv[:, 2], w_out.T
    return jnp.concatenate(
        [q[:, :128], k[:, :128], v[:, :128], q[:, 128:], v[:, 128:], k[:, 128:], o[:, 128:], o[:, :128]],
        axis=1,
    )


def unpack_attn(g):
    q = jnp.concatenate([g[:, 0:128], g[:, 384:448]], axis=1)
    k = jnp.concatenate([g[:, 128:256], g[:, 512:576]], axis=1)
    v = jnp.concatenate([g[:, 256:384], g[:, 448:512]], axis=1)
    o = jnp.concatenate([g[:, 640:768], g[:, 576:640]], axis=1)
    return jnp.stack([q, k, v], axis=1), o.T


def body(
    links,
    layer_input,
    w_qkv,
    bias_qv,
    w_out,
    bias_out,
    gain_attn,
    shift_attn,
    gain_mlp,
    shift_mlp,
    w_up,
    bias_up,
    w_down,
    bias_down,
    cotangent,
):
    fsdp = lax.axis_index("fsdp")
    place = jnp.stack([fsdp // 2, fsdp % 2]).astype(jnp.int32)
    row = lambda v: v.reshape(1, -1)
    count = links.count

    small = jnp.concatenate([bias_qv[0], bias_qv[1], bias_up])
    small_y = links.send(small, links.y)
    smalls = [small, links.send(small, links.core), small_y, links.send(small_y, links.core)]
    heads = bias_qv.shape[1]

    attn_w = gather(links, place, pack_attn(w_qkv, w_out))
    up_w = gather(links, place, w_up)
    down_w = gather(links, place, w_down.T)

    n1, n1t, cott, sum_down = start_call(layer_input, cotangent, row(gain_attn), row(shift_attn))

    proj, mixed, lse = [], [], []
    for j in range(4):
        bq, bv = smalls[j][:heads].astype(F32), smalls[j][heads : 2 * heads].astype(F32)
        none = jnp.zeros((128,), F32)
        bias = jnp.concatenate([bq[:128], none, bv[:128], bq[128:], bv[128:], none])
        p, m, s = attend_call(n1, attn_w[j], row(bias))
        proj.append(p)
        mixed.append(m)
        lse.append(s)

    middle, n2, n2t = middle_call(
        layer_input, row(bias_out), row(gain_mlp), row(shift_mlp), mixed, attn_w
    )

    hidden, pre, sum_up = [None] * 4, [None] * 4, [None] * 4
    half_up, half_down = [None] * 2, [None] * 2
    for dy in (1, 0):
        js = (2 * dy, 2 * dy + 1)
        out = feed_call(
            place,
            count,
            n2,
            n2t,
            cotangent,
            cott,
            [up_w[j] for j in js],
            [down_w[j] for j in js],
            [row(smalls[j][2 * heads :].astype(F32)) for j in js],
        )
        for c, j in enumerate(js):
            hidden[j], pre[j], sum_up[j] = out[c], out[2 + c], out[8 + c]
        half_up[dy] = scatter_pair(links, out[4], out[5])
        half_down[dy] = scatter_pair(links, out[6], out[7])

    layer_output, gmid, grows, growst, gain_two, shift_two, sum_out = output_call(
        middle, cotangent, row(bias_down), row(gain_mlp), hidden, pre, up_w, down_w
    )
    grad_up = scatter_rest(links, half_up[0], half_up[1])
    grad_down = scatter_rest(links, half_down[0], half_down[1])

    gproj, gattn, sum_proj = [None] * 4, [None] * 4, [None] * 4
    for j in (3, 2, 1, 0):
        gproj[j], gattn[j], sum_proj[j] = attend_back_call(
            place, count, grows, growst, n1t, attn_w[j], proj[j], mixed[j], lse[j]
        )
    half_attn = [scatter_pair(links, gattn[2 * dy], gattn[2 * dy + 1]) for dy in range(2)]
    grad_attn = scatter_rest(links, half_attn[0], half_attn[1])

    grad_input, gain_one, shift_one = finish_call(
        layer_input, gmid, row(gain_attn), gproj, attn_w
    )

    d = layer_input.shape[1]
    groups = []
    for j in range(4):
        s = sum_proj[j][0]
        groups.append(
            jnp.concatenate([s[0:128], s[384:448], s[256:384], s[448:512], sum_up[j][0]])
        )
    rep = jnp.concatenate(
        [v[0] for v in (sum_out, sum_down, gain_one, shift_one, gain_two, shift_two)]
    )
    rep, own = sum_all(links, rep, jnp.stack(groups))
    total_out, total_down, gain_one, shift_one, gain_two, shift_two = rep.reshape(6, d)
    total_qv, total_up = own[: 2 * heads].reshape(2, heads), own[2 * heads :]

    shard_qkv, shard_out = unpack_attn(grad_attn)
    return (
        layer_output,
        grad_input,
        shard_qkv,
        total_qv,
        shard_out,
        total_out,
        gain_one,
        shift_one,
        gain_two,
        shift_two,
        grad_up,
        total_up,
        grad_down.T,
        total_down,
    )


def solution(mesh):
    tokens = P(("fsdp", "tp"), None)
    placed = (
        tokens,
        P("fsdp", None, "tp"),
        P(None, "tp"),
        P("tp", "fsdp"),
        P(),
        P(),
        P(),
        P(),
        P(),
        P("fsdp", "tp"),
        P("tp"),
        P("tp", "fsdp"),
        P(),
        tokens,
    )
    return jax.shard_map(
        functools.partial(body, Links(mesh)),
        mesh=mesh,
        in_specs=placed,
        out_specs=(
            tokens,
            tokens,
            P("fsdp", None, "tp"),
            P(None, "tp"),
            P("tp", "fsdp"),
            P(),
            P(),
            P(),
            P(),
            P(),
            P("fsdp", "tp"),
            P("tp"),
            P("tp", "fsdp"),
            P(),
        ),
        check_vma=False,
    )
```

```python
import functools

import jax
import jax.numpy as jnp
from jax import lax
from jax.experimental import pallas as pl
from jax.experimental.pallas import tpu as pltpu
from jax.sharding import PartitionSpec as P

HEAD_DIM = 64
SEQ_LEN = 512
HALF = 256
EPS = 1e-05
AXES = ("fsdp", "tp")
BF = jnp.bfloat16
F32 = jnp.float32
MB = 1 << 20
SHARE = 0.3
BIAS_OUT, GAIN_ATTN, SHIFT_ATTN, GAIN_MLP, SHIFT_MLP, BIAS_DOWN = (slice(i, i + 1) for i in range(6))
VMEM_MB = 36
SMALL_ATTN = 768


def dot(left, right):
    return lax.dot_general(left, right, (((1,), (0,)), ((), ())), preferred_element_type=F32)


def dot_nt(left, right):
    return lax.dot_general(left, right, (((1,), (1,)), ((), ())), preferred_element_type=F32)


def dot_tn(left, right):
    return lax.dot_general(left, right, (((0,), (0,)), ((), ())), preferred_element_type=F32)


def whole(shape):
    zeros = (0,) * len(shape)
    return pl.BlockSpec(shape, lambda *_: zeros)


def params(limit_mb):
    return pltpu.CompilerParams(vmem_limit_bytes=(VMEM_MB or limit_mb) * MB)


def cost(flops, nbytes, trans=0):
    return pl.CostEstimate(
        flops=int(flops * SHARE), bytes_accessed=int(nbytes * SHARE), transcendentals=int(trans * SHARE)
    )


def unit_rows(rows):
    centre = rows - jnp.mean(rows, axis=-1, keepdims=True)
    spread = lax.rsqrt(jnp.mean(centre * centre, axis=-1, keepdims=True) + EPS)
    return centre * spread, spread


def norm_back(grad_out, unit, spread, gain):
    scaled = grad_out * gain
    inner = jnp.mean(scaled * unit, axis=-1, keepdims=True)
    return spread * (scaled - jnp.mean(scaled, axis=-1, keepdims=True) - unit * inner)


def add_sum(ref, value):
    @pl.when(pl.program_id(0) == 0)
    def _():
        ref[...] = jnp.zeros_like(ref)

    ref[...] += jnp.sum(value, axis=0, keepdims=True)


def start_kernel(x_ref, cot_ref, qv_ref, up_ref, *refs):
    vectors, (n1_ref, sum_ref, small_ref, table_ref) = refs[:6], refs[6:]

    @pl.when(pl.program_id(0) == 0)
    def _():
        for i, ref in enumerate(vectors):
            table_ref[i : i + 1] = ref[...].astype(F32).reshape(1, -1)
        small_ref[...] = jnp.zeros_like(small_ref)
        for c in range(2):
            pair, lone = (0, 384) if c == 0 else (256, 448)
            row = qv_ref[c : c + 1].astype(F32)
            small_ref[:, pair : pair + 128] = row[:, 0:128]
            small_ref[:, lone : lone + HEAD_DIM] = row[:, 128:192]
        small_ref[:, SMALL_ATTN:] = up_ref[...].astype(F32).reshape(1, -1)

    unit, _ = unit_rows(x_ref[...].astype(F32))
    normed = unit * table_ref[GAIN_ATTN] + table_ref[SHIFT_ATTN]
    n1_ref[...] = normed.astype(BF)
    add_sum(sum_ref, cot_ref[...].astype(F32))


def start_call(x, cot, bias_qv, bias_up, vectors):
    rows, d = x.shape
    units = bias_up.shape[0]
    tile = 256
    by_rows = pl.BlockSpec((tile, d), lambda i: (i, 0))
    return pl.pallas_call(
        start_kernel,
        grid=(rows // tile,),
        in_specs=[by_rows, by_rows, whole(bias_qv.shape), whole(bias_up.shape)]
        + [whole(v.shape) for v in vectors],
        out_specs=[by_rows]
        + [whole((1, d)), whole((1, SMALL_ATTN + units)), whole((8, d))],
        out_shape=[
            jax.ShapeDtypeStruct((rows, d), BF),
            jax.ShapeDtypeStruct((1, d), F32),
            jax.ShapeDtypeStruct((1, SMALL_ATTN + units), F32),
            jax.ShapeDtypeStruct((8, d), F32),
        ],
        compiler_params=params(24),
        cost_estimate=cost(0, 10 * rows * d),
        name="start",
    )(x, cot, bias_qv, bias_up, *vectors)


def assemble_kernel(count, place_ref, *refs):
    pieces, out_ref = refs[: 2 * count], refs[2 * count]
    z, x = place_ref[0], place_ref[1]
    for k in range(count):
        for dx in range(2):
            piece = pieces[dx * count + k]
            size = piece.shape[-2]
            slot = lax.rem(z - k + count, count) * 2 + lax.rem(x + dx, 2)
            value = piece[...].reshape(size, piece.shape[-1])
            out_ref[pl.ds(pl.multiple_of(slot * size, size), size)] = value


def assemble(place, pieces):
    count = len(pieces) // 2
    rows, cols = pieces[0][0].shape[-2:]
    specs = []
    for array, lead in pieces:
        block = (1,) * len(lead) + (rows, cols)
        specs.append(pl.BlockSpec(block, lambda *_, lead=lead: lead + (0, 0)))
    return pl.pallas_call(
        functools.partial(assemble_kernel, count),
        grid=(1,),
        in_specs=[pl.BlockSpec(memory_space=pltpu.SMEM)]
        + specs,
        out_specs=whole((2 * count * rows, cols)),
        out_shape=jax.ShapeDtypeStruct((2 * count * rows, cols), BF),
        compiler_params=params(16),
        cost_estimate=cost(0, 8 * count * rows * cols),
        name="assemble",
    )(place, *[array for array, _ in pieces])


HEAD_PLACES = ((0, 1, 2, 0, 0), (0, 1, 2, 64, 64), (3, 4, 3, 0, 64))


def lane_keep(tile, first):
    lanes = lax.broadcasted_iota(jnp.int32, tile.shape, 1)
    keep = (lanes >= first) & (lanes < first + HEAD_DIM)
    return jnp.where(keep, tile, jnp.zeros_like(tile))


def score_block(keys, query, start, stop, first_query):
    scores = dot_nt(keys[start:stop], query)
    if stop - 1 > first_query:
        key_idx = lax.broadcasted_iota(jnp.int32, scores.shape, 0) + start
        query_idx = lax.broadcasted_iota(jnp.int32, scores.shape, 1) + first_query
        scores = jnp.where(key_idx <= query_idx, scores, -1e30)
    return scores


def attend_kernel(n1_ref, w_ref, bias_ref, proj_ref, mixed_ref, lse_ref):
    projected = (dot(n1_ref[...], w_ref[...]) + bias_ref[...].astype(F32)).astype(BF)
    proj_ref[...] = projected
    lse_ref[...] = jnp.zeros_like(lse_ref)
    outs = {}
    for head, (qt, kt, vt, qk_lane, v_lane) in enumerate(HEAD_PLACES):
        query = lane_keep(projected[:, qt * 128 : qt * 128 + 128], qk_lane) * BF(0.125)
        keys = projected[:, kt * 128 : kt * 128 + 128]
        values = projected[:, vt * 128 : vt * 128 + 128]
        for block in range(2):
            first = block * HALF
            last = first + HALF
            scores = score_block(keys, query[first:last], 0, last, first)
            top = jnp.max(scores, axis=0, keepdims=True)
            weight = jnp.exp(scores - top)
            total = jnp.sum(weight, axis=0, keepdims=True)
            mixed = dot_tn(values[0:last], weight.astype(BF)) * (1.0 / total)
            outs[head, block] = mixed[v_lane : v_lane + HEAD_DIM]
            lse_ref[0, head : head + 1, first:last] = top + jnp.log(total)
    for block in range(2):
        first = block * HALF
        rows = slice(first, first + HALF)
        single = jnp.concatenate([jnp.zeros_like(outs[2, block]), outs[2, block]], axis=0)
        pair = jnp.concatenate([outs[0, block], outs[1, block]], axis=0)
        mixed_ref[rows, 0:128] = single.T.astype(BF)
        mixed_ref[rows, 128:256] = pair.T.astype(BF)


def attend_call(n1, w, bias):
    rows, d = n1.shape
    seqs = rows // SEQ_LEN
    return pl.pallas_call(
        attend_kernel,
        grid=(seqs,),
        in_specs=[
            pl.BlockSpec((SEQ_LEN, d), lambda i: (i, 0)),
            pl.BlockSpec((d, 640), lambda i: (0, 0)),
            pl.BlockSpec((1, 640), lambda i: (0, 0)),
        ],
        out_specs=[
            pl.BlockSpec((SEQ_LEN, 640), lambda i: (i, 0)),
            pl.BlockSpec((SEQ_LEN, 256), lambda i: (i, 0)),
            pl.BlockSpec((1, 8, SEQ_LEN), lambda i: (i, 0, 0)),
        ],
        out_shape=[
            jax.ShapeDtypeStruct((rows, 640), BF),
            jax.ShapeDtypeStruct((rows, 256), BF),
            jax.ShapeDtypeStruct((seqs, 8, SEQ_LEN), F32),
        ],
        compiler_params=params(32),
        cost_estimate=cost(6e9, 8e6),
        name="attend",
    )(n1, w, bias)


def middle_kernel(x_ref, table_ref, *refs):
    mixed, weights, (mid_ref, n2_ref) = refs[0:4], refs[4:8], refs[8:]
    attended = table_ref[BIAS_OUT]
    for m, w in zip(mixed, weights):
        attended = attended + dot_nt(m[...], w[...])
    middle = x_ref[...].astype(F32) + attended
    mid_ref[...] = middle
    unit, _ = unit_rows(middle)
    normed = unit * table_ref[GAIN_MLP] + table_ref[SHIFT_MLP]
    n2_ref[...] = normed.astype(BF)


def middle_call(x, table, mixed, weights):
    rows, d = x.shape
    tile = 256
    by_rows = pl.BlockSpec((tile, d), lambda i: (i, 0))
    return pl.pallas_call(
        middle_kernel,
        grid=(rows // tile,),
        in_specs=[by_rows, whole(table.shape)]
        + [pl.BlockSpec((tile, 256), lambda i: (i, 0))] * 4
        + [pl.BlockSpec((d, 256), lambda i: (0, 2))] * 4,
        out_specs=[by_rows, by_rows],
        out_shape=[
            jax.ShapeDtypeStruct((rows, d), F32),
            jax.ShapeDtypeStruct((rows, d), BF),
        ],
        compiler_params=params(24),
        cost_estimate=cost(2 * rows * d * 1024, 16e6),
        name="middle",
    )(x, table, *mixed, *weights)


def gelu_both(value):
    cumulative = 0.5 + 0.5 * lax.erf(value * 2.0**-0.5)
    bell = jnp.exp(-0.5 * value * value)
    return value * cumulative, cumulative + value * bell * (2.0 * 3.141592653589793) ** -0.5


def store_all(ref, lead, place_ref, value, count, got_ref=None, got_lead=()):
    z, x = place_ref[0], place_ref[1]
    size = value.shape[0] // (2 * count)
    for block in range(2 * count):
        slot = lax.rem(x + block % 2, 2) * count + lax.rem(block // 2 - z + count, count)
        part = value[block * size : (block + 1) * size]
        if got_ref is not None:
            part = part + got_ref[got_lead + (slot,)].astype(F32)
        ref[lead + (slot,)] = part.astype(BF)


def store_split(home_ref, away_ref, got_ref, lead, place_ref, value, count):
    z, x = place_ref[0], place_ref[1]
    size = value.shape[0] // (2 * count)
    for pair in range(count):
        slot = lax.rem(pair - z + count, count)
        first = value[2 * pair * size : (2 * pair + 1) * size]
        second = value[(2 * pair + 1) * size : (2 * pair + 2) * size]
        home = jnp.where(x == 0, first, second) + got_ref[lead + (slot,)].astype(F32)
        away = jnp.where(x == 0, second, first) + got_ref[lead + (count + slot,)].astype(F32)
        home_ref[slot] = home.astype(BF)
        away_ref[slot] = away.astype(BF)


def feed_kernel(count, tokens, has_got, place_ref, n2_ref, cot_ref, *refs):
    up_ref, down_ref, bias_ref = refs[0:3]
    got_ref = refs[3] if has_got else None
    outs = refs[3 + has_got :]
    hidden_ref, pre_ref, sum_ref = outs[0:3]
    rows = n2_ref.shape[0]
    up, down, bias = up_ref[...], down_ref[...], bias_ref[...].astype(F32)
    total = jnp.zeros_like(bias)
    for first in range(0, rows, tokens):
        here = slice(first, first + tokens)
        pre = dot(n2_ref[here], up) + bias
        grad_hidden = dot(cot_ref[here], down)
        hidden, slope = gelu_both(pre)
        hidden_ref[here] = hidden.astype(BF)
        grad_pre = (grad_hidden * slope).astype(BF)
        pre_ref[here] = grad_pre
        total = total + jnp.sum(grad_pre.astype(F32), axis=0, keepdims=True)
    sum_ref[...] = total
    grads = (dot_tn(n2_ref[...], pre_ref[...]), dot_tn(cot_ref[...], hidden_ref[...]))
    if has_got:
        store_split(outs[3], outs[4], got_ref, (0,), place_ref, grads[0], count)
        store_all(outs[5], (), place_ref, grads[1], count, got_ref, (1,))
    else:
        store_all(outs[3], (0,), place_ref, grads[0], count)
        store_all(outs[3], (1,), place_ref, grads[1], count)


def feed_call(place, count, n2, cot, up, down, small, got=None):
    rows, d = n2.shape
    units = up.shape[1]
    tile = 256
    shard = d // (2 * count)
    cols = lambda n: pl.BlockSpec((n, tile), lambda i: (0, i))
    hid = jax.ShapeDtypeStruct((rows, units), BF)
    both_spec = pl.BlockSpec((2, 2 * count, shard, tile), lambda i: (0, 0, 0, i))
    if got is None:
        grad_specs = [both_spec]
        grads = [jax.ShapeDtypeStruct((2, 2 * count, shard, units), BF)]
    else:
        grad_specs = [pl.BlockSpec((n, shard, tile), lambda i: (0, 0, i)) for n in (count, count, 2 * count)]
        grads = [jax.ShapeDtypeStruct((n, shard, units), BF) for n in (count, count, 2 * count)]
    gots = () if got is None else (got,)
    return pl.pallas_call(
        functools.partial(feed_kernel, count, 512, len(gots)),
        grid=(units // tile,),
        in_specs=[
            pl.BlockSpec(memory_space=pltpu.SMEM),
            whole((rows, d)),
            whole((rows, d)),
            cols(d),
            cols(d),
            pl.BlockSpec((1, tile), lambda i: (0, SMALL_ATTN // tile + i)),
        ]
        + [both_spec] * len(gots),
        out_specs=[cols(rows)] * 2 + [cols(1)] + grad_specs,
        out_shape=[hid] * 2 + [jax.ShapeDtypeStruct((1, units), F32)] + grads,
        compiler_params=params(40),
        cost_estimate=cost(2 * 4 * rows * d * units, 16e6, rows * units),
        name="feed",
    )(place, n2, cot, up, down, small, *gots)


def turn_kernel(_, mid_ref, cot_ref, table_ref, *refs):
    pre, ups = refs[0:4], refs[4:8]
    gmid_ref, grows_ref, gain_sum, shift_sum, bias_sum = refs[-5:]
    grad = None
    for g, w in zip(pre, ups):
        term = dot_nt(g[...], w[...])
        grad = term if grad is None else grad + term
    unit, spread = unit_rows(mid_ref[...])
    add_sum(gain_sum, grad * unit)
    add_sum(shift_sum, grad)
    back = norm_back(grad, unit, spread, table_ref[GAIN_MLP])
    grad_middle = cot_ref[...].astype(F32) + back
    gmid_ref[...] = grad_middle
    rows = grad_middle.astype(BF)
    grows_ref[...] = rows
    add_sum(bias_sum, rows.astype(F32))


def turn_call(place, middle, cot, table, pre, ups):
    rows, d = middle.shape
    units = ups[0].shape[1]
    tile = 256
    by_rows = pl.BlockSpec((tile, d), lambda i: (i, 0))
    kept = pl.BlockSpec((d, units), lambda i: (0, 0), pipeline_mode=pl.Buffered(1))
    total = jax.ShapeDtypeStruct((1, d), F32)
    return pl.pallas_call(
        turn_kernel,
        grid=(rows // tile,),
        in_specs=[pl.BlockSpec(memory_space=pltpu.SMEM), by_rows, by_rows, whole(table.shape)]
        + [pl.BlockSpec((tile, units), lambda i: (i, 0))] * 4
        + [kept] * 4,
        out_specs=[by_rows] * 2 + [whole((1, d))] * 3,
        out_shape=[
            jax.ShapeDtypeStruct((rows, d), F32),
            jax.ShapeDtypeStruct((rows, d), BF),
            total,
            total,
            total,
        ],
        compiler_params=params(32),
        cost_estimate=cost(2 * 4 * rows * d * units, 20e6),
        name="turn",
    )(place, middle, cot, table, *pre, *ups)


def output_kernel(_, mid_ref, table_ref, *refs):
    hidden, downs, out_ref = refs[0:4], refs[4:8], refs[-1]
    mlp = table_ref[BIAS_DOWN]
    for h, w in zip(hidden, downs):
        mlp = mlp + dot_nt(h[...], w[...])
    out_ref[...] = (mid_ref[...] + mlp).astype(BF)


def output_call(place, middle, table, hidden, downs):
    rows, d = middle.shape
    units = downs[0].shape[1]
    tile = 256
    by_rows = pl.BlockSpec((tile, d), lambda i: (i, 0))
    kept = pl.BlockSpec((d, units), lambda i: (0, 0), pipeline_mode=pl.Buffered(1))
    return pl.pallas_call(
        output_kernel,
        grid=(rows // tile,),
        in_specs=[pl.BlockSpec(memory_space=pltpu.SMEM), by_rows, whole(table.shape)]
        + [pl.BlockSpec((tile, units), lambda i: (i, 0))] * 4
        + [kept] * 4,
        out_specs=by_rows,
        out_shape=jax.ShapeDtypeStruct((rows, d), BF),
        compiler_params=params(32),
        cost_estimate=cost(2 * 4 * rows * d * units, 16e6),
        name="output",
    )(place, middle, table, *hidden, *downs)


def attend_back_kernel(
    count,
    has_got,
    place_ref,
    grows_ref,
    n1_ref,
    w_ref,
    proj_ref,
    mixed_ref,
    lse_ref,
    *refs,
):
    got_ref = refs[0] if has_got else None
    total = refs[-1]
    gproj_ref, sum_ref, *grad_refs = refs[-5:-1] if has_got else refs[-4:-1]
    step = pl.program_id(0)
    projected = proj_ref[...]
    grad_mixed = dot(grows_ref[...], w_ref[...]).astype(BF)
    parts = {}
    early = lax.broadcasted_iota(jnp.int32, (HALF, HALF), 0) <= lax.broadcasted_iota(jnp.int32, (HALF, HALF), 1)
    jobs = []
    for head, (qt, kt, vt, qk_lane, v_lane) in enumerate(HEAD_PLACES):
        mt = 0 if head == 2 else 1
        query = lane_keep(projected[:, qt * 128 : qt * 128 + 128], qk_lane) * BF(0.125)
        keys = projected[:, kt * 128 : kt * 128 + 128]
        values = projected[:, vt * 128 : vt * 128 + 128]
        grads = lane_keep(grad_mixed[:, mt * 128 : mt * 128 + 128], v_lane)
        parts["k", head] = [None, None]
        parts["v", head] = [None, None]
        for block in range(2):
            rows = slice(block * HALF, block * HALF + HALF)
            jobs.append((head, block, qk_lane, query[rows], keys, values, grads[rows]))

    def first_stage(job):
        head, block, _, qb, keys, values, gb = job
        last = block * HALF + HALF
        return dot_nt(keys[0:last], qb), dot_nt(values[0:last], gb)

    def last_stage(job, scores, gprobs):
        head, block, qk_lane, qb, keys, values, gb = job
        last = block * HALF + HALF
        lse = lse_ref[0, head : head + 1, last - HALF : last]
        probs = jnp.exp(scores - lse)
        corner = jnp.where(early, probs[last - HALF :], 0.0)
        probs = jnp.concatenate([probs[: last - HALF], corner], axis=0) if block else corner
        both = probs * gprobs
        delta = jnp.sum(both, axis=0, keepdims=True)
        gscores = (both - probs * delta).astype(BF)
        gq = dot_tn(keys[0:last], gscores) * 0.125
        parts["q", head, block] = gq[qk_lane : qk_lane + HEAD_DIM]
        gk = dot(gscores, qb)
        gv = dot(probs.astype(BF), gb)
        for name, got in (("k", gk), ("v", gv)):
            held = parts[name, head]
            for b in range(block + 1):
                part = got[b * HALF : b * HALF + HALF]
                held[b] = part if held[b] is None else held[b] + part

    waiting = None
    for job in jobs + [None]:
        ahead = None if job is None else (job, *first_stage(job))
        if waiting is not None:
            last_stage(*waiting)
        waiting = ahead
    for block in range(2):
        rows = slice(block * HALF, block * HALF + HALF)
        pair = jnp.concatenate([parts["q", 0, block], parts["q", 1, block]], axis=0).T
        lone = parts["q", 2, block]
        lone = jnp.concatenate([lone, jnp.zeros_like(lone)], axis=0).T
        gproj_ref[rows, 0:128] = pair.astype(BF)
        gproj_ref[rows, 128:256] = (parts["k", 0][block] + parts["k", 1][block]).astype(BF)
        gproj_ref[rows, 256:384] = (parts["v", 0][block] + parts["v", 1][block]).astype(BF)
        gproj_ref[rows, 384:512] = (lone + parts["v", 2][block]).astype(BF)
        gproj_ref[rows, 512:640] = parts["k", 2][block].astype(BF)
    gproj = gproj_ref[...]
    add_sum(sum_ref, gproj.astype(F32))
    grad_a = dot_tn(n1_ref[...], gproj)
    grad_b = dot_tn(grows_ref[...], mixed_ref[...])
    grad = jnp.concatenate(
        [grad_a[:, 0:512], grad_a[:, 512:640] + grad_b[:, 0:128], grad_b[:, 128:256]], axis=1
    )

    @pl.when(step == 0)
    def _():
        total[...] = grad

    @pl.when(step > 0)
    def _():
        total[...] += grad

    @pl.when(step == pl.num_programs(0) - 1)
    def _():
        if has_got:
            store_split(*grad_refs, got_ref, (), place_ref, total[...], count)
        else:
            store_all(*grad_refs, (), place_ref, total[...], count)


def attend_back_call(place, count, grows, n1, w, proj, mixed, lse, got=None):
    rows, d = grows.shape
    seqs = rows // SEQ_LEN
    shard = d // (2 * count)
    by_rows = lambda n: pl.BlockSpec((SEQ_LEN, n), lambda i: (i, 0))
    gots = () if got is None else (got,)
    both = (2 * count, shard, 768)
    grads = [both] if got is None else [(count, shard, 768)] * 2
    return pl.pallas_call(
        functools.partial(attend_back_kernel, count, len(gots)),
        grid=(seqs,),
        in_specs=[
            pl.BlockSpec(memory_space=pltpu.SMEM),
            by_rows(d),
            by_rows(d),
            pl.BlockSpec((d, 256), lambda i: (0, 2)),
            by_rows(640),
            by_rows(256),
            pl.BlockSpec((1, 8, SEQ_LEN), lambda i: (i, 0, 0)),
        ]
        + [whole(both)] * len(gots),
        out_specs=[by_rows(640), whole((1, 640))] + [whole(g) for g in grads],
        out_shape=[jax.ShapeDtypeStruct((rows, 640), BF), jax.ShapeDtypeStruct((1, 640), F32)]
        + [jax.ShapeDtypeStruct(g, BF) for g in grads],
        scratch_shapes=[pltpu.VMEM((d, 768), F32)],
        compiler_params=params(40),
        cost_estimate=cost(10e9, 12e6),
        name="attend_back",
    )(place, grows, n1, w, proj, mixed, lse, *gots)


def finish_kernel(_, x_ref, gmid_ref, table_ref, *refs):
    gproj, weights, known, sum_proj, sum_up = refs[0:4], refs[4:8], refs[8:12], refs[12:16], refs[16:20]
    out_ref, keep_ref, away_ref, gain_sum, shift_sum = refs[20:]
    grad = None
    for g, w in zip(gproj, weights):
        term = dot_nt(g[...], w[...])
        grad = term if grad is None else grad + term
    unit, spread = unit_rows(x_ref[...].astype(F32))
    add_sum(gain_sum, grad * unit)
    add_sum(shift_sum, grad)
    back = norm_back(grad, unit, spread, table_ref[GAIN_ATTN])
    out_ref[...] = (gmid_ref[...] + back).astype(BF)

    @pl.when(pl.program_id(0) == pl.num_programs(0) - 1)
    def _():
        shared = jnp.concatenate(
            [r[...] for r in known] + [gain_sum[...], shift_sum[...]], axis=1
        )
        for dy in range(2):
            for dc, ref in enumerate((keep_ref, away_ref)):
                row = jnp.concatenate([shared, sum_proj[2 * dy + dc][...], sum_up[2 * dy + dc][...]], axis=1)
                ref[dy : dy + 1] = row


def finish_call(place, x, gmid, table, gproj, weights, known, sum_proj, sum_up):
    rows, d = x.shape
    tile = 256
    by_rows = pl.BlockSpec((tile, d), lambda i: (i, 0))
    width = 6 * d + sum_proj[0].shape[1] + sum_up[0].shape[1]
    return pl.pallas_call(
        finish_kernel,
        grid=(rows // tile,),
        in_specs=[pl.BlockSpec(memory_space=pltpu.SMEM), by_rows, by_rows, whole(table.shape)]
        + [pl.BlockSpec((tile, 640), lambda i: (i, 0))] * 4
        + [pl.BlockSpec((d, 640), lambda i: (0, 0))] * 4
        + [whole(v.shape) for v in (*known, *sum_proj, *sum_up)],
        out_specs=[by_rows, whole((2, width)), whole((2, width))],
        out_shape=[jax.ShapeDtypeStruct((rows, d), BF)] + [jax.ShapeDtypeStruct((2, width), F32)] * 2,
        scratch_shapes=[pltpu.VMEM((1, d), F32)] * 2,
        compiler_params=params(32),
        cost_estimate=cost(2 * 4 * rows * d * 640, 16e6),
        name="finish",
    )(place, x, gmid, table, *gproj, *weights, *known, *sum_proj, *sum_up)


class Links:
    def __init__(self, mesh):
        self.count = mesh.shape["fsdp"] // 2
        places = [
            (z, x, y, c)
            for z in range(self.count)
            for x in range(2)
            for y in range(2)
            for c in range(2)
        ]

        def index(z, x, y, c):
            return ((z * 2 + x) * 2 + y) * 2 + c

        def pairs(move):
            return [(index(*p), index(*move(*p))) for p in places]

        self.core = pairs(lambda z, x, y, c: (z, x, y, 1 - c))
        self.y = pairs(lambda z, x, y, c: (z, x, 1 - y, c))
        self.x = pairs(lambda z, x, y, c: (z, 1 - x, y, c))
        self.ring = pairs(lambda z, x, y, c: ((z + 1) % self.count, x, y, c))
        self.far = [
            pairs(lambda z, x, y, c, k=k: ((z + k) % self.count, x, y, c)) for k in range(self.count)
        ]
        self.back = [
            pairs(lambda z, x, y, c, k=k: ((z - k) % self.count, x, y, c)) for k in range(self.count)
        ]
        self.xy = pairs(lambda z, x, y, c: (z, 1 - x, 1 - y, c))
        self.trees = []
        step = 1
        while step < self.count:
            size = 4 if step * 4 <= self.count else 2
            self.trees.append(
                [pairs(lambda z, x, y, c, b=step * k: (z ^ b, x, y, c)) for k in range(1, size)]
            )
            step *= size

    @staticmethod
    def send(value, pairs):
        return lax.ppermute(value, AXES, pairs)


def plus(*terms, kind=BF):
    total = terms[0].astype(F32)
    for term in terms[1:]:
        total = total + term.astype(F32)
    return total.astype(kind)


def tie(value, *others):
    return lax.optimization_barrier((value, others))[0]


def ring_from(links, first):
    held = [first]
    for _ in range(links.count - 1):
        held.append(links.send(held[-1], links.ring))
    return held


def gather_and_attend(links, place, attn, up, down, n1, smalls):
    n = links.count
    half = n // 2

    near, lines, others, quads = [attn], [], [], []
    pair = jnp.stack([up, links.send(up, links.x)])
    steps = [jnp.stack([pair, links.send(tie(pair, n1), links.y)])]
    for k in range(1, n):
        before = ()
        if k == 2:
            before = (n1, pair)
        if k == half + 1:
            before += (others[0], smalls[2], steps[0])
        near.append(links.send(tie(near[-1], *before) if before else near[-1], links.ring))
        if (k + 1) % half == 0:
            lines.append(jnp.stack(near[-half:]))
            others.append(links.send(lines[-1], links.x))
            quads.append(links.send(jnp.stack([lines[-1], others[-1]]), links.y))
    steps.append(links.send(steps[0], links.ring))
    line = jnp.stack([down] + [links.send(down, links.far[k]) for k in range(1, n)])

    own = assemble(place, [(v[k // half], (k % half,)) for v in (lines, others) for k in range(n)])
    attn_w = [own, links.send(own, links.core)]
    proj, mixed, lse = [], [], []

    def attend(j, *before):
        p, m, s = attend_call(n1, attn_w[j], tie(smalls[j], *before) if before else smalls[j])
        proj.append(p)
        mixed.append(m)
        lse.append(s)

    attend(0)
    steps.append(links.send(tie(steps[1], mixed[0]), links.ring))
    line = tie(line, others[1], smalls[1], smalls[3])
    other = links.send(line, links.x)
    beyond = [links.send(tie(v, quads[1]), links.y) for v in (line, other)]
    attend(1, mixed[0])
    own = assemble(tie(place, mixed[1]), [(quads[k // half], (dx, k % half)) for dx in range(2) for k in range(n)])
    attn_w += [own, links.send(own, links.core)]
    attend(2, mixed[1], steps[2])
    for k in range(2, n - 1):
        steps.append(links.send(tie(steps[-1], mixed[1], other), links.ring))
    attend(3, mixed[2])

    last = tie(place, mixed[3])
    up_w, down_w = [], []
    for dy in range(2):
        own = assemble(last, [(v, (dy, dx)) for dx in range(2) for v in steps])
        up_w += [own, links.send(own, links.core)]
        own = assemble(last, [(v, (k,)) for v in ((line, other), beyond)[dy] for k in range(n)])
        down_w += [own, links.send(own, links.core)]
    return attn_w, up_w, down_w, proj, mixed, lse


def spread_sum(links, home):
    got = [links.send(home[k], links.far[k]) for k in range(1, links.count)]
    return plus(home[0], *got, kind=F32)


def sum_all(links, keep, away):
    rows = keep + links.send(away, links.core)
    near, far = rows[0:1], rows[1:2]
    total = (near + links.send(near, links.x)) + (
        links.send(far, links.y) + links.send(far, links.xy)
    )
    for pairs in links.trees:
        got = [total] + [links.send(total, p) for p in pairs]
        while len(got) > 1:
            got = [got[i] + got[i + 1] for i in range(0, len(got), 2)]
        total = got[0]
    return total


def pack_attn(w_qkv, w_out):
    q, k, v, o = w_qkv[:, 0], w_qkv[:, 1], w_qkv[:, 2], w_out.T
    return jnp.concatenate(
        [q[:, :128], k[:, :128], v[:, :128], q[:, 128:], v[:, 128:], k[:, 128:], o[:, 128:], o[:, :128]],
        axis=1,
    )


def unpack_attn(g):
    q = jnp.concatenate([g[:, 0:128], g[:, 384:448]], axis=1)
    k = jnp.concatenate([g[:, 128:256], g[:, 512:576]], axis=1)
    v = jnp.concatenate([g[:, 256:384], g[:, 448:512]], axis=1)
    o = jnp.concatenate([g[:, 640:768], g[:, 576:640]], axis=1)
    return jnp.stack([q, k, v], axis=1), o.T


def body(
    links,
    layer_input,
    w_qkv,
    bias_qv,
    w_out,
    bias_out,
    gain_attn,
    shift_attn,
    gain_mlp,
    shift_mlp,
    w_up,
    bias_up,
    w_down,
    bias_down,
    cotangent,
):
    fsdp = lax.axis_index("fsdp")
    place = jnp.stack([fsdp // 2, fsdp % 2]).astype(jnp.int32)
    count = links.count
    n1, sum_down, small, table = start_call(
        layer_input,
        cotangent,
        bias_qv,
        bias_up,
        (bias_out, gain_attn, shift_attn, gain_mlp, shift_mlp, bias_down),
    )
    small_y = links.send(small, links.y)
    smalls = [small, links.send(small, links.core), small_y, links.send(small_y, links.core)]
    attn_w, up_w, down_w, proj, mixed, lse = gather_and_attend(
        links, place, pack_attn(w_qkv, w_out), w_up, w_down.T, n1, smalls
    )

    middle, n2 = middle_call(tie(layer_input, up_w[0], up_w[2]), table, mixed, attn_w)

    hidden, pre, sum_up = [None] * 4, [None] * 4, [None] * 4
    up_home, up_away, down_sum = [None] * 2, [None] * 2, [None] * 2
    gots = [None] * 4
    for j in (1, 3, 0, 2):
        out = feed_call(
            place, count, n2, cotangent, up_w[j], down_w[j], smalls[j], gots[j]
        )
        hidden[j], pre[j], sum_up[j] = out[0:3]
        if j % 2:
            gots[j - 1] = links.send(out[3], links.core)
        else:
            up_home[j // 2], up_away[j // 2], down_sum[j // 2] = out[3:6]

    got_x0 = links.send(up_away[0], links.x)
    got_x1 = links.send(up_away[1], links.x)
    got_down = links.send(down_sum[1], links.y)
    gmid, grows, gain_two, shift_two, sum_out = turn_call(
        place, middle, cotangent, table, pre, up_w
    )

    gproj, sum_proj = [None] * 4, [None] * 4
    attn_home, attn_away = [None] * 2, [None] * 2

    def back(j, got, *before):
        out = attend_back_call(
            tie(place, *before) if before else place,
            count,
            grows,
            n1,
            attn_w[j],
            proj[j],
            mixed[j],
            lse[j],
            got,
        )
        gproj[j], sum_proj[j] = out[0:2]
        if j % 2:
            return links.send(out[2], links.core)
        attn_home[j // 2], attn_away[j // 2] = out[2:4]

    got_three = back(3, None, got_x0)
    up_beyond = plus(up_home[1], got_x1)
    got_up = links.send(up_beyond, links.y)
    got_one = back(1, None, up_beyond)
    down_away = plus(down_sum[0][count:], got_down[count:])
    got_x = links.send(down_away, links.x)
    back(2, got_three, down_away)
    got_a1 = links.send(attn_away[1], links.x)
    up_all = plus(up_home[0], got_x0, got_up)
    back(0, got_one, up_all, sum_proj[2])
    grad_up = spread_sum(links, up_all)
    got_a0 = links.send(attn_away[0], links.x)
    attn_beyond = plus(attn_home[1], got_a1)
    got_attn = links.send(attn_beyond, links.y)
    down_all = plus(down_sum[0][:count], got_down[:count], got_x)
    grad_down = spread_sum(links, down_all)
    grad_input, keep, away = finish_call(
        tie(place, attn_beyond, down_all),
        layer_input,
        gmid,
        table,
        gproj,
        attn_w,
        (sum_out, sum_down, gain_two, shift_two),
        sum_proj,
        sum_up,
    )
    attn_all = plus(attn_home[0], got_a0, got_attn)
    parts = [attn_all[0]] + [links.send(attn_all[k], links.far[k]) for k in range(1, count)]
    sums = sum_all(links, keep, away)
    layer_output = output_call(tie(place, sums, attn_all), middle, table, hidden, down_w)
    grad_attn = plus(*parts, kind=F32)

    d = layer_input.shape[1]
    heads = bias_qv.shape[1]
    vec = sums[0]
    total_out, total_down, gain_two, shift_two, gain_one, shift_one = (
        vec[i * d : (i + 1) * d] for i in range(6)
    )
    own = vec[6 * d :]
    total_qv = jnp.stack(
        [
            jnp.concatenate([own[0:128], own[384:448]]),
            jnp.concatenate([own[256:384], own[448:512]]),
        ]
    )
    total_up = own[640:]

    shard_qkv, shard_out = unpack_attn(grad_attn)
    return (
        layer_output,
        grad_input,
        shard_qkv,
        total_qv,
        shard_out,
        total_out,
        gain_one,
        shift_one,
        gain_two,
        shift_two,
        grad_up,
        total_up,
        grad_down.T,
        total_down,
    )


def solution(mesh):
    tokens = P(("fsdp", "tp"), None)
    placed = (
        tokens,
        P("fsdp", None, "tp"),
        P(None, "tp"),
        P("tp", "fsdp"),
        P(),
        P(),
        P(),
        P(),
        P(),
        P("fsdp", "tp"),
        P("tp"),
        P("tp", "fsdp"),
        P(),
        tokens,
    )
    return jax.shard_map(
        functools.partial(body, Links(mesh)),
        mesh=mesh,
        in_specs=placed,
        out_specs=(
            tokens,
            tokens,
            P("fsdp", None, "tp"),
            P(None, "tp"),
            P("tp", "fsdp"),
            P(),
            P(),
            P(),
            P(),
            P(),
            P("fsdp", "tp"),
            P("tp"),
            P("tp", "fsdp"),
            P(),
        ),
        check_vma=False,
    )
```

```python
import functools

import jax
import jax.numpy as jnp
from jax import lax
from jax.experimental import pallas as pl
from jax.experimental.pallas import tpu as pltpu
from jax.sharding import PartitionSpec as P

HEAD_DIM = 64
SEQ_LEN = 512
HALF = 256
EPS = 1e-05
AXES = ("fsdp", "tp")
BF = jnp.bfloat16
F32 = jnp.float32
MB = 1 << 20
SHARE = 0.3
BIAS_OUT, GAIN_ATTN, SHIFT_ATTN, GAIN_MLP, SHIFT_MLP, BIAS_DOWN = (slice(i, i + 1) for i in range(6))
VMEM_MB = {"start": 60, "feed": 60, "attend_back": 60, "turn": 60, "finish": 60, "output": 60}
SMALL_ATTN = 768


def dot(left, right):
    return lax.dot_general(left, right, (((1,), (0,)), ((), ())), preferred_element_type=F32)


def dot_nt(left, right):
    return lax.dot_general(left, right, (((1,), (1,)), ((), ())), preferred_element_type=F32)


def dot_tn(left, right):
    return lax.dot_general(left, right, (((0,), (0,)), ((), ())), preferred_element_type=F32)


def whole(shape):
    zeros = (0,) * len(shape)
    return pl.BlockSpec(shape, lambda *_: zeros)


def params(kernel):
    return pltpu.CompilerParams(vmem_limit_bytes=VMEM_MB.get(kernel, 36) * MB)


def cost(flops, nbytes, trans=0):
    return pl.CostEstimate(
        flops=int(flops * SHARE), bytes_accessed=int(nbytes * SHARE), transcendentals=int(trans * SHARE)
    )


def unit_rows(rows):
    centre = rows - jnp.mean(rows, axis=-1, keepdims=True)
    spread = lax.rsqrt(jnp.mean(centre * centre, axis=-1, keepdims=True) + EPS)
    return centre * spread, spread


def norm_back(grad_out, unit, spread, gain):
    scaled = grad_out * gain
    inner = jnp.mean(scaled * unit, axis=-1, keepdims=True)
    return spread * (scaled - jnp.mean(scaled, axis=-1, keepdims=True) - unit * inner)


def add_sum(ref, value):
    @pl.when(pl.program_id(0) == 0)
    def _():
        ref[...] = jnp.zeros_like(ref)

    ref[...] += jnp.sum(value, axis=0, keepdims=True)


def start_kernel(x_ref, cot_ref, qv_ref, up_ref, *refs):
    vectors, (n1_ref, sum_ref, small_ref, table_ref) = refs[:6], refs[6:]

    @pl.when(pl.program_id(0) == 0)
    def _():
        for i, ref in enumerate(vectors):
            table_ref[i : i + 1] = ref[...].astype(F32).reshape(1, -1)
        small_ref[...] = jnp.zeros_like(small_ref)
        for c in range(2):
            pair, lone = (0, 384) if c == 0 else (256, 448)
            row = qv_ref[c : c + 1].astype(F32)
            small_ref[:, pair : pair + 128] = row[:, 0:128]
            small_ref[:, lone : lone + HEAD_DIM] = row[:, 128:192]
        small_ref[:, SMALL_ATTN:] = up_ref[...].astype(F32).reshape(1, -1)

    unit, _ = unit_rows(x_ref[...].astype(F32))
    normed = unit * table_ref[GAIN_ATTN] + table_ref[SHIFT_ATTN]
    n1_ref[...] = normed.astype(BF)
    add_sum(sum_ref, cot_ref[...].astype(F32))


def start_call(x, cot, bias_qv, bias_up, vectors):
    rows, d = x.shape
    units = bias_up.shape[0]
    tile = 256
    by_rows = pl.BlockSpec((tile, d), lambda i: (i, 0))
    return pl.pallas_call(
        start_kernel,
        grid=(rows // tile,),
        in_specs=[by_rows, by_rows, whole(bias_qv.shape), whole(bias_up.shape)]
        + [whole(v.shape) for v in vectors],
        out_specs=[by_rows]
        + [whole((1, d)), whole((1, SMALL_ATTN + units)), whole((8, d))],
        out_shape=[
            jax.ShapeDtypeStruct((rows, d), BF),
            jax.ShapeDtypeStruct((1, d), F32),
            jax.ShapeDtypeStruct((1, SMALL_ATTN + units), F32),
            jax.ShapeDtypeStruct((8, d), F32),
        ],
        compiler_params=params("start"),
        cost_estimate=cost(0, 10 * rows * d),
        name="start",
    )(x, cot, bias_qv, bias_up, *vectors)


def piece_specs(pieces, cols, index):
    rows = pieces[0][0].shape[-2]
    return [
        pl.BlockSpec((1,) * len(lead) + (rows, cols), lambda i, lead=lead: lead + (0, index(i)))
        for _, lead in pieces
    ]


def place_pieces(place_ref, pieces, out_ref):
    count = len(pieces) // 2
    z, x = place_ref[0], place_ref[1]
    for k in range(count):
        for dx in range(2):
            piece = pieces[dx * count + k]
            size, cols = piece.shape[-2:]
            slot = lax.rem(z - k + count, count) * 2 + lax.rem(x + dx, 2)
            out_ref[pl.ds(pl.multiple_of(slot * size, size), size)] = piece[...].reshape(size, cols)


HEAD_PLACES = ((0, 1, 2, 0, 0), (0, 1, 2, 64, 64), (3, 4, 3, 0, 64))


def lane_keep(tile, first):
    lanes = lax.broadcasted_iota(jnp.int32, tile.shape, 1)
    keep = (lanes >= first) & (lanes < first + HEAD_DIM)
    return jnp.where(keep, tile, jnp.zeros_like(tile))


def score_block(keys, query, start, stop, first_query):
    scores = dot_nt(keys[start:stop], query)
    if stop - 1 > first_query:
        key_idx = lax.broadcasted_iota(jnp.int32, scores.shape, 0) + start
        query_idx = lax.broadcasted_iota(jnp.int32, scores.shape, 1) + first_query
        scores = jnp.where(key_idx <= query_idx, scores, -1e30)
    return scores


def attend_kernel(place_ref, n1_ref, bias_ref, *refs):
    pieces, (w_ref, proj_ref, mixed_ref, lse_ref) = refs[:-4], refs[-4:]

    @pl.when(pl.program_id(0) == 0)
    def _():
        place_pieces(place_ref, pieces, w_ref)

    projected = (dot(n1_ref[...], w_ref[:, 0:640]) + bias_ref[...].astype(F32)).astype(BF)
    proj_ref[...] = projected
    lse_ref[...] = jnp.zeros_like(lse_ref)
    outs = {}
    for head, (qt, kt, vt, qk_lane, v_lane) in enumerate(HEAD_PLACES):
        query = lane_keep(projected[:, qt * 128 : qt * 128 + 128], qk_lane) * BF(0.125)
        keys = projected[:, kt * 128 : kt * 128 + 128]
        values = projected[:, vt * 128 : vt * 128 + 128]
        for block in range(2):
            first = block * HALF
            last = first + HALF
            scores = score_block(keys, query[first:last], 0, last, first)
            top = jnp.max(scores, axis=0, keepdims=True)
            weight = jnp.exp(scores - top)
            total = jnp.sum(weight, axis=0, keepdims=True)
            mixed = dot_tn(values[0:last], weight.astype(BF)) * (1.0 / total)
            outs[head, block] = mixed[v_lane : v_lane + HEAD_DIM]
            lse_ref[0, head : head + 1, first:last] = top + jnp.log(total)
    for block in range(2):
        first = block * HALF
        rows = slice(first, first + HALF)
        single = jnp.concatenate([jnp.zeros_like(outs[2, block]), outs[2, block]], axis=0)
        pair = jnp.concatenate([outs[0, block], outs[1, block]], axis=0)
        mixed_ref[rows, 0:128] = single.T.astype(BF)
        mixed_ref[rows, 128:256] = pair.T.astype(BF)


def attend_call(place, n1, pieces, bias):
    rows, d = n1.shape
    seqs = rows // SEQ_LEN
    return pl.pallas_call(
        attend_kernel,
        grid=(seqs,),
        in_specs=[
            pl.BlockSpec(memory_space=pltpu.SMEM),
            pl.BlockSpec((SEQ_LEN, d), lambda i: (i, 0)),
            pl.BlockSpec((1, 640), lambda i: (0, 0)),
        ]
        + piece_specs(pieces, 768, lambda i: 0),
        out_specs=[
            whole((d, 768)),
            pl.BlockSpec((SEQ_LEN, 640), lambda i: (i, 0)),
            pl.BlockSpec((SEQ_LEN, 256), lambda i: (i, 0)),
            pl.BlockSpec((1, 8, SEQ_LEN), lambda i: (i, 0, 0)),
        ],
        out_shape=[
            jax.ShapeDtypeStruct((d, 768), BF),
            jax.ShapeDtypeStruct((rows, 640), BF),
            jax.ShapeDtypeStruct((rows, 256), BF),
            jax.ShapeDtypeStruct((seqs, 8, SEQ_LEN), F32),
        ],
        compiler_params=params("attend"),
        cost_estimate=cost(6e9, 8e6),
        name="attend",
    )(place, n1, bias, *[array for array, _ in pieces])


def middle_kernel(x_ref, table_ref, *refs):
    mixed, weights, (mid_ref, n2_ref) = refs[0:4], refs[4:8], refs[8:]
    attended = table_ref[BIAS_OUT]
    for m, w in zip(mixed, weights):
        attended = attended + dot_nt(m[...], w[...])
    middle = x_ref[...].astype(F32) + attended
    mid_ref[...] = middle
    unit, _ = unit_rows(middle)
    normed = unit * table_ref[GAIN_MLP] + table_ref[SHIFT_MLP]
    n2_ref[...] = normed.astype(BF)


def middle_call(x, table, mixed, weights):
    rows, d = x.shape
    tile = 256
    by_rows = pl.BlockSpec((tile, d), lambda i: (i, 0))
    return pl.pallas_call(
        middle_kernel,
        grid=(rows // tile,),
        in_specs=[by_rows, whole(table.shape)]
        + [pl.BlockSpec((tile, 256), lambda i: (i, 0))] * 4
        + [pl.BlockSpec((d, 256), lambda i: (0, 2))] * 4,
        out_specs=[by_rows, by_rows],
        out_shape=[
            jax.ShapeDtypeStruct((rows, d), F32),
            jax.ShapeDtypeStruct((rows, d), BF),
        ],
        compiler_params=params("middle"),
        cost_estimate=cost(2 * rows * d * 1024, 16e6),
        name="middle",
    )(x, table, *mixed, *weights)


def gelu_both(value):
    cumulative = 0.5 + 0.5 * lax.erf(value * 2.0**-0.5)
    bell = jnp.exp(-0.5 * value * value)
    return value * cumulative, cumulative + value * bell * (2.0 * 3.141592653589793) ** -0.5


def store_all(ref, lead, place_ref, value, count, got_ref=None, got_lead=()):
    z, x = place_ref[0], place_ref[1]
    size = value.shape[0] // (2 * count)
    for block in range(2 * count):
        slot = lax.rem(x + block % 2, 2) * count + lax.rem(block // 2 - z + count, count)
        part = value[block * size : (block + 1) * size]
        if got_ref is not None:
            part = part + got_ref[got_lead + (slot,)].astype(F32)
        ref[lead + (slot,)] = part.astype(BF)


def store_split(home_ref, away_ref, got_ref, lead, place_ref, value, count):
    z, x = place_ref[0], place_ref[1]
    size = value.shape[0] // (2 * count)
    for pair in range(count):
        slot = lax.rem(pair - z + count, count)
        first = value[2 * pair * size : (2 * pair + 1) * size]
        second = value[(2 * pair + 1) * size : (2 * pair + 2) * size]
        home = jnp.where(x == 0, first, second) + got_ref[lead + (slot,)].astype(F32)
        away = jnp.where(x == 0, second, first) + got_ref[lead + (count + slot,)].astype(F32)
        home_ref[slot] = home.astype(BF)
        away_ref[slot] = away.astype(BF)


def feed_kernel(count, tokens, has_got, place_ref, n2_ref, cot_ref, bias_ref, *refs):
    ups, downs, refs = refs[: 2 * count], refs[2 * count : 4 * count], refs[4 * count :]
    got_ref = refs[0] if has_got else None
    hidden_ref, pre_ref, sum_ref, up_ref, down_ref, *outs = refs[has_got:]
    place_pieces(place_ref, ups, up_ref)
    place_pieces(place_ref, downs, down_ref)
    rows = n2_ref.shape[0]
    up, down, bias = up_ref[...], down_ref[...], bias_ref[...].astype(F32)
    total = jnp.zeros_like(bias)
    for first in range(0, rows, tokens):
        here = slice(first, first + tokens)
        pre = dot(n2_ref[here], up) + bias
        grad_hidden = dot(cot_ref[here], down)
        hidden, slope = gelu_both(pre)
        hidden_ref[here] = hidden.astype(BF)
        grad_pre = (grad_hidden * slope).astype(BF)
        pre_ref[here] = grad_pre
        total = total + jnp.sum(grad_pre.astype(F32), axis=0, keepdims=True)
    sum_ref[...] = total
    grads = (dot_tn(n2_ref[...], pre_ref[...]), dot_tn(cot_ref[...], hidden_ref[...]))
    if has_got:
        store_split(outs[0], outs[1], got_ref, (0,), place_ref, grads[0], count)
        store_all(outs[2], (), place_ref, grads[1], count, got_ref, (1,))
    else:
        store_all(outs[0], (0,), place_ref, grads[0], count)
        store_all(outs[0], (1,), place_ref, grads[1], count)


def feed_call(place, count, n2, cot, ups, downs, small, got=None):
    rows, d = n2.shape
    units = ups[0][0].shape[-1]
    tile = 256
    shard = d // (2 * count)
    cols = lambda n: pl.BlockSpec((n, tile), lambda i: (0, i))
    hid = jax.ShapeDtypeStruct((rows, units), BF)
    both_spec = pl.BlockSpec((2, 2 * count, shard, tile), lambda i: (0, 0, 0, i))
    if got is None:
        grad_specs = [both_spec]
        grads = [jax.ShapeDtypeStruct((2, 2 * count, shard, units), BF)]
    else:
        grad_specs = [pl.BlockSpec((n, shard, tile), lambda i: (0, 0, i)) for n in (count, count, 2 * count)]
        grads = [jax.ShapeDtypeStruct((n, shard, units), BF) for n in (count, count, 2 * count)]
    gots = () if got is None else (got,)
    return pl.pallas_call(
        functools.partial(feed_kernel, count, 512, len(gots)),
        grid=(units // tile,),
        in_specs=[
            pl.BlockSpec(memory_space=pltpu.SMEM),
            whole((rows, d)),
            whole((rows, d)),
            pl.BlockSpec((1, tile), lambda i: (0, SMALL_ATTN // tile + i)),
        ]
        + piece_specs(ups, tile, lambda i: i)
        + piece_specs(downs, tile, lambda i: i)
        + [both_spec] * len(gots),
        out_specs=[cols(rows)] * 2 + [cols(1)] + [cols(d)] * 2 + grad_specs,
        out_shape=[hid] * 2
        + [jax.ShapeDtypeStruct((1, units), F32)]
        + [jax.ShapeDtypeStruct((d, units), BF)] * 2
        + grads,
        compiler_params=params("feed"),
        cost_estimate=cost(2 * 4 * rows * d * units, 16e6, rows * units),
        name="feed",
    )(place, n2, cot, small, *[a for a, _ in ups], *[a for a, _ in downs], *gots)


def turn_kernel(_, mid_ref, cot_ref, table_ref, *refs):
    pre, ups = refs[0:4], refs[4:8]
    gmid_ref, grows_ref, gain_sum, shift_sum, bias_sum = refs[-5:]
    grad = None
    for g, w in zip(pre, ups):
        term = dot_nt(g[...], w[...])
        grad = term if grad is None else grad + term
    unit, spread = unit_rows(mid_ref[...])
    add_sum(gain_sum, grad * unit)
    add_sum(shift_sum, grad)
    back = norm_back(grad, unit, spread, table_ref[GAIN_MLP])
    grad_middle = cot_ref[...].astype(F32) + back
    gmid_ref[...] = grad_middle
    rows = grad_middle.astype(BF)
    grows_ref[...] = rows
    add_sum(bias_sum, rows.astype(F32))


def turn_call(place, middle, cot, table, pre, ups):
    rows, d = middle.shape
    units = ups[0].shape[1]
    tile = 256
    by_rows = pl.BlockSpec((tile, d), lambda i: (i, 0))
    kept = pl.BlockSpec((d, units), lambda i: (0, 0), pipeline_mode=pl.Buffered(1))
    total = jax.ShapeDtypeStruct((1, d), F32)
    return pl.pallas_call(
        turn_kernel,
        grid=(rows // tile,),
        in_specs=[pl.BlockSpec(memory_space=pltpu.SMEM), by_rows, by_rows, whole(table.shape)]
        + [pl.BlockSpec((tile, units), lambda i: (i, 0))] * 4
        + [kept] * 4,
        out_specs=[by_rows] * 2 + [whole((1, d))] * 3,
        out_shape=[
            jax.ShapeDtypeStruct((rows, d), F32),
            jax.ShapeDtypeStruct((rows, d), BF),
            total,
            total,
            total,
        ],
        compiler_params=params("turn"),
        cost_estimate=cost(2 * 4 * rows * d * units, 20e6),
        name="turn",
    )(place, middle, cot, table, *pre, *ups)


def output_kernel(_, mid_ref, table_ref, *refs):
    hidden, downs, out_ref = refs[0:4], refs[4:8], refs[-1]
    mlp = table_ref[BIAS_DOWN]
    for h, w in zip(hidden, downs):
        mlp = mlp + dot_nt(h[...], w[...])
    out_ref[...] = (mid_ref[...] + mlp).astype(BF)


def output_call(place, middle, table, hidden, downs):
    rows, d = middle.shape
    units = downs[0].shape[1]
    tile = 256
    by_rows = pl.BlockSpec((tile, d), lambda i: (i, 0))
    kept = pl.BlockSpec((d, units), lambda i: (0, 0), pipeline_mode=pl.Buffered(1))
    return pl.pallas_call(
        output_kernel,
        grid=(rows // tile,),
        in_specs=[pl.BlockSpec(memory_space=pltpu.SMEM), by_rows, whole(table.shape)]
        + [pl.BlockSpec((tile, units), lambda i: (i, 0))] * 4
        + [kept] * 4,
        out_specs=by_rows,
        out_shape=jax.ShapeDtypeStruct((rows, d), BF),
        compiler_params=params("output"),
        cost_estimate=cost(2 * 4 * rows * d * units, 16e6),
        name="output",
    )(place, middle, table, *hidden, *downs)


def attend_back_kernel(count, has_got, place_ref, lse_ref, grows_hbm, w_hbm, proj_hbm, n1_hbm, mixed_hbm, *refs):
    got_hbm = refs[0] if has_got else None
    gproj_hbm, sum_ref, *grad_refs = refs[has_got : has_got + 3 + has_got]
    grows, w, projs, n1, mixed, got, gproj_all, sems, out_sems = refs[has_got + 3 + has_got :]
    seqs = lse_ref.shape[0]

    def of_seq(seq):
        return pl.ds(pl.multiple_of(seq * SEQ_LEN, SEQ_LEN), SEQ_LEN)

    def seq_copies(seq):
        return [
            pltpu.make_async_copy(hbm.at[of_seq(seq)], ref.at[of_seq(seq)], sems.at[i, seq])
            for i, (hbm, ref) in enumerate(((grows_hbm, grows), (proj_hbm, projs)))
        ]

    def out_copy(seq):
        return pltpu.make_async_copy(gproj_all.at[of_seq(seq)], gproj_hbm.at[of_seq(seq)], out_sems.at[seq])

    w_copy = pltpu.make_async_copy(w_hbm.at[:, 512:768], w, sems.at[2, 0])
    late = [
        pltpu.make_async_copy(n1_hbm, n1, sems.at[3, 0]),
        pltpu.make_async_copy(mixed_hbm, mixed, sems.at[4, 0]),
    ]
    if has_got:
        late.append(pltpu.make_async_copy(got_hbm, got, sems.at[5, 0]))
    w_copy.start()
    for seq in range(seqs):
        for copy in seq_copies(seq):
            copy.start()
    for copy in late:
        copy.start()
    w_copy.wait()

    @pl.loop(0, seqs)
    def _(seq):
        for copy in seq_copies(seq):
            copy.wait()
        projected = projs[of_seq(seq)]
        grad_mixed = dot(grows[of_seq(seq)], w[...]).astype(BF)
        out = gproj_all.at[of_seq(seq)]
        parts = {}
        early = lax.broadcasted_iota(jnp.int32, (HALF, HALF), 0) <= lax.broadcasted_iota(jnp.int32, (HALF, HALF), 1)
        jobs = []
        for head, (qt, kt, vt, qk_lane, v_lane) in enumerate(HEAD_PLACES):
            mt = 0 if head == 2 else 1
            query = lane_keep(projected[:, qt * 128 : qt * 128 + 128], qk_lane) * BF(0.125)
            keys = projected[:, kt * 128 : kt * 128 + 128]
            values = projected[:, vt * 128 : vt * 128 + 128]
            grads = lane_keep(grad_mixed[:, mt * 128 : mt * 128 + 128], v_lane)
            parts["k", head] = [None, None]
            parts["v", head] = [None, None]
            for block in range(2):
                rows = slice(block * HALF, block * HALF + HALF)
                jobs.append((head, block, qk_lane, query[rows], keys, values, grads[rows]))

        def first_stage(job):
            head, block, _, qb, keys, values, gb = job
            last = block * HALF + HALF
            return dot_nt(keys[0:last], qb), dot_nt(values[0:last], gb)

        def last_stage(job, scores, gprobs):
            head, block, qk_lane, qb, keys, values, gb = job
            last = block * HALF + HALF
            lse = lse_ref[seq, head : head + 1, last - HALF : last]
            probs = jnp.exp(scores - lse)
            corner = jnp.where(early, probs[last - HALF :], 0.0)
            probs = jnp.concatenate([probs[: last - HALF], corner], axis=0) if block else corner
            both = probs * gprobs
            delta = jnp.sum(both, axis=0, keepdims=True)
            gscores = (both - probs * delta).astype(BF)
            gq = dot_tn(keys[0:last], gscores) * 0.125
            parts["q", head, block] = gq[qk_lane : qk_lane + HEAD_DIM]
            gk = dot(gscores, qb)
            gv = dot(probs.astype(BF), gb)
            for name, got in (("k", gk), ("v", gv)):
                held = parts[name, head]
                for b in range(block + 1):
                    part = got[b * HALF : b * HALF + HALF]
                    held[b] = part if held[b] is None else held[b] + part

        waiting = None
        for job in jobs + [None]:
            ahead = None if job is None else (job, *first_stage(job))
            if waiting is not None:
                last_stage(*waiting)
            waiting = ahead
        for block in range(2):
            rows = slice(block * HALF, block * HALF + HALF)
            pair = jnp.concatenate([parts["q", 0, block], parts["q", 1, block]], axis=0).T
            lone = parts["q", 2, block]
            lone = jnp.concatenate([lone, jnp.zeros_like(lone)], axis=0).T
            out[rows, 0:128] = pair.astype(BF)
            out[rows, 128:256] = (parts["k", 0][block] + parts["k", 1][block]).astype(BF)
            out[rows, 256:384] = (parts["v", 0][block] + parts["v", 1][block]).astype(BF)
            out[rows, 384:512] = (lone + parts["v", 2][block]).astype(BF)
            out[rows, 512:640] = parts["k", 2][block].astype(BF)
        out_copy(seq).start()

    gproj = gproj_all[...]
    sum_ref[...] = jnp.sum(gproj.astype(F32), axis=0, keepdims=True)
    for copy in late:
        copy.wait()
    grad_a = dot_tn(n1[...], gproj)
    grad_b = dot_tn(grows[...], mixed[...])
    grad = jnp.concatenate(
        [grad_a[:, 0:512], grad_a[:, 512:640] + grad_b[:, 0:128], grad_b[:, 128:256]], axis=1
    )
    if has_got:
        store_split(*grad_refs, got, (), place_ref, grad, count)
    else:
        store_all(*grad_refs, (), place_ref, grad, count)
    for seq in range(seqs):
        out_copy(seq).wait()


def attend_back_call(place, count, grows, n1, w, proj, mixed, lse, got=None):
    rows, d = grows.shape
    seqs = rows // SEQ_LEN
    shard = d // (2 * count)
    gots = () if got is None else (got,)
    both = (2 * count, shard, 768)
    grads = [both] if got is None else [(count, shard, 768)] * 2
    hbm = pl.BlockSpec(memory_space=pl.ANY)
    return pl.pallas_call(
        functools.partial(attend_back_kernel, count, len(gots)),
        grid=(1,),
        in_specs=[pl.BlockSpec(memory_space=pltpu.SMEM), whole(lse.shape)] + [hbm] * (5 + len(gots)),
        out_specs=[hbm, whole((1, 640))] + [whole(g) for g in grads],
        out_shape=[jax.ShapeDtypeStruct((rows, 640), BF), jax.ShapeDtypeStruct((1, 640), F32)]
        + [jax.ShapeDtypeStruct(g, BF) for g in grads],
        scratch_shapes=[
            pltpu.VMEM((rows, d), BF),
            pltpu.VMEM((d, 256), BF),
            pltpu.VMEM((rows, 640), BF),
            pltpu.VMEM((rows, d), BF),
            pltpu.VMEM((rows, 256), BF),
            pltpu.VMEM(both if got is not None else (8, 16, 128), BF),
            pltpu.VMEM((rows, 640), BF),
            pltpu.SemaphoreType.DMA((6, seqs)),
            pltpu.SemaphoreType.DMA((seqs,)),
        ],
        compiler_params=params("attend_back"),
        cost_estimate=cost(10e9, 12e6),
        name="attend_back",
    )(place, lse, grows, w, proj, n1, mixed, *gots)


def finish_kernel(_, x_ref, gmid_ref, table_ref, *refs):
    gproj, weights, known, sum_proj, sum_up = refs[0:4], refs[4:8], refs[8:12], refs[12:16], refs[16:20]
    out_ref, keep_ref, away_ref, gain_sum, shift_sum = refs[20:]
    grad = None
    for g, w in zip(gproj, weights):
        term = dot_nt(g[...], w[...])
        grad = term if grad is None else grad + term
    unit, spread = unit_rows(x_ref[...].astype(F32))
    add_sum(gain_sum, grad * unit)
    add_sum(shift_sum, grad)
    back = norm_back(grad, unit, spread, table_ref[GAIN_ATTN])
    out_ref[...] = (gmid_ref[...] + back).astype(BF)

    @pl.when(pl.program_id(0) == pl.num_programs(0) - 1)
    def _():
        shared = jnp.concatenate(
            [r[...] for r in known] + [gain_sum[...], shift_sum[...]], axis=1
        )
        for dy in range(2):
            for dc, ref in enumerate((keep_ref, away_ref)):
                row = jnp.concatenate([shared, sum_proj[2 * dy + dc][...], sum_up[2 * dy + dc][...]], axis=1)
                ref[dy : dy + 1] = row


def finish_call(place, x, gmid, table, gproj, weights, known, sum_proj, sum_up):
    rows, d = x.shape
    tile = 256
    by_rows = pl.BlockSpec((tile, d), lambda i: (i, 0))
    width = 6 * d + sum_proj[0].shape[1] + sum_up[0].shape[1]
    return pl.pallas_call(
        finish_kernel,
        grid=(rows // tile,),
        in_specs=[pl.BlockSpec(memory_space=pltpu.SMEM), by_rows, by_rows, whole(table.shape)]
        + [pl.BlockSpec((tile, 640), lambda i: (i, 0))] * 4
        + [pl.BlockSpec((d, 640), lambda i: (0, 0))] * 4
        + [whole(v.shape) for v in (*known, *sum_proj, *sum_up)],
        out_specs=[by_rows, whole((2, width)), whole((2, width))],
        out_shape=[jax.ShapeDtypeStruct((rows, d), BF)] + [jax.ShapeDtypeStruct((2, width), F32)] * 2,
        scratch_shapes=[pltpu.VMEM((1, d), F32)] * 2,
        compiler_params=params("finish"),
        cost_estimate=cost(2 * 4 * rows * d * 640, 16e6),
        name="finish",
    )(place, x, gmid, table, *gproj, *weights, *known, *sum_proj, *sum_up)


class Links:
    def __init__(self, mesh):
        self.count = mesh.shape["fsdp"] // 2
        places = [
            (z, x, y, c)
            for z in range(self.count)
            for x in range(2)
            for y in range(2)
            for c in range(2)
        ]

        def index(z, x, y, c):
            return ((z * 2 + x) * 2 + y) * 2 + c

        def pairs(move):
            return [(index(*p), index(*move(*p))) for p in places]

        self.core = pairs(lambda z, x, y, c: (z, x, y, 1 - c))
        self.y = pairs(lambda z, x, y, c: (z, x, 1 - y, c))
        self.x = pairs(lambda z, x, y, c: (z, 1 - x, y, c))
        self.ring = pairs(lambda z, x, y, c: ((z + 1) % self.count, x, y, c))
        self.far = [
            pairs(lambda z, x, y, c, k=k: ((z + k) % self.count, x, y, c)) for k in range(self.count)
        ]
        self.back = [
            pairs(lambda z, x, y, c, k=k: ((z - k) % self.count, x, y, c)) for k in range(self.count)
        ]
        self.xy = pairs(lambda z, x, y, c: (z, 1 - x, 1 - y, c))
        self.trees = []
        step = 1
        while step < self.count:
            size = 4 if step * 4 <= self.count else 2
            self.trees.append(
                [pairs(lambda z, x, y, c, b=step * k: (z ^ b, x, y, c)) for k in range(1, size)]
            )
            step *= size

    @staticmethod
    def send(value, pairs):
        return lax.ppermute(value, AXES, pairs)


def plus(*terms, kind=BF):
    total = terms[0].astype(F32)
    for term in terms[1:]:
        total = total + term.astype(F32)
    return total.astype(kind)


def tie(value, *others):
    return lax.optimization_barrier((value, others))[0]


def ring_from(links, first):
    held = [first]
    for _ in range(links.count - 1):
        held.append(links.send(held[-1], links.ring))
    return held


def gather_and_attend(links, place, attn, up, down, n1, smalls, layer_input, table):
    n = links.count
    half = n // 2
    small_y = links.send(smalls, links.y)

    near = [jnp.stack([attn, down])]
    done = (n1,)
    for k in range(1, n):
        now = near[-1] if k == 1 else tie(near[-1], *done)
        if k == 3:
            joint = links.send(jnp.concatenate([now, steps[0].reshape((4,) + up.shape)]), links.ring)
            near.append(joint[:2])
            steps.append(joint[2:].reshape(steps[0].shape))
        else:
            near.append(links.send(now, links.ring))
        done = (near[-1],)
        if k == 1:
            pair = jnp.stack([up, links.send(up, links.x)])
            done += (pair, n1, smalls)
        if k == 2:
            steps = [jnp.stack([pair, links.send(tie(pair, near[1]), links.y)])]
            done += (steps[0], small_y)
        if k == half:
            lines = [jnp.stack([v[0] for v in near[:half]])]
            others = [links.send(lines[0], links.x)]
            done += (others[0],)
        if k == half + 1:
            quads = [links.send(tie(jnp.stack([lines[0], others[0]]), *near[half:-1]), links.y)]
            smalls = [smalls, links.send(smalls, links.core), small_y, links.send(small_y, links.core)]
            done += (smalls[1], smalls[3], quads[0])

    lines.append(tie(jnp.stack([v[0] for v in near[half:]]), *done))
    others.append(links.send(lines[1], links.x))
    line = jnp.stack([v[1] for v in near])
    beyond = [links.send(tie(line, *done), links.y)]
    steps.append(links.send(tie(steps[-1], *done), links.ring))
    core = lambda values: [links.send(v, links.core) for v in values]

    def from_lines(*pair):
        return [(v[k // half], (k % half,)) for v in pair for k in range(n)]

    def from_quads(quads):
        return [(quads[k // half], (dx, k % half)) for dx in range(2) for k in range(n)]

    quads.append(links.send(jnp.stack([lines[1], others[1]]), links.y))
    far = links.send(tie(line, others[1]), links.x)

    attn_w, proj, mixed, lse = [], [], [], []

    def attend(pieces, *before):
        j = len(proj)
        w, p, m, s = attend_call(tie(place, *before) if before else place, n1, pieces, smalls[j])
        attn_w.append(w)
        proj.append(p)
        mixed.append(m)
        lse.append(s)

    attend(from_lines(lines, others))
    attend(from_lines(core(lines), core(others)), mixed[0])
    quads_core = core([quads[0], tie(quads[1], mixed[1])])
    beyond.append(links.send(tie(beyond[0], far), links.x))
    for _ in range(3, n):
        steps.append(links.send(tie(steps[-1], mixed[1]), links.ring))
    attend(from_quads(quads), mixed[1], quads[1], far, steps[2])
    attend(from_quads(quads_core), mixed[2])
    middle, n2 = middle_call(layer_input, table, mixed, attn_w)

    steps[-1] = tie(steps[-1], mixed[3])
    up_core = core(steps)
    up_w = [[(v, (dy, dx)) for dx in range(2) for v in vs] for dy in range(2) for vs in (steps, up_core)]
    down_w = [
        [(v, (k,)) for v in vs for k in range(n)]
        for pair in ((line, far), beyond)
        for vs in (pair, core(pair))
    ]
    return attn_w, up_w, down_w, proj, mixed, lse, smalls, middle, n2


def spread_sum(links, home):
    got = [links.send(home[k], links.far[k]) for k in range(1, links.count)]
    return plus(home[0], *got, kind=F32)


def sum_all(links, keep, away):
    rows = keep + links.send(away, links.core)
    near, far = rows[0:1], rows[1:2]
    total = (near + links.send(near, links.x)) + (
        links.send(far, links.y) + links.send(far, links.xy)
    )
    for pairs in links.trees:
        got = [total] + [links.send(total, p) for p in pairs]
        while len(got) > 1:
            got = [got[i] + got[i + 1] for i in range(0, len(got), 2)]
        total = got[0]
    return total


def pack_attn(w_qkv, w_out):
    q, k, v, o = w_qkv[:, 0], w_qkv[:, 1], w_qkv[:, 2], w_out.T
    return jnp.concatenate(
        [q[:, :128], k[:, :128], v[:, :128], q[:, 128:], v[:, 128:], k[:, 128:], o[:, 128:], o[:, :128]],
        axis=1,
    )


def unpack_attn(g):
    q = jnp.concatenate([g[:, 0:128], g[:, 384:448]], axis=1)
    k = jnp.concatenate([g[:, 128:256], g[:, 512:576]], axis=1)
    v = jnp.concatenate([g[:, 256:384], g[:, 448:512]], axis=1)
    o = jnp.concatenate([g[:, 640:768], g[:, 576:640]], axis=1)
    return jnp.stack([q, k, v], axis=1), o.T


def body(
    links,
    layer_input,
    w_qkv,
    bias_qv,
    w_out,
    bias_out,
    gain_attn,
    shift_attn,
    gain_mlp,
    shift_mlp,
    w_up,
    bias_up,
    w_down,
    bias_down,
    cotangent,
):
    fsdp = lax.axis_index("fsdp")
    place = jnp.stack([fsdp // 2, fsdp % 2]).astype(jnp.int32)
    count = links.count
    n1, sum_down, small, table = start_call(
        layer_input,
        cotangent,
        bias_qv,
        bias_up,
        (bias_out, gain_attn, shift_attn, gain_mlp, shift_mlp, bias_down),
    )
    attn_w, up_w, down_w, proj, mixed, lse, smalls, middle, n2 = gather_and_attend(
        links, place, pack_attn(w_qkv, w_out), w_up, w_down.T, n1, small, layer_input, table
    )

    hidden, pre, sum_up = [None] * 4, [None] * 4, [None] * 4
    up_home, up_away, down_sum = [None] * 2, [None] * 2, [None] * 2
    gots = [None] * 4
    for j in (1, 3, 0, 2):
        out = feed_call(
            place, count, n2, cotangent, up_w[j], down_w[j], smalls[j], gots[j]
        )
        hidden[j], pre[j], sum_up[j], up_w[j], down_w[j] = out[0:5]
        if j % 2:
            gots[j - 1] = links.send(out[5], links.core)
        else:
            up_home[j // 2], up_away[j // 2], down_sum[j // 2] = out[5:8]

    got_x0 = links.send(up_away[0], links.x)
    got_x1 = links.send(up_away[1], links.x)
    got_down = links.send(down_sum[1], links.y)
    gmid, grows, gain_two, shift_two, sum_out = turn_call(
        place, middle, cotangent, table, pre, up_w
    )

    gproj, sum_proj = [None] * 4, [None] * 4
    attn_home, attn_away = [None] * 2, [None] * 2

    def back(j, got, *before):
        out = attend_back_call(
            tie(place, *before) if before else place,
            count,
            grows,
            n1,
            attn_w[j],
            proj[j],
            mixed[j],
            lse[j],
            got,
        )
        gproj[j], sum_proj[j] = out[0:2]
        if j % 2:
            return links.send(out[2], links.core)
        attn_home[j // 2], attn_away[j // 2] = out[2:4]

    got_three = back(3, None, got_x0)
    up_beyond = plus(up_home[1], got_x1)
    got_up = links.send(up_beyond, links.y)
    got_one = back(1, None, up_beyond)
    down_away = plus(down_sum[0][count:], got_down[count:])
    got_x = links.send(down_away, links.x)
    back(2, got_three, down_away)
    got_a1 = links.send(attn_away[1], links.x)
    up_all = plus(up_home[0], got_x0, got_up)
    down_all = plus(down_sum[0][:count], got_down[:count], got_x)
    back(0, got_one, up_all, down_all, sum_proj[2])
    grad_up = spread_sum(links, up_all)
    grad_down = spread_sum(links, down_all)
    got_a0 = links.send(attn_away[0], links.x)
    attn_beyond = plus(attn_home[1], got_a1)
    got_attn = links.send(attn_beyond, links.y)
    grad_input, keep, away = finish_call(
        tie(place, attn_beyond, grad_up),
        layer_input,
        gmid,
        table,
        gproj,
        attn_w,
        (sum_out, sum_down, gain_two, shift_two),
        sum_proj,
        sum_up,
    )
    attn_all = plus(tie(attn_home[0], keep), got_a0, got_attn)
    parts = [attn_all[0]] + [links.send(attn_all[k], links.far[k]) for k in range(1, count)]
    before = (keep, attn_all, grad_up, grad_down)
    layer_output = output_call(tie(place, *before), middle, table, hidden, down_w)
    sums = sum_all(links, keep, tie(away, layer_output, *parts))
    grad_attn = plus(*parts, kind=F32)

    d = layer_input.shape[1]
    heads = bias_qv.shape[1]
    vec = sums[0]
    total_out, total_down, gain_two, shift_two, gain_one, shift_one = (
        vec[i * d : (i + 1) * d] for i in range(6)
    )
    own = vec[6 * d :]
    total_qv = jnp.stack(
        [
            jnp.concatenate([own[0:128], own[384:448]]),
            jnp.concatenate([own[256:384], own[448:512]]),
        ]
    )
    total_up = own[640:]

    shard_qkv, shard_out = unpack_attn(grad_attn)
    return (
        layer_output,
        grad_input,
        shard_qkv,
        total_qv,
        shard_out,
        total_out,
        gain_one,
        shift_one,
        gain_two,
        shift_two,
        grad_up,
        total_up,
        grad_down.T,
        total_down,
    )


def solution(mesh):
    tokens = P(("fsdp", "tp"), None)
    placed = (
        tokens,
        P("fsdp", None, "tp"),
        P(None, "tp"),
        P("tp", "fsdp"),
        P(),
        P(),
        P(),
        P(),
        P(),
        P("fsdp", "tp"),
        P("tp"),
        P("tp", "fsdp"),
        P(),
        tokens,
    )
    return jax.shard_map(
        functools.partial(body, Links(mesh)),
        mesh=mesh,
        in_specs=placed,
        out_specs=(
            tokens,
            tokens,
            P("fsdp", None, "tp"),
            P(None, "tp"),
            P("tp", "fsdp"),
            P(),
            P(),
            P(),
            P(),
            P(),
            P("fsdp", "tp"),
            P("tp"),
            P("tp", "fsdp"),
            P(),
        ),
        check_vma=False,
    )
```

```python
import functools

import jax
import jax.numpy as jnp
from jax import lax
from jax.experimental import pallas as pl
from jax.experimental.pallas import tpu as pltpu
from jax.sharding import PartitionSpec as P

HEAD_DIM = 64
SEQ_LEN = 512
HALF = 256
EPS = 1e-05
AXES = ("fsdp", "tp")
BF = jnp.bfloat16
F32 = jnp.float32
MB = 1 << 20
SHARE = 0.3
BIAS_OUT, GAIN_ATTN, SHIFT_ATTN, GAIN_MLP, SHIFT_MLP, BIAS_DOWN = (slice(i, i + 1) for i in range(6))
VMEM_MB = {"start": 60, "feed": 60, "attend_back": 60, "turn": 60, "finish": 60, "output": 60}
SMALL_ATTN = 768


def dot(left, right):
    return lax.dot_general(left, right, (((1,), (0,)), ((), ())), preferred_element_type=F32)


def dot_nt(left, right):
    return lax.dot_general(left, right, (((1,), (1,)), ((), ())), preferred_element_type=F32)


def dot_tn(left, right):
    return lax.dot_general(left, right, (((0,), (0,)), ((), ())), preferred_element_type=F32)


def whole(shape):
    zeros = (0,) * len(shape)
    return pl.BlockSpec(shape, lambda *_: zeros)


def params(kernel):
    return pltpu.CompilerParams(vmem_limit_bytes=VMEM_MB.get(kernel, 36) * MB)


def cost(flops, nbytes, trans=0):
    return pl.CostEstimate(
        flops=int(flops * SHARE), bytes_accessed=int(nbytes * SHARE), transcendentals=int(trans * SHARE)
    )


def unit_rows(rows):
    centre = rows - jnp.mean(rows, axis=-1, keepdims=True)
    spread = lax.rsqrt(jnp.mean(centre * centre, axis=-1, keepdims=True) + EPS)
    return centre * spread, spread


def norm_back(grad_out, unit, spread, gain):
    scaled = grad_out * gain
    inner = jnp.mean(scaled * unit, axis=-1, keepdims=True)
    return spread * (scaled - jnp.mean(scaled, axis=-1, keepdims=True) - unit * inner)


def start_sums(*refs):
    @pl.when(pl.program_id(0) == 0)
    def _():
        for ref in refs:
            ref[...] = jnp.zeros_like(ref)


def add_sum(ref, value):
    ref[...] += jnp.sum(value, axis=0, keepdims=True)


def start_kernel(x_ref, cot_ref, qv_ref, up_ref, *refs):
    vectors, (n1_ref, sum_ref, small_ref, table_ref) = refs[:6], refs[6:]
    start_sums(sum_ref)

    @pl.when(pl.program_id(0) == 0)
    def _():
        for i, ref in enumerate(vectors):
            table_ref[i : i + 1] = ref[...].astype(F32).reshape(1, -1)
        small_ref[...] = jnp.zeros_like(small_ref)
        for c in range(2):
            pair, lone = (0, 384) if c == 0 else (256, 448)
            row = qv_ref[c : c + 1].astype(F32)
            small_ref[:, pair : pair + 128] = row[:, 0:128]
            small_ref[:, lone : lone + HEAD_DIM] = row[:, 128:192]
        small_ref[:, SMALL_ATTN:] = up_ref[...].astype(F32).reshape(1, -1)

    unit, _ = unit_rows(x_ref[...].astype(F32))
    normed = unit * table_ref[GAIN_ATTN] + table_ref[SHIFT_ATTN]
    n1_ref[...] = normed.astype(BF)
    add_sum(sum_ref, cot_ref[...].astype(F32))


def start_call(x, cot, bias_qv, bias_up, vectors):
    rows, d = x.shape
    units = bias_up.shape[0]
    tile = 256
    by_rows = pl.BlockSpec((tile, d), lambda i: (i, 0))
    return pl.pallas_call(
        start_kernel,
        grid=(rows // tile,),
        in_specs=[by_rows, by_rows, whole(bias_qv.shape), whole(bias_up.shape)]
        + [whole(v.shape) for v in vectors],
        out_specs=[by_rows]
        + [whole((1, d)), whole((1, SMALL_ATTN + units)), whole((8, d))],
        out_shape=[
            jax.ShapeDtypeStruct((rows, d), BF),
            jax.ShapeDtypeStruct((1, d), F32),
            jax.ShapeDtypeStruct((1, SMALL_ATTN + units), F32),
            jax.ShapeDtypeStruct((8, d), F32),
        ],
        compiler_params=params("start"),
        cost_estimate=cost(0, 10 * rows * d),
        name="start",
    )(x, cot, bias_qv, bias_up, *vectors)


def piece_specs(pieces, cols, index):
    rows = pieces[0][0].shape[-2]
    return [
        pl.BlockSpec((1,) * len(lead) + (rows, cols), lambda i, lead=lead: lead + (0, index(i)))
        for _, lead in pieces
    ]


def place_pieces(place_ref, pieces, out_ref):
    count = len(pieces) // 2
    z, x = place_ref[0], place_ref[1]
    for k in range(count):
        for dx in range(2):
            piece = pieces[dx * count + k]
            size, cols = piece.shape[-2:]
            slot = lax.rem(z - k + count, count) * 2 + lax.rem(x + dx, 2)
            out_ref[pl.ds(pl.multiple_of(slot * size, size), size)] = piece[...].reshape(size, cols)


HEAD_PLACES = ((0, 1, 2, 0, 0), (0, 1, 2, 64, 64), (3, 4, 3, 0, 64))


def lane_keep(tile, first):
    lanes = lax.broadcasted_iota(jnp.int32, tile.shape, 1)
    keep = (lanes >= first) & (lanes < first + HEAD_DIM)
    return jnp.where(keep, tile, jnp.zeros_like(tile))


def score_block(keys, query, start, stop, first_query):
    scores = dot_nt(keys[start:stop], query)
    if stop - 1 > first_query:
        key_idx = lax.broadcasted_iota(jnp.int32, scores.shape, 0) + start
        query_idx = lax.broadcasted_iota(jnp.int32, scores.shape, 1) + first_query
        scores = jnp.where(key_idx <= query_idx, scores, -1e30)
    return scores


def attend_kernel(place_ref, n1_ref, bias_ref, *refs):
    pieces, (w_ref, proj_ref, mixed_ref, lse_ref) = refs[:-4], refs[-4:]

    @pl.when(pl.program_id(0) == 0)
    def _():
        place_pieces(place_ref, pieces, w_ref)

    projected = (dot(n1_ref[...], w_ref[:, 0:640]) + bias_ref[...].astype(F32)).astype(BF)
    proj_ref[...] = projected
    lse_ref[...] = jnp.zeros_like(lse_ref)
    outs = {}
    for head, (qt, kt, vt, qk_lane, v_lane) in enumerate(HEAD_PLACES):
        query = lane_keep(projected[:, qt * 128 : qt * 128 + 128], qk_lane) * BF(0.125)
        keys = projected[:, kt * 128 : kt * 128 + 128]
        values = projected[:, vt * 128 : vt * 128 + 128]
        for block in range(2):
            first = block * HALF
            last = first + HALF
            scores = score_block(keys, query[first:last], 0, last, first)
            top = jnp.max(scores, axis=0, keepdims=True)
            weight = jnp.exp(scores - top)
            total = jnp.sum(weight, axis=0, keepdims=True)
            mixed = dot_tn(values[0:last], weight.astype(BF)) * (1.0 / total)
            outs[head, block] = mixed[v_lane : v_lane + HEAD_DIM]
            lse_ref[0, head : head + 1, first:last] = top + jnp.log(total)
    for block in range(2):
        first = block * HALF
        rows = slice(first, first + HALF)
        single = jnp.concatenate([jnp.zeros_like(outs[2, block]), outs[2, block]], axis=0)
        pair = jnp.concatenate([outs[0, block], outs[1, block]], axis=0)
        mixed_ref[rows, 0:128] = single.T.astype(BF)
        mixed_ref[rows, 128:256] = pair.T.astype(BF)


def attend_call(place, n1, pieces, bias):
    rows, d = n1.shape
    seqs = rows // SEQ_LEN
    return pl.pallas_call(
        attend_kernel,
        grid=(seqs,),
        in_specs=[
            pl.BlockSpec(memory_space=pltpu.SMEM),
            pl.BlockSpec((SEQ_LEN, d), lambda i: (i, 0)),
            pl.BlockSpec((1, 640), lambda i: (0, 0)),
        ]
        + piece_specs(pieces, 768, lambda i: 0),
        out_specs=[
            whole((d, 768)),
            pl.BlockSpec((SEQ_LEN, 640), lambda i: (i, 0)),
            pl.BlockSpec((SEQ_LEN, 256), lambda i: (i, 0)),
            pl.BlockSpec((1, 8, SEQ_LEN), lambda i: (i, 0, 0)),
        ],
        out_shape=[
            jax.ShapeDtypeStruct((d, 768), BF),
            pltpu.HBM((rows, 640), BF),
            jax.ShapeDtypeStruct((rows, 256), BF),
            pltpu.HBM((seqs, 8, SEQ_LEN), F32),
        ],
        compiler_params=params("attend"),
        cost_estimate=cost(6e9, 8e6),
        name="attend",
    )(place, n1, bias, *[array for array, _ in pieces])


def middle_kernel(x_ref, table_ref, *refs):
    mixed, weights, (mid_ref, n2_ref) = refs[0:4], refs[4:8], refs[8:]
    attended = table_ref[BIAS_OUT]
    for m, w in zip(mixed, weights):
        attended = attended + dot_nt(m[...], w[...])
    middle = x_ref[...].astype(F32) + attended
    mid_ref[...] = middle
    unit, _ = unit_rows(middle)
    normed = unit * table_ref[GAIN_MLP] + table_ref[SHIFT_MLP]
    n2_ref[...] = normed.astype(BF)


def middle_call(x, table, mixed, weights):
    rows, d = x.shape
    tile = 256
    by_rows = pl.BlockSpec((tile, d), lambda i: (i, 0))
    return pl.pallas_call(
        middle_kernel,
        grid=(rows // tile,),
        in_specs=[by_rows, whole(table.shape)]
        + [pl.BlockSpec((tile, 256), lambda i: (i, 0))] * 4
        + [pl.BlockSpec((d, 256), lambda i: (0, 2))] * 4,
        out_specs=[by_rows, by_rows],
        out_shape=[pltpu.HBM((rows, d), F32), pltpu.HBM((rows, d), BF)],
        compiler_params=params("middle"),
        cost_estimate=cost(2 * rows * d * 1024, 16e6),
        name="middle",
    )(x, table, *mixed, *weights)


def gelu_both(value):
    cumulative = 0.5 + 0.5 * lax.erf(value * 2.0**-0.5)
    bell = jnp.exp(-0.5 * value * value)
    return value * cumulative, cumulative + value * bell * (2.0 * 3.141592653589793) ** -0.5


def store_all(ref, lead, place_ref, value, count, got_ref=None, got_lead=()):
    z, x = place_ref[0], place_ref[1]
    size = value.shape[0] // (2 * count)
    for block in range(2 * count):
        slot = lax.rem(x + block % 2, 2) * count + lax.rem(block // 2 - z + count, count)
        part = value[block * size : (block + 1) * size]
        if got_ref is not None:
            part = part + got_ref[got_lead + (slot,)].astype(F32)
        ref[lead + (slot,)] = part.astype(BF)


def store_split(home_ref, away_ref, got_ref, lead, place_ref, value, count):
    z, x = place_ref[0], place_ref[1]
    size = value.shape[0] // (2 * count)
    for pair in range(count):
        slot = lax.rem(pair - z + count, count)
        first = value[2 * pair * size : (2 * pair + 1) * size]
        second = value[(2 * pair + 1) * size : (2 * pair + 2) * size]
        home = jnp.where(x == 0, first, second) + got_ref[lead + (slot,)].astype(F32)
        away = jnp.where(x == 0, second, first) + got_ref[lead + (count + slot,)].astype(F32)
        home_ref[slot] = home.astype(BF)
        away_ref[slot] = away.astype(BF)


def feed_kernel(count, tokens, has_got, place_ref, n2_ref, cot_ref, bias_ref, *refs):
    ups, downs, refs = refs[: 2 * count], refs[2 * count : 4 * count], refs[4 * count :]
    got_ref = refs[0] if has_got else None
    hidden_ref, pre_ref, sum_ref, up_ref, down_ref, *outs = refs[has_got:]
    place_pieces(place_ref, ups, up_ref)
    place_pieces(place_ref, downs, down_ref)
    rows = n2_ref.shape[0]
    up, down, bias = up_ref[...], down_ref[...], bias_ref[...].astype(F32)
    total = jnp.zeros_like(bias)
    for first in range(0, rows, tokens):
        here = slice(first, first + tokens)
        pre = dot(n2_ref[here], up) + bias
        grad_hidden = dot(cot_ref[here], down)
        hidden, slope = gelu_both(pre)
        hidden_ref[here] = hidden.astype(BF)
        grad_pre = (grad_hidden * slope).astype(BF)
        pre_ref[here] = grad_pre
        total = total + jnp.sum(grad_pre.astype(F32), axis=0, keepdims=True)
    sum_ref[...] = total
    grads = (dot_tn(n2_ref[...], pre_ref[...]), dot_tn(cot_ref[...], hidden_ref[...]))
    if has_got:
        store_split(outs[0], outs[1], got_ref, (0,), place_ref, grads[0], count)
        store_all(outs[2], (), place_ref, grads[1], count, got_ref, (1,))
    else:
        store_all(outs[0], (0,), place_ref, grads[0], count)
        store_all(outs[0], (1,), place_ref, grads[1], count)


def feed_call(place, count, n2, cot, ups, downs, small, got=None):
    rows, d = n2.shape
    units = ups[0][0].shape[-1]
    tile = 256
    shard = d // (2 * count)
    cols = lambda n: pl.BlockSpec((n, tile), lambda i: (0, i))
    hid = jax.ShapeDtypeStruct((rows, units), BF)
    both_spec = pl.BlockSpec((2, 2 * count, shard, tile), lambda i: (0, 0, 0, i))
    if got is None:
        grad_specs = [both_spec]
        grads = [jax.ShapeDtypeStruct((2, 2 * count, shard, units), BF)]
    else:
        grad_specs = [pl.BlockSpec((n, shard, tile), lambda i: (0, 0, i)) for n in (count, count, 2 * count)]
        grads = [jax.ShapeDtypeStruct((n, shard, units), BF) for n in (count, count, 2 * count)]
    gots = () if got is None else (got,)
    return pl.pallas_call(
        functools.partial(feed_kernel, count, 512, len(gots)),
        grid=(units // tile,),
        in_specs=[
            pl.BlockSpec(memory_space=pltpu.SMEM),
            whole((rows, d)),
            whole((rows, d)),
            pl.BlockSpec((1, tile), lambda i: (0, SMALL_ATTN // tile + i)),
        ]
        + piece_specs(ups, tile, lambda i: i)
        + piece_specs(downs, tile, lambda i: i)
        + [both_spec] * len(gots),
        out_specs=[cols(rows)] * 2 + [cols(1)] + [cols(d)] * 2 + grad_specs,
        out_shape=[hid] * 2
        + [jax.ShapeDtypeStruct((1, units), F32)]
        + [jax.ShapeDtypeStruct((d, units), BF)] * 2
        + grads,
        compiler_params=params("feed"),
        cost_estimate=cost(2 * 4 * rows * d * units, 16e6, rows * units),
        name="feed",
    )(place, n2, cot, small, *[a for a, _ in ups], *[a for a, _ in downs], *gots)


def turn_kernel(_, mid_ref, cot_ref, table_ref, *refs):
    pre, ups = refs[0:4], refs[4:8]
    gmid_ref, grows_ref, gain_sum, shift_sum, bias_sum = refs[-5:]
    start_sums(gain_sum, shift_sum, bias_sum)
    grad = None
    for g, w in zip(pre, ups):
        term = dot_nt(g[...], w[...])
        grad = term if grad is None else grad + term
    unit, spread = unit_rows(mid_ref[...])
    add_sum(gain_sum, grad * unit)
    add_sum(shift_sum, grad)
    back = norm_back(grad, unit, spread, table_ref[GAIN_MLP])
    grad_middle = cot_ref[...].astype(F32) + back
    gmid_ref[...] = grad_middle
    rows = grad_middle.astype(BF)
    grows_ref[...] = rows
    add_sum(bias_sum, rows.astype(F32))


def turn_call(place, middle, cot, table, pre, ups):
    rows, d = middle.shape
    units = ups[0].shape[1]
    tile = 256
    by_rows = pl.BlockSpec((tile, d), lambda i: (i, 0))
    kept = pl.BlockSpec((d, units), lambda i: (0, 0), pipeline_mode=pl.Buffered(1))
    total = jax.ShapeDtypeStruct((1, d), F32)
    return pl.pallas_call(
        turn_kernel,
        grid=(rows // tile,),
        in_specs=[pl.BlockSpec(memory_space=pltpu.SMEM), by_rows, by_rows, whole(table.shape)]
        + [pl.BlockSpec((tile, units), lambda i: (i, 0))] * 4
        + [kept] * 4,
        out_specs=[by_rows] * 2 + [whole((1, d))] * 3,
        out_shape=[
            jax.ShapeDtypeStruct((rows, d), F32),
            jax.ShapeDtypeStruct((rows, d), BF),
            total,
            total,
            total,
        ],
        compiler_params=params("turn"),
        cost_estimate=cost(2 * 4 * rows * d * units, 20e6),
        name="turn",
    )(place, middle, cot, table, *pre, *ups)


def output_kernel(_, mid_ref, table_ref, *refs):
    hidden, downs, out_ref = refs[0:4], refs[4:8], refs[-1]
    mlp = table_ref[BIAS_DOWN]
    for h, w in zip(hidden, downs):
        mlp = mlp + dot_nt(h[...], w[...])
    out_ref[...] = (mid_ref[...] + mlp).astype(BF)


def output_call(place, middle, table, hidden, downs):
    rows, d = middle.shape
    units = downs[0].shape[1]
    tile = 256
    by_rows = pl.BlockSpec((tile, d), lambda i: (i, 0))
    kept = pl.BlockSpec((d, units), lambda i: (0, 0), pipeline_mode=pl.Buffered(1))
    return pl.pallas_call(
        output_kernel,
        grid=(rows // tile,),
        in_specs=[pl.BlockSpec(memory_space=pltpu.SMEM), by_rows, whole(table.shape)]
        + [pl.BlockSpec((tile, units), lambda i: (i, 0))] * 4
        + [kept] * 4,
        out_specs=by_rows,
        out_shape=jax.ShapeDtypeStruct((rows, d), BF),
        compiler_params=params("output"),
        cost_estimate=cost(2 * 4 * rows * d * units, 16e6),
        name="output",
    )(place, middle, table, *hidden, *downs)


def attend_back_kernel(count, has_got, place_ref, lse_ref, grows_hbm, w_hbm, proj_hbm, n1_hbm, mixed_hbm, *refs):
    got_hbm = refs[0] if has_got else None
    gproj_hbm, sum_ref, *grad_refs = refs[has_got : has_got + 3 + has_got]
    grows, w, projs, n1, mixed, got, gproj_all, sems, out_sems = refs[has_got + 3 + has_got :]
    seqs = lse_ref.shape[0]

    def of_seq(seq):
        return pl.ds(pl.multiple_of(seq * SEQ_LEN, SEQ_LEN), SEQ_LEN)

    def seq_copies(seq):
        return [
            pltpu.make_async_copy(hbm.at[of_seq(seq)], ref.at[of_seq(seq)], sems.at[i, seq])
            for i, (hbm, ref) in enumerate(((grows_hbm, grows), (proj_hbm, projs)))
        ]

    def out_copy(seq):
        return pltpu.make_async_copy(gproj_all.at[of_seq(seq)], gproj_hbm.at[of_seq(seq)], out_sems.at[seq])

    w_copy = pltpu.make_async_copy(w_hbm.at[:, 512:768], w, sems.at[2, 0])
    late = [
        pltpu.make_async_copy(n1_hbm, n1, sems.at[3, 0]),
        pltpu.make_async_copy(mixed_hbm, mixed, sems.at[4, 0]),
    ]
    if has_got:
        late.append(pltpu.make_async_copy(got_hbm, got, sems.at[5, 0]))
    w_copy.start()
    for seq in range(seqs):
        for copy in seq_copies(seq):
            copy.start()
    for copy in late:
        copy.start()
    w_copy.wait()

    @pl.loop(0, seqs)
    def _(seq):
        for copy in seq_copies(seq):
            copy.wait()
        projected = projs[of_seq(seq)]
        grad_mixed = dot(grows[of_seq(seq)], w[...]).astype(BF)
        out = gproj_all.at[of_seq(seq)]
        parts = {}
        early = lax.broadcasted_iota(jnp.int32, (HALF, HALF), 0) <= lax.broadcasted_iota(jnp.int32, (HALF, HALF), 1)
        jobs = []
        for head, (qt, kt, vt, qk_lane, v_lane) in enumerate(HEAD_PLACES):
            mt = 0 if head == 2 else 1
            query = lane_keep(projected[:, qt * 128 : qt * 128 + 128], qk_lane) * BF(0.125)
            keys = projected[:, kt * 128 : kt * 128 + 128]
            values = projected[:, vt * 128 : vt * 128 + 128]
            grads = lane_keep(grad_mixed[:, mt * 128 : mt * 128 + 128], v_lane)
            parts["k", head] = [None, None]
            parts["v", head] = [None, None]
            for block in range(2):
                rows = slice(block * HALF, block * HALF + HALF)
                jobs.append((head, block, qk_lane, query[rows], keys, values, grads[rows]))

        def first_stage(job):
            head, block, _, qb, keys, values, gb = job
            last = block * HALF + HALF
            return dot_nt(keys[0:last], qb), dot_nt(values[0:last], gb)

        def last_stage(job, scores, gprobs):
            head, block, qk_lane, qb, keys, values, gb = job
            last = block * HALF + HALF
            lse = lse_ref[seq, head : head + 1, last - HALF : last]
            probs = jnp.exp(scores - lse)
            corner = jnp.where(early, probs[last - HALF :], 0.0)
            probs = jnp.concatenate([probs[: last - HALF], corner], axis=0) if block else corner
            both = probs * gprobs
            delta = jnp.sum(both, axis=0, keepdims=True)
            gscores = (both - probs * delta).astype(BF)
            gq = dot_tn(keys[0:last], gscores) * 0.125
            parts["q", head, block] = gq[qk_lane : qk_lane + HEAD_DIM]
            gk = dot(gscores, qb)
            gv = dot(probs.astype(BF), gb)
            for name, got in (("k", gk), ("v", gv)):
                held = parts[name, head]
                for b in range(block + 1):
                    part = got[b * HALF : b * HALF + HALF]
                    held[b] = part if held[b] is None else held[b] + part

        waiting = None
        for job in jobs + [None]:
            ahead = None if job is None else (job, *first_stage(job))
            if waiting is not None:
                last_stage(*waiting)
            waiting = ahead
        for block in range(2):
            rows = slice(block * HALF, block * HALF + HALF)
            pair = jnp.concatenate([parts["q", 0, block], parts["q", 1, block]], axis=0).T
            lone = parts["q", 2, block]
            lone = jnp.concatenate([lone, jnp.zeros_like(lone)], axis=0).T
            out[rows, 0:128] = pair.astype(BF)
            out[rows, 128:256] = (parts["k", 0][block] + parts["k", 1][block]).astype(BF)
            out[rows, 256:384] = (parts["v", 0][block] + parts["v", 1][block]).astype(BF)
            out[rows, 384:512] = (lone + parts["v", 2][block]).astype(BF)
            out[rows, 512:640] = parts["k", 2][block].astype(BF)
        out_copy(seq).start()

    gproj = gproj_all[...]
    sum_ref[...] = jnp.sum(gproj.astype(F32), axis=0, keepdims=True)
    for copy in late:
        copy.wait()
    grad_a = dot_tn(n1[...], gproj)
    grad_b = dot_tn(grows[...], mixed[...])
    grad = jnp.concatenate(
        [grad_a[:, 0:512], grad_a[:, 512:640] + grad_b[:, 0:128], grad_b[:, 128:256]], axis=1
    )
    if has_got:
        store_split(*grad_refs, got, (), place_ref, grad, count)
    else:
        store_all(*grad_refs, (), place_ref, grad, count)
    for seq in range(seqs):
        out_copy(seq).wait()


def attend_back_call(place, count, grows, n1, w, proj, mixed, lse, got=None):
    rows, d = grows.shape
    seqs = rows // SEQ_LEN
    shard = d // (2 * count)
    gots = () if got is None else (got,)
    both = (2 * count, shard, 768)
    grads = [both] if got is None else [(count, shard, 768)] * 2
    hbm = pl.BlockSpec(memory_space=pl.ANY)
    return pl.pallas_call(
        functools.partial(attend_back_kernel, count, len(gots)),
        grid=(1,),
        in_specs=[pl.BlockSpec(memory_space=pltpu.SMEM), whole(lse.shape)] + [hbm] * (5 + len(gots)),
        out_specs=[hbm, whole((1, 640))] + [whole(g) for g in grads],
        out_shape=[jax.ShapeDtypeStruct((rows, 640), BF), jax.ShapeDtypeStruct((1, 640), F32)]
        + [jax.ShapeDtypeStruct(g, BF) for g in grads],
        scratch_shapes=[
            pltpu.VMEM((rows, d), BF),
            pltpu.VMEM((d, 256), BF),
            pltpu.VMEM((rows, 640), BF),
            pltpu.VMEM((rows, d), BF),
            pltpu.VMEM((rows, 256), BF),
            pltpu.VMEM(both if got is not None else (8, 16, 128), BF),
            pltpu.VMEM((rows, 640), BF),
            pltpu.SemaphoreType.DMA((6, seqs)),
            pltpu.SemaphoreType.DMA((seqs,)),
        ],
        compiler_params=params("attend_back"),
        cost_estimate=cost(10e9, 12e6),
        name="attend_back",
    )(place, lse, grows, w, proj, n1, mixed, *gots)


def finish_kernel(_, x_ref, gmid_ref, table_ref, *refs):
    gproj, weights, known, sum_proj, sum_up = refs[0:4], refs[4:8], refs[8:12], refs[12:16], refs[16:20]
    out_ref, keep_ref, away_ref, gain_sum, shift_sum = refs[20:]
    start_sums(gain_sum, shift_sum)
    grad = None
    for g, w in zip(gproj, weights):
        term = dot_nt(g[...], w[...])
        grad = term if grad is None else grad + term
    unit, spread = unit_rows(x_ref[...].astype(F32))
    add_sum(gain_sum, grad * unit)
    add_sum(shift_sum, grad)
    back = norm_back(grad, unit, spread, table_ref[GAIN_ATTN])
    out_ref[...] = (gmid_ref[...] + back).astype(BF)

    @pl.when(pl.program_id(0) == pl.num_programs(0) - 1)
    def _():
        shared = jnp.concatenate(
            [r[...] for r in known] + [gain_sum[...], shift_sum[...]], axis=1
        )
        for dy in range(2):
            for dc, ref in enumerate((keep_ref, away_ref)):
                row = jnp.concatenate([shared, sum_proj[2 * dy + dc][...], sum_up[2 * dy + dc][...]], axis=1)
                ref[dy : dy + 1] = row


def finish_call(place, x, gmid, table, gproj, weights, known, sum_proj, sum_up):
    rows, d = x.shape
    tile = 256
    by_rows = pl.BlockSpec((tile, d), lambda i: (i, 0))
    width = 6 * d + sum_proj[0].shape[1] + sum_up[0].shape[1]
    return pl.pallas_call(
        finish_kernel,
        grid=(rows // tile,),
        in_specs=[pl.BlockSpec(memory_space=pltpu.SMEM), by_rows, by_rows, whole(table.shape)]
        + [pl.BlockSpec((tile, 640), lambda i: (i, 0))] * 4
        + [pl.BlockSpec((d, 640), lambda i: (0, 0))] * 4
        + [whole(v.shape) for v in (*known, *sum_proj, *sum_up)],
        out_specs=[by_rows, whole((2, width)), whole((2, width))],
        out_shape=[jax.ShapeDtypeStruct((rows, d), BF)] + [jax.ShapeDtypeStruct((2, width), F32)] * 2,
        scratch_shapes=[pltpu.VMEM((1, d), F32)] * 2,
        compiler_params=params("finish"),
        cost_estimate=cost(2 * 4 * rows * d * 640, 16e6),
        name="finish",
    )(place, x, gmid, table, *gproj, *weights, *known, *sum_proj, *sum_up)


class Links:
    def __init__(self, mesh):
        self.count = mesh.shape["fsdp"] // 2
        places = [
            (z, x, y, c)
            for z in range(self.count)
            for x in range(2)
            for y in range(2)
            for c in range(2)
        ]

        def index(z, x, y, c):
            return ((z * 2 + x) * 2 + y) * 2 + c

        def pairs(move):
            return [(index(*p), index(*move(*p))) for p in places]

        self.core = pairs(lambda z, x, y, c: (z, x, y, 1 - c))
        self.y = pairs(lambda z, x, y, c: (z, x, 1 - y, c))
        self.x = pairs(lambda z, x, y, c: (z, 1 - x, y, c))
        self.ring = pairs(lambda z, x, y, c: ((z + 1) % self.count, x, y, c))
        self.far = [
            pairs(lambda z, x, y, c, k=k: ((z + k) % self.count, x, y, c)) for k in range(self.count)
        ]
        self.back = [
            pairs(lambda z, x, y, c, k=k: ((z - k) % self.count, x, y, c)) for k in range(self.count)
        ]
        self.xy = pairs(lambda z, x, y, c: (z, 1 - x, 1 - y, c))
        self.trees = []
        step = 1
        while step < self.count:
            size = 4 if step * 4 <= self.count else 2
            self.trees.append(
                [pairs(lambda z, x, y, c, b=step * k: (z ^ b, x, y, c)) for k in range(1, size)]
            )
            step *= size

    @staticmethod
    def send(value, pairs):
        return lax.ppermute(value, AXES, pairs)


def plus(*terms, kind=BF):
    total = terms[0].astype(F32)
    for term in terms[1:]:
        total = total + term.astype(F32)
    return total.astype(kind)


def tie(value, *others):
    return lax.optimization_barrier((value, others))[0]


def ring_from(links, first):
    held = [first]
    for _ in range(links.count - 1):
        held.append(links.send(held[-1], links.ring))
    return held


def gather_and_attend(links, place, attn, up, down, n1, smalls, layer_input, table):
    n = links.count
    half = n // 2
    small_y = links.send(smalls, links.y)

    near = [jnp.stack([attn, down])]
    done = (n1,)
    for k in range(1, n):
        now = near[-1] if k == 1 else tie(near[-1], *done)
        if k == 3:
            joint = links.send(jnp.concatenate([now, steps[0].reshape((4,) + up.shape)]), links.ring)
            near.append(joint[:2])
            steps.append(joint[2:].reshape(steps[0].shape))
        else:
            near.append(links.send(now, links.ring))
        done = (near[-1],)
        if k == 1:
            pair = jnp.stack([up, links.send(up, links.x)])
            done += (pair, n1, smalls)
        if k == 2:
            steps = [jnp.stack([pair, links.send(tie(pair, near[1]), links.y)])]
            done += (steps[0], small_y)
        if k == half:
            lines = [jnp.stack([v[0] for v in near[:half]])]
            others = [links.send(lines[0], links.x)]
            done += (others[0],)
        if k == half + 1:
            quads = [links.send(tie(jnp.stack([lines[0], others[0]]), *near[half:-1]), links.y)]
            smalls = [smalls, links.send(smalls, links.core), small_y, links.send(small_y, links.core)]
            done += (smalls[1], smalls[3], quads[0])

    lines.append(tie(jnp.stack([v[0] for v in near[half:]]), *done))
    others.append(links.send(lines[1], links.x))
    line = jnp.stack([v[1] for v in near])
    beyond = [links.send(tie(line, *done), links.y)]
    steps.append(links.send(tie(steps[-1], *done), links.ring))
    core = lambda values: [links.send(v, links.core) for v in values]

    def from_lines(*pair):
        return [(v[k // half], (k % half,)) for v in pair for k in range(n)]

    def from_quads(quads):
        return [(quads[k // half], (dx, k % half)) for dx in range(2) for k in range(n)]

    quads.append(links.send(jnp.stack([lines[1], others[1]]), links.y))
    far = links.send(tie(line, others[1]), links.x)

    attn_w, proj, mixed, lse = [], [], [], []

    def attend(pieces, *before):
        j = len(proj)
        w, p, m, s = attend_call(tie(place, *before) if before else place, n1, pieces, smalls[j])
        attn_w.append(w)
        proj.append(p)
        mixed.append(m)
        lse.append(s)

    attend(from_lines(lines, others))
    attend(from_lines(core(lines), core(others)), mixed[0])
    quads_core = core([quads[0], tie(quads[1], mixed[1])])
    beyond.append(links.send(tie(beyond[0], far), links.x))
    for _ in range(3, n):
        steps.append(links.send(tie(steps[-1], mixed[1]), links.ring))
    attend(from_quads(quads), mixed[1], quads[1], far, steps[2])
    attend(from_quads(quads_core), mixed[2])
    middle, n2 = middle_call(layer_input, table, mixed, attn_w)

    steps[-1] = tie(steps[-1], mixed[3])
    up_core = core(steps)
    up_w = [[(v, (dy, dx)) for dx in range(2) for v in vs] for dy in range(2) for vs in (steps, up_core)]
    down_w = [
        [(v, (k,)) for v in vs for k in range(n)]
        for pair in ((line, far), beyond)
        for vs in (pair, core(pair))
    ]
    return attn_w, up_w, down_w, proj, mixed, lse, smalls, middle, n2


def spread_sum(links, home):
    got = [links.send(home[k], links.far[k]) for k in range(1, links.count)]
    return plus(home[0], *got, kind=F32)


def sum_near(links, keep, away):
    rows = keep + links.send(away, links.core)
    near, far = rows[0:1], rows[1:2]
    return (near + links.send(near, links.x)) + (
        links.send(far, links.y) + links.send(far, links.xy)
    )


def sum_far(links, total):
    for pairs in links.trees:
        got = [total] + [links.send(total, p) for p in pairs]
        while len(got) > 1:
            got = [got[i] + got[i + 1] for i in range(0, len(got), 2)]
        total = got[0]
    return total


def pack_attn(w_qkv, w_out):
    q, k, v, o = w_qkv[:, 0], w_qkv[:, 1], w_qkv[:, 2], w_out.T
    return jnp.concatenate(
        [q[:, :128], k[:, :128], v[:, :128], q[:, 128:], v[:, 128:], k[:, 128:], o[:, 128:], o[:, :128]],
        axis=1,
    )


def unpack_attn(g):
    q = jnp.concatenate([g[:, 0:128], g[:, 384:448]], axis=1)
    k = jnp.concatenate([g[:, 128:256], g[:, 512:576]], axis=1)
    v = jnp.concatenate([g[:, 256:384], g[:, 448:512]], axis=1)
    o = jnp.concatenate([g[:, 640:768], g[:, 576:640]], axis=1)
    return jnp.stack([q, k, v], axis=1), o.T


def body(
    links,
    layer_input,
    w_qkv,
    bias_qv,
    w_out,
    bias_out,
    gain_attn,
    shift_attn,
    gain_mlp,
    shift_mlp,
    w_up,
    bias_up,
    w_down,
    bias_down,
    cotangent,
):
    fsdp = lax.axis_index("fsdp")
    place = jnp.stack([fsdp // 2, fsdp % 2]).astype(jnp.int32)
    count = links.count
    n1, sum_down, small, table = start_call(
        layer_input,
        cotangent,
        bias_qv,
        bias_up,
        (bias_out, gain_attn, shift_attn, gain_mlp, shift_mlp, bias_down),
    )
    attn_w, up_w, down_w, proj, mixed, lse, smalls, middle, n2 = gather_and_attend(
        links, place, pack_attn(w_qkv, w_out), w_up, w_down.T, n1, small, layer_input, table
    )

    hidden, pre, sum_up = [None] * 4, [None] * 4, [None] * 4
    up_home, up_away, down_sum = [None] * 2, [None] * 2, [None] * 2
    gots = [None] * 4
    for j in (1, 3, 0, 2):
        out = feed_call(
            place, count, n2, cotangent, up_w[j], down_w[j], smalls[j], gots[j]
        )
        hidden[j], pre[j], sum_up[j], up_w[j], down_w[j] = out[0:5]
        if j % 2:
            gots[j - 1] = links.send(out[5], links.core)
        else:
            up_home[j // 2], up_away[j // 2], down_sum[j // 2] = out[5:8]

    got_x0 = links.send(up_away[0], links.x)
    got_x1 = links.send(up_away[1], links.x)
    got_down = links.send(down_sum[1], links.y)
    gmid, grows, gain_two, shift_two, sum_out = turn_call(
        place, middle, cotangent, table, pre, up_w
    )

    gproj, sum_proj = [None] * 4, [None] * 4
    attn_home, attn_away = [None] * 2, [None] * 2

    def back(j, got, *before):
        out = attend_back_call(
            tie(place, *before) if before else place,
            count,
            grows,
            n1,
            attn_w[j],
            proj[j],
            mixed[j],
            lse[j],
            got,
        )
        gproj[j], sum_proj[j] = out[0:2]
        if j % 2:
            return links.send(out[2], links.core)
        attn_home[j // 2], attn_away[j // 2] = out[2:4]

    got_three = back(3, None, got_x0)
    up_beyond = plus(up_home[1], got_x1)
    got_up = links.send(up_beyond, links.y)
    got_one = back(1, None, up_beyond)
    down_away = plus(down_sum[0][count:], got_down[count:])
    got_x = links.send(down_away, links.x)
    back(2, got_three, down_away)
    got_a1 = links.send(attn_away[1], links.x)
    up_all = plus(up_home[0], got_x0, got_up)
    down_all = plus(down_sum[0][:count], got_down[:count], got_x)
    back(0, got_one, up_all, down_all, sum_proj[2])
    grad_up = spread_sum(links, up_all)
    grad_down = spread_sum(links, down_all)
    got_a0 = links.send(attn_away[0], links.x)
    attn_beyond = plus(attn_home[1], got_a1)
    got_attn = links.send(attn_beyond, links.y)
    grad_input, keep, away = finish_call(
        tie(place, attn_beyond, grad_up),
        layer_input,
        gmid,
        table,
        gproj,
        attn_w,
        (sum_out, sum_down, gain_two, shift_two),
        sum_proj,
        sum_up,
    )
    attn_all = plus(tie(attn_home[0], keep), got_a0, got_attn)
    parts = [attn_all[0]] + [links.send(attn_all[k], links.far[k]) for k in range(1, count)]
    total = sum_near(links, keep, tie(away, attn_all))
    before = (total, attn_all, grad_up, grad_down)
    layer_output = output_call(tie(place, *before), middle, table, hidden, down_w)
    sums = sum_far(links, tie(total, layer_output, *parts))
    grad_attn = plus(*parts, kind=F32)

    d = layer_input.shape[1]
    heads = bias_qv.shape[1]
    vec = sums[0]
    total_out, total_down, gain_two, shift_two, gain_one, shift_one = (
        vec[i * d : (i + 1) * d] for i in range(6)
    )
    own = vec[6 * d :]
    total_qv = jnp.stack(
        [
            jnp.concatenate([own[0:128], own[384:448]]),
            jnp.concatenate([own[256:384], own[448:512]]),
        ]
    )
    total_up = own[640:]

    shard_qkv, shard_out = unpack_attn(grad_attn)
    return (
        layer_output,
        grad_input,
        shard_qkv,
        total_qv,
        shard_out,
        total_out,
        gain_one,
        shift_one,
        gain_two,
        shift_two,
        grad_up,
        total_up,
        grad_down.T,
        total_down,
    )


def solution(mesh):
    tokens = P(("fsdp", "tp"), None)
    placed = (
        tokens,
        P("fsdp", None, "tp"),
        P(None, "tp"),
        P("tp", "fsdp"),
        P(),
        P(),
        P(),
        P(),
        P(),
        P("fsdp", "tp"),
        P("tp"),
        P("tp", "fsdp"),
        P(),
        tokens,
    )
    return jax.shard_map(
        functools.partial(body, Links(mesh)),
        mesh=mesh,
        in_specs=placed,
        out_specs=(
            tokens,
            tokens,
            P("fsdp", None, "tp"),
            P(None, "tp"),
            P("tp", "fsdp"),
            P(),
            P(),
            P(),
            P(),
            P(),
            P("fsdp", "tp"),
            P("tp"),
            P("tp", "fsdp"),
            P(),
        ),
        check_vma=False,
    )
```

```python
import functools

import jax
import jax.numpy as jnp
from jax import lax
from jax.experimental import pallas as pl
from jax.experimental.pallas import tpu as pltpu
from jax.sharding import PartitionSpec as P

HEAD_DIM = 64
SEQ_LEN = 512
HALF = 256
EPS = 1e-05
AXES = ("fsdp", "tp")
BF = jnp.bfloat16
F32 = jnp.float32
MB = 1 << 20
SHARE = 0.3
BIAS_OUT, GAIN_ATTN, SHIFT_ATTN, GAIN_MLP, SHIFT_MLP, BIAS_DOWN = (slice(i, i + 1) for i in range(6))
VMEM_MB = {"start": 60, "feed": 60, "attend_back": 60, "turn": 60, "finish": 60, "output": 60}
SMALL_ATTN = 768


def dot(left, right):
    return lax.dot_general(left, right, (((1,), (0,)), ((), ())), preferred_element_type=F32)


def dot_nt(left, right):
    return lax.dot_general(left, right, (((1,), (1,)), ((), ())), preferred_element_type=F32)


def dot_tn(left, right):
    return lax.dot_general(left, right, (((0,), (0,)), ((), ())), preferred_element_type=F32)


def whole(shape):
    zeros = (0,) * len(shape)
    return pl.BlockSpec(shape, lambda *_: zeros)


def params(kernel):
    return pltpu.CompilerParams(vmem_limit_bytes=VMEM_MB.get(kernel, 36) * MB)


def cost(flops, nbytes, trans=0):
    return pl.CostEstimate(
        flops=int(flops * SHARE), bytes_accessed=int(nbytes * SHARE), transcendentals=int(trans * SHARE)
    )


def unit_rows(rows):
    centre = rows - jnp.mean(rows, axis=-1, keepdims=True)
    spread = lax.rsqrt(jnp.mean(centre * centre, axis=-1, keepdims=True) + EPS)
    return centre * spread, spread


def norm_back(grad_out, unit, spread, gain):
    scaled = grad_out * gain
    inner = jnp.mean(scaled * unit, axis=-1, keepdims=True)
    return spread * (scaled - jnp.mean(scaled, axis=-1, keepdims=True) - unit * inner)


def start_sums(*refs):
    @pl.when(pl.program_id(0) == 0)
    def _():
        for ref in refs:
            ref[...] = jnp.zeros_like(ref)


def add_sum(ref, value):
    ref[...] += jnp.sum(value, axis=0, keepdims=True)


def start_kernel(x_ref, cot_ref, qv_ref, up_ref, *refs):
    vectors, (n1_ref, sum_ref, small_ref, table_ref) = refs[:6], refs[6:]
    start_sums(sum_ref)

    @pl.when(pl.program_id(0) == 0)
    def _():
        for i, ref in enumerate(vectors):
            table_ref[i : i + 1] = ref[...].astype(F32).reshape(1, -1)
        small_ref[...] = jnp.zeros_like(small_ref)
        for c in range(2):
            pair, lone = (0, 384) if c == 0 else (256, 448)
            row = qv_ref[c : c + 1].astype(F32)
            small_ref[:, pair : pair + 128] = row[:, 0:128]
            small_ref[:, lone : lone + HEAD_DIM] = row[:, 128:192]
        small_ref[:, SMALL_ATTN:] = up_ref[...].astype(F32).reshape(1, -1)

    unit, _ = unit_rows(x_ref[...].astype(F32))
    normed = unit * table_ref[GAIN_ATTN] + table_ref[SHIFT_ATTN]
    n1_ref[...] = normed.astype(BF)
    add_sum(sum_ref, cot_ref[...].astype(F32))


def start_call(x, cot, bias_qv, bias_up, vectors):
    rows, d = x.shape
    units = bias_up.shape[0]
    tile = 256
    by_rows = pl.BlockSpec((tile, d), lambda i: (i, 0))
    return pl.pallas_call(
        start_kernel,
        grid=(rows // tile,),
        in_specs=[by_rows, by_rows, whole(bias_qv.shape), whole(bias_up.shape)]
        + [whole(v.shape) for v in vectors],
        out_specs=[by_rows]
        + [whole((1, d)), whole((1, SMALL_ATTN + units)), whole((8, d))],
        out_shape=[
            jax.ShapeDtypeStruct((rows, d), BF),
            jax.ShapeDtypeStruct((1, d), F32),
            jax.ShapeDtypeStruct((1, SMALL_ATTN + units), F32),
            jax.ShapeDtypeStruct((8, d), F32),
        ],
        compiler_params=params("start"),
        cost_estimate=cost(0, 10 * rows * d),
        name="start",
    )(x, cot, bias_qv, bias_up, *vectors)


def piece_specs(pieces, cols, index):
    rows = pieces[0][0].shape[-2]
    return [
        pl.BlockSpec((1,) * len(lead) + (rows, cols), lambda i, lead=lead: lead + (0, index(i)))
        for _, lead in pieces
    ]


def place_pieces(place_ref, pieces, out_ref):
    count = len(pieces) // 2
    z, x = place_ref[0], place_ref[1]
    for k in range(count):
        for dx in range(2):
            piece = pieces[dx * count + k]
            size, cols = piece.shape[-2:]
            slot = lax.rem(z - k + count, count) * 2 + lax.rem(x + dx, 2)
            out_ref[pl.ds(pl.multiple_of(slot * size, size), size)] = piece[...].reshape(size, cols)


HEAD_PLACES = ((0, 1, 2, 0, 0), (0, 1, 2, 64, 64), (3, 4, 3, 0, 64))


def lane_keep(tile, first):
    lanes = lax.broadcasted_iota(jnp.int32, tile.shape, 1)
    keep = (lanes >= first) & (lanes < first + HEAD_DIM)
    return jnp.where(keep, tile, jnp.zeros_like(tile))


def attend_kernel(place_ref, n1_ref, bias_ref, *refs):
    pieces, (w_ref, proj_ref, mixed_ref, lse_ref) = refs[:-4], refs[-4:]

    @pl.when(pl.program_id(0) == 0)
    def _():
        place_pieces(place_ref, pieces, w_ref)

    projected = (dot(n1_ref[...], w_ref[:, 0:640]) + bias_ref[...].astype(F32)).astype(BF)
    proj_ref[...] = projected
    lse_ref[...] = jnp.zeros_like(lse_ref)
    outs = {}
    early = lax.broadcasted_iota(jnp.int32, (HALF, HALF), 0) <= lax.broadcasted_iota(jnp.int32, (HALF, HALF), 1)
    jobs = []
    for head, (qt, kt, vt, qk_lane, v_lane) in enumerate(HEAD_PLACES):
        query = lane_keep(projected[:, qt * 128 : qt * 128 + 128], qk_lane) * BF(0.125)
        keys = projected[:, kt * 128 : kt * 128 + 128]
        values = projected[:, vt * 128 : vt * 128 + 128]
        for block in range(2):
            first, last = block * HALF, block * HALF + HALF
            jobs.append((head, first, last, query[first:last], keys[0:last], values[0:last], v_lane))

    def last_stage(job, scores):
        head, first, last, _, _, values, v_lane = job
        corner = jnp.where(early, scores[first:], -1e30)
        scores = jnp.concatenate([scores[:first], corner], axis=0) if first else corner
        top = jnp.max(scores, axis=0, keepdims=True)
        weight = jnp.exp(scores - top)
        total = jnp.sum(weight, axis=0, keepdims=True)
        mixed = dot_tn(values, weight.astype(BF)) * (1.0 / total)
        outs[head, first // HALF] = mixed[v_lane : v_lane + HEAD_DIM]
        lse_ref[0, head : head + 1, first:last] = top + jnp.log(total)

    waiting = None
    for job in jobs + [None]:
        ahead = None if job is None else (job, dot_nt(job[4], job[3]))
        if waiting is not None:
            last_stage(*waiting)
        waiting = ahead
    for block in range(2):
        first = block * HALF
        rows = slice(first, first + HALF)
        single = jnp.concatenate([jnp.zeros_like(outs[2, block]), outs[2, block]], axis=0)
        pair = jnp.concatenate([outs[0, block], outs[1, block]], axis=0)
        mixed_ref[rows, 0:128] = single.T.astype(BF)
        mixed_ref[rows, 128:256] = pair.T.astype(BF)


def attend_call(place, n1, pieces, bias):
    rows, d = n1.shape
    seqs = rows // SEQ_LEN
    return pl.pallas_call(
        attend_kernel,
        grid=(seqs,),
        in_specs=[
            pl.BlockSpec(memory_space=pltpu.SMEM),
            pl.BlockSpec((SEQ_LEN, d), lambda i: (i, 0)),
            pl.BlockSpec((1, 640), lambda i: (0, 0)),
        ]
        + piece_specs(pieces, 768, lambda i: 0),
        out_specs=[
            whole((d, 768)),
            pl.BlockSpec((SEQ_LEN, 640), lambda i: (i, 0)),
            pl.BlockSpec((SEQ_LEN, 256), lambda i: (i, 0)),
            pl.BlockSpec((1, 8, SEQ_LEN), lambda i: (i, 0, 0)),
        ],
        out_shape=[
            jax.ShapeDtypeStruct((d, 768), BF),
            pltpu.HBM((rows, 640), BF),
            jax.ShapeDtypeStruct((rows, 256), BF),
            pltpu.HBM((seqs, 8, SEQ_LEN), F32),
        ],
        compiler_params=params("attend"),
        cost_estimate=cost(6e9, 8e6),
        name="attend",
    )(place, n1, bias, *[array for array, _ in pieces])


def middle_kernel(x_ref, table_ref, *refs):
    mixed, weights, (mid_ref, n2_ref) = refs[0:4], refs[4:8], refs[8:]
    attended = table_ref[BIAS_OUT]
    for m, w in zip(mixed, weights):
        attended = attended + dot_nt(m[...], w[...])
    middle = x_ref[...].astype(F32) + attended
    mid_ref[...] = middle
    unit, _ = unit_rows(middle)
    normed = unit * table_ref[GAIN_MLP] + table_ref[SHIFT_MLP]
    n2_ref[...] = normed.astype(BF)


def middle_call(x, table, mixed, weights):
    rows, d = x.shape
    tile = 256
    by_rows = pl.BlockSpec((tile, d), lambda i: (i, 0))
    return pl.pallas_call(
        middle_kernel,
        grid=(rows // tile,),
        in_specs=[by_rows, whole(table.shape)]
        + [pl.BlockSpec((tile, 256), lambda i: (i, 0))] * 4
        + [pl.BlockSpec((d, 256), lambda i: (0, 2))] * 4,
        out_specs=[by_rows, by_rows],
        out_shape=[pltpu.HBM((rows, d), F32), pltpu.HBM((rows, d), BF)],
        compiler_params=params("middle"),
        cost_estimate=cost(2 * rows * d * 1024, 16e6),
        name="middle",
    )(x, table, *mixed, *weights)


def gelu_both(value):
    cumulative = 0.5 + 0.5 * lax.erf(value * 2.0**-0.5)
    bell = jnp.exp(-0.5 * value * value)
    return value * cumulative, cumulative + value * bell * (2.0 * 3.141592653589793) ** -0.5


def store_all(ref, lead, place_ref, value, count, got_ref=None, got_lead=()):
    z, x = place_ref[0], place_ref[1]
    size = value.shape[0] // (2 * count)
    for block in range(2 * count):
        slot = lax.rem(x + block % 2, 2) * count + lax.rem(block // 2 - z + count, count)
        part = value[block * size : (block + 1) * size]
        if got_ref is not None:
            part = part + got_ref[got_lead + (slot,)].astype(F32)
        ref[lead + (slot,)] = part.astype(BF)


def store_split(home_ref, away_ref, got_ref, lead, place_ref, value, count):
    z, x = place_ref[0], place_ref[1]
    size = value.shape[0] // (2 * count)
    for pair in range(count):
        slot = lax.rem(pair - z + count, count)
        first = value[2 * pair * size : (2 * pair + 1) * size]
        second = value[(2 * pair + 1) * size : (2 * pair + 2) * size]
        home = jnp.where(x == 0, first, second) + got_ref[lead + (slot,)].astype(F32)
        away = jnp.where(x == 0, second, first) + got_ref[lead + (count + slot,)].astype(F32)
        home_ref[slot] = home.astype(BF)
        away_ref[slot] = away.astype(BF)


def feed_kernel(count, tokens, has_got, place_ref, n2_ref, cot_ref, bias_ref, *refs):
    ups, downs, refs = refs[: 2 * count], refs[2 * count : 4 * count], refs[4 * count :]
    got_ref = refs[0] if has_got else None
    hidden_ref, pre_ref, sum_ref, up_ref, down_ref, *outs = refs[has_got:]
    place_pieces(place_ref, ups, up_ref)
    place_pieces(place_ref, downs, down_ref)
    rows = n2_ref.shape[0]
    up, down, bias = up_ref[...], down_ref[...], bias_ref[...].astype(F32)
    total = jnp.zeros_like(bias)
    for first in range(0, rows, tokens):
        here = slice(first, first + tokens)
        pre = dot(n2_ref[here], up) + bias
        grad_hidden = dot(cot_ref[here], down)
        hidden, slope = gelu_both(pre)
        hidden_ref[here] = hidden.astype(BF)
        grad_pre = (grad_hidden * slope).astype(BF)
        pre_ref[here] = grad_pre
        total = total + jnp.sum(grad_pre.astype(F32), axis=0, keepdims=True)
    sum_ref[...] = total
    grads = (dot_tn(n2_ref[...], pre_ref[...]), dot_tn(cot_ref[...], hidden_ref[...]))
    if has_got:
        store_split(outs[0], outs[1], got_ref, (0,), place_ref, grads[0], count)
        store_all(outs[2], (), place_ref, grads[1], count, got_ref, (1,))
    else:
        store_all(outs[0], (0,), place_ref, grads[0], count)
        store_all(outs[0], (1,), place_ref, grads[1], count)


def feed_call(place, count, n2, cot, ups, downs, small, got=None):
    rows, d = n2.shape
    units = ups[0][0].shape[-1]
    tile = 256
    shard = d // (2 * count)
    cols = lambda n: pl.BlockSpec((n, tile), lambda i: (0, i))
    hid = jax.ShapeDtypeStruct((rows, units), BF)
    both_spec = pl.BlockSpec((2, 2 * count, shard, tile), lambda i: (0, 0, 0, i))
    if got is None:
        grad_specs = [both_spec]
        grads = [jax.ShapeDtypeStruct((2, 2 * count, shard, units), BF)]
    else:
        grad_specs = [pl.BlockSpec((n, shard, tile), lambda i: (0, 0, i)) for n in (count, count, 2 * count)]
        grads = [jax.ShapeDtypeStruct((n, shard, units), BF) for n in (count, count, 2 * count)]
    gots = () if got is None else (got,)
    return pl.pallas_call(
        functools.partial(feed_kernel, count, 512, len(gots)),
        grid=(units // tile,),
        in_specs=[
            pl.BlockSpec(memory_space=pltpu.SMEM),
            whole((rows, d)),
            whole((rows, d)),
            pl.BlockSpec((1, tile), lambda i: (0, SMALL_ATTN // tile + i)),
        ]
        + piece_specs(ups, tile, lambda i: i)
        + piece_specs(downs, tile, lambda i: i)
        + [both_spec] * len(gots),
        out_specs=[cols(rows)] * 2 + [cols(1)] + [cols(d)] * 2 + grad_specs,
        out_shape=[hid] * 2
        + [jax.ShapeDtypeStruct((1, units), F32)]
        + [jax.ShapeDtypeStruct((d, units), BF)] * 2
        + grads,
        compiler_params=params("feed"),
        cost_estimate=cost(2 * 4 * rows * d * units, 16e6, rows * units),
        name="feed",
    )(place, n2, cot, small, *[a for a, _ in ups], *[a for a, _ in downs], *gots)


def turn_kernel(_, mid_ref, cot_ref, table_ref, *refs):
    pre, ups = refs[0:4], refs[4:8]
    gmid_ref, grows_ref, gain_sum, shift_sum, bias_sum = refs[-5:]
    start_sums(gain_sum, shift_sum, bias_sum)
    grad = None
    for g, w in zip(pre, ups):
        term = dot_nt(g[...], w[...])
        grad = term if grad is None else grad + term
    unit, spread = unit_rows(mid_ref[...])
    add_sum(gain_sum, grad * unit)
    add_sum(shift_sum, grad)
    back = norm_back(grad, unit, spread, table_ref[GAIN_MLP])
    grad_middle = cot_ref[...].astype(F32) + back
    gmid_ref[...] = grad_middle
    rows = grad_middle.astype(BF)
    grows_ref[...] = rows
    add_sum(bias_sum, rows.astype(F32))


def turn_call(place, middle, cot, table, pre, ups):
    rows, d = middle.shape
    units = ups[0].shape[1]
    tile = 256
    by_rows = pl.BlockSpec((tile, d), lambda i: (i, 0))
    kept = pl.BlockSpec((d, units), lambda i: (0, 0), pipeline_mode=pl.Buffered(1))
    total = jax.ShapeDtypeStruct((1, d), F32)
    return pl.pallas_call(
        turn_kernel,
        grid=(rows // tile,),
        in_specs=[pl.BlockSpec(memory_space=pltpu.SMEM), by_rows, by_rows, whole(table.shape)]
        + [pl.BlockSpec((tile, units), lambda i: (i, 0))] * 4
        + [kept] * 4,
        out_specs=[by_rows] * 2 + [whole((1, d))] * 3,
        out_shape=[
            jax.ShapeDtypeStruct((rows, d), F32),
            jax.ShapeDtypeStruct((rows, d), BF),
            total,
            total,
            total,
        ],
        compiler_params=params("turn"),
        cost_estimate=cost(2 * 4 * rows * d * units, 20e6),
        name="turn",
    )(place, middle, cot, table, *pre, *ups)


def output_kernel(_, mid_ref, table_ref, *refs):
    hidden, downs, out_ref = refs[0:4], refs[4:8], refs[-1]
    mlp = table_ref[BIAS_DOWN]
    for h, w in zip(hidden, downs):
        mlp = mlp + dot_nt(h[...], w[...])
    out_ref[...] = (mid_ref[...] + mlp).astype(BF)


def output_call(place, middle, table, hidden, downs):
    rows, d = middle.shape
    units = downs[0].shape[1]
    tile = 256
    by_rows = pl.BlockSpec((tile, d), lambda i: (i, 0))
    kept = pl.BlockSpec((d, units), lambda i: (0, 0), pipeline_mode=pl.Buffered(1))
    return pl.pallas_call(
        output_kernel,
        grid=(rows // tile,),
        in_specs=[pl.BlockSpec(memory_space=pltpu.SMEM), by_rows, whole(table.shape)]
        + [pl.BlockSpec((tile, units), lambda i: (i, 0))] * 4
        + [kept] * 4,
        out_specs=by_rows,
        out_shape=jax.ShapeDtypeStruct((rows, d), BF),
        compiler_params=params("output"),
        cost_estimate=cost(2 * 4 * rows * d * units, 16e6),
        name="output",
    )(place, middle, table, *hidden, *downs)


def attend_back_kernel(count, has_got, place_ref, lse_ref, grows_hbm, w_hbm, proj_hbm, n1_hbm, mixed_hbm, *refs):
    got_hbm = refs[0] if has_got else None
    gproj_hbm, sum_ref, *grad_refs = refs[has_got : has_got + 3 + has_got]
    grows, w, projs, n1, mixed, got, gproj_all, sems, out_sems = refs[has_got + 3 + has_got :]
    seqs = lse_ref.shape[0]

    def of_seq(seq):
        return pl.ds(pl.multiple_of(seq * SEQ_LEN, SEQ_LEN), SEQ_LEN)

    def seq_copies(seq):
        return [
            pltpu.make_async_copy(hbm.at[of_seq(seq)], ref.at[of_seq(seq)], sems.at[i, seq])
            for i, (hbm, ref) in enumerate(((grows_hbm, grows), (proj_hbm, projs)))
        ]

    def out_copy(seq):
        return pltpu.make_async_copy(gproj_all.at[of_seq(seq)], gproj_hbm.at[of_seq(seq)], out_sems.at[seq])

    w_copy = pltpu.make_async_copy(w_hbm.at[:, 512:768], w, sems.at[2, 0])
    late = [
        pltpu.make_async_copy(n1_hbm, n1, sems.at[3, 0]),
        pltpu.make_async_copy(mixed_hbm, mixed, sems.at[4, 0]),
    ]
    if has_got:
        late.append(pltpu.make_async_copy(got_hbm, got, sems.at[5, 0]))
    w_copy.start()
    for seq in range(seqs):
        for copy in seq_copies(seq):
            copy.start()
    for copy in late:
        copy.start()
    w_copy.wait()

    @pl.loop(0, seqs)
    def _(seq):
        for copy in seq_copies(seq):
            copy.wait()
        projected = projs[of_seq(seq)]
        grad_mixed = dot(grows[of_seq(seq)], w[...]).astype(BF)
        out = gproj_all.at[of_seq(seq)]
        parts = {}
        early = lax.broadcasted_iota(jnp.int32, (HALF, HALF), 0) <= lax.broadcasted_iota(jnp.int32, (HALF, HALF), 1)
        jobs = []
        for head, (qt, kt, vt, qk_lane, v_lane) in enumerate(HEAD_PLACES):
            mt = 0 if head == 2 else 1
            query = lane_keep(projected[:, qt * 128 : qt * 128 + 128], qk_lane) * BF(0.125)
            keys = projected[:, kt * 128 : kt * 128 + 128]
            values = projected[:, vt * 128 : vt * 128 + 128]
            grads = lane_keep(grad_mixed[:, mt * 128 : mt * 128 + 128], v_lane)
            parts["k", head] = [None, None]
            parts["v", head] = [None, None]
            for block in range(2):
                rows = slice(block * HALF, block * HALF + HALF)
                jobs.append((head, block, qk_lane, query[rows], keys, values, grads[rows]))

        def first_stage(job):
            head, block, _, qb, keys, values, gb = job
            last = block * HALF + HALF
            return dot_nt(keys[0:last], qb), dot_nt(values[0:last], gb)

        def last_stage(job, scores, gprobs):
            head, block, qk_lane, qb, keys, values, gb = job
            last = block * HALF + HALF
            lse = lse_ref[seq, head : head + 1, last - HALF : last]
            probs = jnp.exp(scores - lse)
            corner = jnp.where(early, probs[last - HALF :], 0.0)
            probs = jnp.concatenate([probs[: last - HALF], corner], axis=0) if block else corner
            both = probs * gprobs
            delta = jnp.sum(both, axis=0, keepdims=True)
            gscores = (both - probs * delta).astype(BF)
            gq = dot_tn(keys[0:last], gscores) * 0.125
            parts["q", head, block] = gq[qk_lane : qk_lane + HEAD_DIM]
            gk = dot(gscores, qb)
            gv = dot(probs.astype(BF), gb)
            for name, got in (("k", gk), ("v", gv)):
                held = parts[name, head]
                for b in range(block + 1):
                    part = got[b * HALF : b * HALF + HALF]
                    held[b] = part if held[b] is None else held[b] + part

        waiting = None
        for job in jobs + [None]:
            ahead = None if job is None else (job, *first_stage(job))
            if waiting is not None:
                last_stage(*waiting)
            waiting = ahead
        for block in range(2):
            rows = slice(block * HALF, block * HALF + HALF)
            pair = jnp.concatenate([parts["q", 0, block], parts["q", 1, block]], axis=0).T
            lone = parts["q", 2, block]
            lone = jnp.concatenate([lone, jnp.zeros_like(lone)], axis=0).T
            out[rows, 0:128] = pair.astype(BF)
            out[rows, 128:256] = (parts["k", 0][block] + parts["k", 1][block]).astype(BF)
            out[rows, 256:384] = (parts["v", 0][block] + parts["v", 1][block]).astype(BF)
            out[rows, 384:512] = (lone + parts["v", 2][block]).astype(BF)
            out[rows, 512:640] = parts["k", 2][block].astype(BF)
        out_copy(seq).start()

    gproj = gproj_all[...]
    sum_ref[...] = jnp.sum(gproj.astype(F32), axis=0, keepdims=True)
    for copy in late:
        copy.wait()
    grad_a = dot_tn(n1[...], gproj)
    grad_b = dot_tn(grows[...], mixed[...])
    grad = jnp.concatenate(
        [grad_a[:, 0:512], grad_a[:, 512:640] + grad_b[:, 0:128], grad_b[:, 128:256]], axis=1
    )
    if has_got:
        store_split(*grad_refs, got, (), place_ref, grad, count)
    else:
        store_all(*grad_refs, (), place_ref, grad, count)
    for seq in range(seqs):
        out_copy(seq).wait()


def attend_back_call(place, count, grows, n1, w, proj, mixed, lse, got=None):
    rows, d = grows.shape
    seqs = rows // SEQ_LEN
    shard = d // (2 * count)
    gots = () if got is None else (got,)
    both = (2 * count, shard, 768)
    grads = [both] if got is None else [(count, shard, 768)] * 2
    hbm = pl.BlockSpec(memory_space=pl.ANY)
    return pl.pallas_call(
        functools.partial(attend_back_kernel, count, len(gots)),
        grid=(1,),
        in_specs=[pl.BlockSpec(memory_space=pltpu.SMEM), whole(lse.shape)] + [hbm] * (5 + len(gots)),
        out_specs=[hbm, whole((1, 640))] + [whole(g) for g in grads],
        out_shape=[jax.ShapeDtypeStruct((rows, 640), BF), jax.ShapeDtypeStruct((1, 640), F32)]
        + [jax.ShapeDtypeStruct(g, BF) for g in grads],
        scratch_shapes=[
            pltpu.VMEM((rows, d), BF),
            pltpu.VMEM((d, 256), BF),
            pltpu.VMEM((rows, 640), BF),
            pltpu.VMEM((rows, d), BF),
            pltpu.VMEM((rows, 256), BF),
            pltpu.VMEM(both if got is not None else (8, 16, 128), BF),
            pltpu.VMEM((rows, 640), BF),
            pltpu.SemaphoreType.DMA((6, seqs)),
            pltpu.SemaphoreType.DMA((seqs,)),
        ],
        compiler_params=params("attend_back"),
        cost_estimate=cost(10e9, 12e6),
        name="attend_back",
    )(place, lse, grows, w, proj, n1, mixed, *gots)


def finish_kernel(_, x_ref, gmid_ref, table_ref, *refs):
    gproj, weights, known, sum_proj, sum_up = refs[0:4], refs[4:8], refs[8:12], refs[12:16], refs[16:20]
    out_ref, keep_ref, away_ref, gain_sum, shift_sum = refs[20:]
    start_sums(gain_sum, shift_sum)
    grad = None
    for g, w in zip(gproj, weights):
        term = dot_nt(g[...], w[...])
        grad = term if grad is None else grad + term
    unit, spread = unit_rows(x_ref[...].astype(F32))
    add_sum(gain_sum, grad * unit)
    add_sum(shift_sum, grad)
    back = norm_back(grad, unit, spread, table_ref[GAIN_ATTN])
    out_ref[...] = (gmid_ref[...] + back).astype(BF)

    @pl.when(pl.program_id(0) == pl.num_programs(0) - 1)
    def _():
        shared = jnp.concatenate(
            [r[...] for r in known] + [gain_sum[...], shift_sum[...]], axis=1
        )
        for dy in range(2):
            for dc, ref in enumerate((keep_ref, away_ref)):
                row = jnp.concatenate([shared, sum_proj[2 * dy + dc][...], sum_up[2 * dy + dc][...]], axis=1)
                ref[dy : dy + 1] = row


def finish_call(place, x, gmid, table, gproj, weights, known, sum_proj, sum_up):
    rows, d = x.shape
    tile = 256
    by_rows = pl.BlockSpec((tile, d), lambda i: (i, 0))
    width = 6 * d + sum_proj[0].shape[1] + sum_up[0].shape[1]
    return pl.pallas_call(
        finish_kernel,
        grid=(rows // tile,),
        in_specs=[pl.BlockSpec(memory_space=pltpu.SMEM), by_rows, by_rows, whole(table.shape)]
        + [pl.BlockSpec((tile, 640), lambda i: (i, 0))] * 4
        + [pl.BlockSpec((d, 640), lambda i: (0, 0))] * 4
        + [whole(v.shape) for v in (*known, *sum_proj, *sum_up)],
        out_specs=[by_rows, whole((2, width)), whole((2, width))],
        out_shape=[jax.ShapeDtypeStruct((rows, d), BF)] + [jax.ShapeDtypeStruct((2, width), F32)] * 2,
        scratch_shapes=[pltpu.VMEM((1, d), F32)] * 2,
        compiler_params=params("finish"),
        cost_estimate=cost(2 * 4 * rows * d * 640, 16e6),
        name="finish",
    )(place, x, gmid, table, *gproj, *weights, *known, *sum_proj, *sum_up)


class Links:
    def __init__(self, mesh):
        self.count = mesh.shape["fsdp"] // 2
        places = [
            (z, x, y, c)
            for z in range(self.count)
            for x in range(2)
            for y in range(2)
            for c in range(2)
        ]

        def index(z, x, y, c):
            return ((z * 2 + x) * 2 + y) * 2 + c

        def pairs(move):
            return [(index(*p), index(*move(*p))) for p in places]

        self.core = pairs(lambda z, x, y, c: (z, x, y, 1 - c))
        self.y = pairs(lambda z, x, y, c: (z, x, 1 - y, c))
        self.x = pairs(lambda z, x, y, c: (z, 1 - x, y, c))
        self.ring = pairs(lambda z, x, y, c: ((z + 1) % self.count, x, y, c))
        self.far = [
            pairs(lambda z, x, y, c, k=k: ((z + k) % self.count, x, y, c)) for k in range(self.count)
        ]
        self.back = [
            pairs(lambda z, x, y, c, k=k: ((z - k) % self.count, x, y, c)) for k in range(self.count)
        ]
        self.xy = pairs(lambda z, x, y, c: (z, 1 - x, 1 - y, c))
        self.trees = []
        step = 1
        while step < self.count:
            size = 4 if step * 4 <= self.count else 2
            self.trees.append(
                [pairs(lambda z, x, y, c, b=step * k: (z ^ b, x, y, c)) for k in range(1, size)]
            )
            step *= size

    @staticmethod
    def send(value, pairs):
        return lax.ppermute(value, AXES, pairs)


def plus(*terms, kind=BF):
    total = terms[0].astype(F32)
    for term in terms[1:]:
        total = total + term.astype(F32)
    return total.astype(kind)


def tie(value, *others):
    return lax.optimization_barrier((value, others))[0]


def ring_from(links, first):
    held = [first]
    for _ in range(links.count - 1):
        held.append(links.send(held[-1], links.ring))
    return held


def gather_and_attend(links, place, attn, up, down, n1, smalls, layer_input, table):
    n = links.count
    half = n // 2
    small_y = links.send(smalls, links.y)

    near = [jnp.stack([attn, down])]
    done = (n1,)
    for k in range(1, n):
        now = near[-1] if k == 1 else tie(near[-1], *done)
        near.append(links.send(now, links.ring))
        if k == 3:
            steps.append(links.send(tie(steps[0], near[2]), links.ring))
        done = (near[-1],)
        if k == 1:
            pair = jnp.stack([up, links.send(up, links.x)])
            done += (pair, n1, smalls)
        if k == 2:
            steps = [jnp.stack([pair, links.send(tie(pair, near[1]), links.y)])]
            done += (steps[0], small_y)
        if k == half:
            lines = [jnp.stack([v[0] for v in near[:half]])]
            others = [links.send(lines[0], links.x)]
            done += (others[0],)
        if k == half + 1:
            quads = [links.send(tie(jnp.stack([lines[0], others[0]]), *near[half:-1]), links.y)]
            smalls = [smalls, links.send(smalls, links.core), small_y, links.send(small_y, links.core)]
            done += (smalls[1], smalls[3], quads[0])

    lines.append(tie(jnp.stack([v[0] for v in near[half:]]), *done))
    others.append(links.send(lines[1], links.x))
    line = jnp.stack([v[1] for v in near])
    beyond = [links.send(tie(line, *done), links.y)]
    steps.append(links.send(tie(steps[-1], *done), links.ring))
    core = lambda values: [links.send(v, links.core) for v in values]

    def from_lines(*pair):
        return [(v[k // half], (k % half,)) for v in pair for k in range(n)]

    def from_quads(quads):
        return [(quads[k // half], (dx, k % half)) for dx in range(2) for k in range(n)]

    quads.append(links.send(jnp.stack([lines[1], others[1]]), links.y))
    far = links.send(tie(line, others[1]), links.x)

    attn_w, proj, mixed, lse = [], [], [], []

    def attend(pieces, *before):
        j = len(proj)
        w, p, m, s = attend_call(tie(place, *before) if before else place, n1, pieces, smalls[j])
        attn_w.append(w)
        proj.append(p)
        mixed.append(m)
        lse.append(s)

    attend(from_lines(lines, others))
    attend(from_lines(core(lines), core(others)), mixed[0])
    quads_core = core([quads[0], tie(quads[1], mixed[1])])
    beyond.append(links.send(tie(beyond[0], far), links.x))
    for _ in range(3, n):
        steps.append(links.send(tie(steps[-1], mixed[1]), links.ring))
    attend(from_quads(quads), mixed[1], quads[1], far, steps[2])
    attend(from_quads(quads_core), mixed[2])
    middle, n2 = middle_call(layer_input, table, mixed, attn_w)

    steps[-1] = tie(steps[-1], mixed[3])
    up_core = core(steps)
    up_w = [[(v, (dy, dx)) for dx in range(2) for v in vs] for dy in range(2) for vs in (steps, up_core)]
    down_w = [
        [(v, (k,)) for v in vs for k in range(n)]
        for pair in ((line, far), beyond)
        for vs in (pair, core(pair))
    ]
    return attn_w, up_w, down_w, proj, mixed, lse, smalls, middle, n2


def spread_sum(links, home):
    got = [links.send(home[k], links.far[k]) for k in range(1, links.count)]
    return plus(home[0], *got, kind=F32)


def sum_near(links, keep, away):
    rows = keep + links.send(away, links.core)
    near, far = rows[0:1], rows[1:2]
    return (near + links.send(near, links.x)) + (
        links.send(far, links.y) + links.send(far, links.xy)
    )


def sum_far(links, total):
    for pairs in links.trees:
        got = [total] + [links.send(total, p) for p in pairs]
        while len(got) > 1:
            got = [got[i] + got[i + 1] for i in range(0, len(got), 2)]
        total = got[0]
    return total


def pack_attn(w_qkv, w_out):
    q, k, v, o = w_qkv[:, 0], w_qkv[:, 1], w_qkv[:, 2], w_out.T
    return jnp.concatenate(
        [q[:, :128], k[:, :128], v[:, :128], q[:, 128:], v[:, 128:], k[:, 128:], o[:, 128:], o[:, :128]],
        axis=1,
    )


def unpack_attn(g):
    q = jnp.concatenate([g[:, 0:128], g[:, 384:448]], axis=1)
    k = jnp.concatenate([g[:, 128:256], g[:, 512:576]], axis=1)
    v = jnp.concatenate([g[:, 256:384], g[:, 448:512]], axis=1)
    o = jnp.concatenate([g[:, 640:768], g[:, 576:640]], axis=1)
    return jnp.stack([q, k, v], axis=1), o.T


def body(
    links,
    layer_input,
    w_qkv,
    bias_qv,
    w_out,
    bias_out,
    gain_attn,
    shift_attn,
    gain_mlp,
    shift_mlp,
    w_up,
    bias_up,
    w_down,
    bias_down,
    cotangent,
):
    fsdp = lax.axis_index("fsdp")
    place = jnp.stack([fsdp // 2, fsdp % 2]).astype(jnp.int32)
    count = links.count
    n1, sum_down, small, table = start_call(
        layer_input,
        cotangent,
        bias_qv,
        bias_up,
        (bias_out, gain_attn, shift_attn, gain_mlp, shift_mlp, bias_down),
    )
    attn_w, up_w, down_w, proj, mixed, lse, smalls, middle, n2 = gather_and_attend(
        links, place, pack_attn(w_qkv, w_out), w_up, w_down.T, n1, small, layer_input, table
    )

    hidden, pre, sum_up = [None] * 4, [None] * 4, [None] * 4
    up_home, up_away, down_sum = [None] * 2, [None] * 2, [None] * 2
    gots = [None] * 4
    for j in (1, 3, 0, 2):
        out = feed_call(
            place, count, n2, cotangent, up_w[j], down_w[j], smalls[j], gots[j]
        )
        hidden[j], pre[j], sum_up[j], up_w[j], down_w[j] = out[0:5]
        if j % 2:
            gots[j - 1] = links.send(out[5], links.core)
        else:
            up_home[j // 2], up_away[j // 2], down_sum[j // 2] = out[5:8]

    got_x0 = links.send(up_away[0], links.x)
    got_x1 = links.send(up_away[1], links.x)
    got_down = links.send(down_sum[1], links.y)
    gmid, grows, gain_two, shift_two, sum_out = turn_call(
        place, middle, cotangent, table, pre, up_w
    )

    gproj, sum_proj = [None] * 4, [None] * 4
    attn_home, attn_away = [None] * 2, [None] * 2

    def back(j, got, *before):
        out = attend_back_call(
            tie(place, *before) if before else place,
            count,
            grows,
            n1,
            attn_w[j],
            proj[j],
            mixed[j],
            lse[j],
            got,
        )
        gproj[j], sum_proj[j] = out[0:2]
        if j % 2:
            return links.send(out[2], links.core)
        attn_home[j // 2], attn_away[j // 2] = out[2:4]

    got_three = back(3, None, got_x0)
    up_beyond = plus(up_home[1], got_x1)
    got_up = links.send(up_beyond, links.y)
    got_one = back(1, None, up_beyond)
    down_away = plus(down_sum[0][count:], got_down[count:])
    got_x = links.send(down_away, links.x)
    back(2, got_three, down_away)
    got_a1 = links.send(attn_away[1], links.x)
    up_all = plus(up_home[0], got_x0, got_up)
    down_all = plus(down_sum[0][:count], got_down[:count], got_x)
    back(0, got_one, up_all, down_all, sum_proj[2])
    grad_up = spread_sum(links, up_all)
    grad_down = spread_sum(links, down_all)
    got_a0 = links.send(attn_away[0], links.x)
    attn_beyond = plus(attn_home[1], got_a1)
    got_attn = links.send(attn_beyond, links.y)
    grad_input, keep, away = finish_call(
        tie(place, attn_beyond, grad_up),
        layer_input,
        gmid,
        table,
        gproj,
        attn_w,
        (sum_out, sum_down, gain_two, shift_two),
        sum_proj,
        sum_up,
    )
    attn_all = plus(tie(attn_home[0], keep), got_a0, got_attn)
    parts = [attn_all[0]] + [links.send(attn_all[k], links.far[k]) for k in range(1, count)]
    total = sum_near(links, keep, tie(away, attn_all))
    before = (total, attn_all, grad_up, grad_down)
    layer_output = output_call(tie(place, *before), middle, table, hidden, down_w)
    sums = sum_far(links, tie(total, layer_output, *parts))
    grad_attn = plus(*parts, kind=F32)

    d = layer_input.shape[1]
    heads = bias_qv.shape[1]
    vec = sums[0]
    total_out, total_down, gain_two, shift_two, gain_one, shift_one = (
        vec[i * d : (i + 1) * d] for i in range(6)
    )
    own = vec[6 * d :]
    total_qv = jnp.stack(
        [
            jnp.concatenate([own[0:128], own[384:448]]),
            jnp.concatenate([own[256:384], own[448:512]]),
        ]
    )
    total_up = own[640:]

    shard_qkv, shard_out = unpack_attn(grad_attn)
    return (
        layer_output,
        grad_input,
        shard_qkv,
        total_qv,
        shard_out,
        total_out,
        gain_one,
        shift_one,
        gain_two,
        shift_two,
        grad_up,
        total_up,
        grad_down.T,
        total_down,
    )


def solution(mesh):
    tokens = P(("fsdp", "tp"), None)
    placed = (
        tokens,
        P("fsdp", None, "tp"),
        P(None, "tp"),
        P("tp", "fsdp"),
        P(),
        P(),
        P(),
        P(),
        P(),
        P("fsdp", "tp"),
        P("tp"),
        P("tp", "fsdp"),
        P(),
        tokens,
    )
    return jax.shard_map(
        functools.partial(body, Links(mesh)),
        mesh=mesh,
        in_specs=placed,
        out_specs=(
            tokens,
            tokens,
            P("fsdp", None, "tp"),
            P(None, "tp"),
            P("tp", "fsdp"),
            P(),
            P(),
            P(),
            P(),
            P(),
            P("fsdp", "tp"),
            P("tp"),
            P("tp", "fsdp"),
            P(),
        ),
        check_vma=False,
    )
```

```python
import functools

import jax
import jax.numpy as jnp
from jax import lax
from jax.experimental import pallas as pl
from jax.experimental.pallas import tpu as pltpu
from jax.sharding import PartitionSpec as P

HEAD_DIM = 64
SEQ_LEN = 512
HALF = 256
EPS = 1e-05
AXES = ("fsdp", "tp")
BF = jnp.bfloat16
F32 = jnp.float32
MB = 1 << 20
SHARE = 0.32
BIAS_OUT, GAIN_ATTN, SHIFT_ATTN, GAIN_MLP, SHIFT_MLP, BIAS_DOWN = (slice(i, i + 1) for i in range(6))
VMEM_MB = {"start": 60, "feed": 60, "attend_back": 60, "turn": 60, "finish": 60, "output": 60}
SMALL_ATTN = 768


def dot(left, right):
    return lax.dot_general(left, right, (((1,), (0,)), ((), ())), preferred_element_type=F32)


def dot_nt(left, right):
    return lax.dot_general(left, right, (((1,), (1,)), ((), ())), preferred_element_type=F32)


def dot_tn(left, right):
    return lax.dot_general(left, right, (((0,), (0,)), ((), ())), preferred_element_type=F32)


def whole(shape):
    zeros = (0,) * len(shape)
    return pl.BlockSpec(shape, lambda *_: zeros)


def params(kernel):
    return pltpu.CompilerParams(vmem_limit_bytes=VMEM_MB.get(kernel, 36) * MB)


def cost(flops, nbytes, trans=0):
    return pl.CostEstimate(
        flops=int(flops * SHARE), bytes_accessed=int(nbytes * SHARE), transcendentals=int(trans * SHARE)
    )


def unit_rows(rows):
    centre = rows - jnp.mean(rows, axis=-1, keepdims=True)
    spread = lax.rsqrt(jnp.mean(centre * centre, axis=-1, keepdims=True) + EPS)
    return centre * spread, spread


def norm_back(grad_out, unit, spread, gain):
    scaled = grad_out * gain
    inner = jnp.mean(scaled * unit, axis=-1, keepdims=True)
    return spread * (scaled - jnp.mean(scaled, axis=-1, keepdims=True) - unit * inner)


def start_sums(*refs):
    @pl.when(pl.program_id(0) == 0)
    def _():
        for ref in refs:
            ref[...] = jnp.zeros_like(ref)


def add_sum(ref, value):
    ref[...] += jnp.sum(value, axis=0, keepdims=True)


def start_kernel(x_ref, cot_ref, qv_ref, up_ref, *refs):
    vectors, (n1_ref, sum_ref, small_ref, table_ref) = refs[:6], refs[6:]
    start_sums(sum_ref)

    @pl.when(pl.program_id(0) == 0)
    def _():
        for i, ref in enumerate(vectors):
            table_ref[i : i + 1] = ref[...].astype(F32).reshape(1, -1)
        small_ref[...] = jnp.zeros_like(small_ref)
        for c in range(2):
            pair, lone = (0, 384) if c == 0 else (256, 448)
            row = qv_ref[c : c + 1].astype(F32)
            small_ref[:, pair : pair + 128] = row[:, 0:128]
            small_ref[:, lone : lone + HEAD_DIM] = row[:, 128:192]
        small_ref[:, SMALL_ATTN:] = up_ref[...].astype(F32).reshape(1, -1)

    unit, _ = unit_rows(x_ref[...].astype(F32))
    normed = unit * table_ref[GAIN_ATTN] + table_ref[SHIFT_ATTN]
    n1_ref[...] = normed.astype(BF)
    add_sum(sum_ref, cot_ref[...].astype(F32))


def start_call(x, cot, bias_qv, bias_up, vectors):
    rows, d = x.shape
    units = bias_up.shape[0]
    tile = 256
    by_rows = pl.BlockSpec((tile, d), lambda i: (i, 0))
    return pl.pallas_call(
        start_kernel,
        grid=(rows // tile,),
        in_specs=[by_rows, by_rows, whole(bias_qv.shape), whole(bias_up.shape)]
        + [whole(v.shape) for v in vectors],
        out_specs=[by_rows]
        + [whole((1, d)), whole((1, SMALL_ATTN + units)), whole((8, d))],
        out_shape=[
            jax.ShapeDtypeStruct((rows, d), BF),
            jax.ShapeDtypeStruct((1, d), F32),
            jax.ShapeDtypeStruct((1, SMALL_ATTN + units), F32),
            jax.ShapeDtypeStruct((8, d), F32),
        ],
        compiler_params=params("start"),
        cost_estimate=cost(0, 10 * rows * d),
        name="start",
    )(x, cot, bias_qv, bias_up, *vectors)


def piece_specs(pieces, cols, index):
    rows = pieces[0][0].shape[-2]
    return [
        pl.BlockSpec((1,) * len(lead) + (rows, cols), lambda i, lead=lead: lead + (0, index(i)))
        for _, lead in pieces
    ]


def place_pieces(place_ref, pieces, out_ref):
    count = len(pieces) // 2
    z, x = place_ref[0], place_ref[1]
    for k in range(count):
        for dx in range(2):
            piece = pieces[dx * count + k]
            size, cols = piece.shape[-2:]
            slot = lax.rem(z - k + count, count) * 2 + lax.rem(x + dx, 2)
            out_ref[pl.ds(pl.multiple_of(slot * size, size), size)] = piece[...].reshape(size, cols)


HEAD_PLACES = ((0, 1, 2, 0, 0), (0, 1, 2, 64, 64), (3, 4, 3, 0, 64))


def lane_keep(tile, first):
    lanes = lax.broadcasted_iota(jnp.int32, tile.shape, 1)
    keep = (lanes >= first) & (lanes < first + HEAD_DIM)
    return jnp.where(keep, tile, jnp.zeros_like(tile))


def attend_kernel(place_ref, n1_ref, bias_ref, *refs):
    pieces, (w_ref, proj_ref, mixed_ref, lse_ref) = refs[:-4], refs[-4:]

    @pl.when(pl.program_id(0) == 0)
    def _():
        place_pieces(place_ref, pieces, w_ref)

    projected = (dot(n1_ref[...], w_ref[:, 0:640]) + bias_ref[...].astype(F32)).astype(BF)
    proj_ref[...] = projected
    lse_ref[...] = jnp.zeros_like(lse_ref)
    outs = {}
    early = lax.broadcasted_iota(jnp.int32, (HALF, HALF), 0) <= lax.broadcasted_iota(jnp.int32, (HALF, HALF), 1)
    jobs = []
    for head, (qt, kt, vt, qk_lane, v_lane) in enumerate(HEAD_PLACES):
        query = lane_keep(projected[:, qt * 128 : qt * 128 + 128], qk_lane) * BF(0.125)
        keys = projected[:, kt * 128 : kt * 128 + 128]
        values = projected[:, vt * 128 : vt * 128 + 128]
        for block in range(2):
            first, last = block * HALF, block * HALF + HALF
            jobs.append((head, first, last, query[first:last], keys[0:last], values[0:last], v_lane))

    def last_stage(job, scores):
        head, first, last, _, _, values, v_lane = job
        corner = jnp.where(early, scores[first:], -1e30)
        scores = jnp.concatenate([scores[:first], corner], axis=0) if first else corner
        top = jnp.max(scores, axis=0, keepdims=True)
        weight = jnp.exp(scores - top)
        total = jnp.sum(weight, axis=0, keepdims=True)
        mixed = dot_tn(values, weight.astype(BF)) * (1.0 / total)
        outs[head, first // HALF] = mixed[v_lane : v_lane + HEAD_DIM]
        lse_ref[0, head : head + 1, first:last] = top + jnp.log(total)

    waiting = None
    for job in jobs + [None]:
        ahead = None if job is None else (job, dot_nt(job[4], job[3]))
        if waiting is not None:
            last_stage(*waiting)
        waiting = ahead
    for block in range(2):
        first = block * HALF
        rows = slice(first, first + HALF)
        single = jnp.concatenate([jnp.zeros_like(outs[2, block]), outs[2, block]], axis=0)
        pair = jnp.concatenate([outs[0, block], outs[1, block]], axis=0)
        mixed_ref[rows, 0:128] = single.T.astype(BF)
        mixed_ref[rows, 128:256] = pair.T.astype(BF)


def attend_call(place, n1, pieces, bias):
    rows, d = n1.shape
    seqs = rows // SEQ_LEN
    return pl.pallas_call(
        attend_kernel,
        grid=(seqs,),
        in_specs=[
            pl.BlockSpec(memory_space=pltpu.SMEM),
            pl.BlockSpec((SEQ_LEN, d), lambda i: (i, 0)),
            pl.BlockSpec((1, 640), lambda i: (0, 0)),
        ]
        + piece_specs(pieces, 768, lambda i: 0),
        out_specs=[
            whole((d, 768)),
            pl.BlockSpec((SEQ_LEN, 640), lambda i: (i, 0)),
            pl.BlockSpec((SEQ_LEN, 256), lambda i: (i, 0)),
            pl.BlockSpec((1, 8, SEQ_LEN), lambda i: (i, 0, 0)),
        ],
        out_shape=[
            jax.ShapeDtypeStruct((d, 768), BF),
            pltpu.HBM((rows, 640), BF),
            jax.ShapeDtypeStruct((rows, 256), BF),
            pltpu.HBM((seqs, 8, SEQ_LEN), F32),
        ],
        compiler_params=params("attend"),
        cost_estimate=cost(6e9, 8e6),
        name="attend",
    )(place, n1, bias, *[array for array, _ in pieces])


def middle_kernel(x_ref, table_ref, *refs):
    mixed, weights, (mid_ref, n2_ref) = refs[0:4], refs[4:8], refs[8:]
    attended = table_ref[BIAS_OUT]
    for m, w in zip(mixed, weights):
        attended = attended + dot_nt(m[...], w[...])
    middle = x_ref[...].astype(F32) + attended
    mid_ref[...] = middle
    unit, _ = unit_rows(middle)
    normed = unit * table_ref[GAIN_MLP] + table_ref[SHIFT_MLP]
    n2_ref[...] = normed.astype(BF)


def middle_call(x, table, mixed, weights):
    rows, d = x.shape
    tile = 256
    by_rows = pl.BlockSpec((tile, d), lambda i: (i, 0))
    return pl.pallas_call(
        middle_kernel,
        grid=(rows // tile,),
        in_specs=[by_rows, whole(table.shape)]
        + [pl.BlockSpec((tile, 256), lambda i: (i, 0))] * 4
        + [pl.BlockSpec((d, 256), lambda i: (0, 2))] * 4,
        out_specs=[by_rows, by_rows],
        out_shape=[pltpu.HBM((rows, d), F32), pltpu.HBM((rows, d), BF)],
        compiler_params=params("middle"),
        cost_estimate=cost(2 * rows * d * 1024, 16e6),
        name="middle",
    )(x, table, *mixed, *weights)


def gelu_both(value):
    cumulative = 0.5 + 0.5 * lax.erf(value * 2.0**-0.5)
    bell = jnp.exp(-0.5 * value * value)
    return value * cumulative, cumulative + value * bell * (2.0 * 3.141592653589793) ** -0.5


def store_all(ref, lead, place_ref, value, count, got_ref=None, got_lead=()):
    z, x = place_ref[0], place_ref[1]
    size = value.shape[0] // (2 * count)
    for block in range(2 * count):
        slot = lax.rem(x + block % 2, 2) * count + lax.rem(block // 2 - z + count, count)
        part = value[block * size : (block + 1) * size]
        if got_ref is not None:
            part = part + got_ref[got_lead + (slot,)].astype(F32)
        ref[lead + (slot,)] = part.astype(BF)


def store_split(home_ref, away_ref, got_ref, lead, place_ref, value, count):
    z, x = place_ref[0], place_ref[1]
    size = value.shape[0] // (2 * count)
    for pair in range(count):
        slot = lax.rem(pair - z + count, count)
        first = value[2 * pair * size : (2 * pair + 1) * size]
        second = value[(2 * pair + 1) * size : (2 * pair + 2) * size]
        home = jnp.where(x == 0, first, second) + got_ref[lead + (slot,)].astype(F32)
        away = jnp.where(x == 0, second, first) + got_ref[lead + (count + slot,)].astype(F32)
        home_ref[slot] = home.astype(BF)
        away_ref[slot] = away.astype(BF)


def feed_kernel(count, tokens, has_got, place_ref, n2_ref, cot_ref, bias_ref, *refs):
    ups, downs, refs = refs[: 2 * count], refs[2 * count : 4 * count], refs[4 * count :]
    got_ref = refs[0] if has_got else None
    hidden_ref, pre_ref, sum_ref, up_ref, down_ref, *outs = refs[has_got:]
    place_pieces(place_ref, ups, up_ref)
    place_pieces(place_ref, downs, down_ref)
    rows = n2_ref.shape[0]
    up, down, bias = up_ref[...], down_ref[...], bias_ref[...].astype(F32)
    total = jnp.zeros_like(bias)
    for first in range(0, rows, tokens):
        here = slice(first, first + tokens)
        pre = dot(n2_ref[here], up) + bias
        grad_hidden = dot(cot_ref[here], down)
        hidden, slope = gelu_both(pre)
        hidden_ref[here] = hidden.astype(BF)
        grad_pre = (grad_hidden * slope).astype(BF)
        pre_ref[here] = grad_pre
        total = total + jnp.sum(grad_pre.astype(F32), axis=0, keepdims=True)
    sum_ref[...] = total
    grads = (dot_tn(n2_ref[...], pre_ref[...]), dot_tn(cot_ref[...], hidden_ref[...]))
    if has_got:
        store_split(outs[0], outs[1], got_ref, (0,), place_ref, grads[0], count)
        store_all(outs[2], (), place_ref, grads[1], count, got_ref, (1,))
    else:
        store_all(outs[0], (0,), place_ref, grads[0], count)
        store_all(outs[0], (1,), place_ref, grads[1], count)


def feed_call(place, count, n2, cot, ups, downs, small, got=None):
    rows, d = n2.shape
    units = ups[0][0].shape[-1]
    tile = 256
    shard = d // (2 * count)
    cols = lambda n: pl.BlockSpec((n, tile), lambda i: (0, i))
    hid = jax.ShapeDtypeStruct((rows, units), BF)
    both_spec = pl.BlockSpec((2, 2 * count, shard, tile), lambda i: (0, 0, 0, i))
    if got is None:
        grad_specs = [both_spec]
        grads = [jax.ShapeDtypeStruct((2, 2 * count, shard, units), BF)]
    else:
        grad_specs = [pl.BlockSpec((n, shard, tile), lambda i: (0, 0, i)) for n in (count, count, 2 * count)]
        grads = [jax.ShapeDtypeStruct((n, shard, units), BF) for n in (count, count, 2 * count)]
    gots = () if got is None else (got,)
    return pl.pallas_call(
        functools.partial(feed_kernel, count, 512, len(gots)),
        grid=(units // tile,),
        in_specs=[
            pl.BlockSpec(memory_space=pltpu.SMEM),
            whole((rows, d)),
            whole((rows, d)),
            pl.BlockSpec((1, tile), lambda i: (0, SMALL_ATTN // tile + i)),
        ]
        + piece_specs(ups, tile, lambda i: i)
        + piece_specs(downs, tile, lambda i: i)
        + [both_spec] * len(gots),
        out_specs=[cols(rows)] * 2 + [cols(1)] + [cols(d)] * 2 + grad_specs,
        out_shape=[hid] * 2
        + [jax.ShapeDtypeStruct((1, units), F32)]
        + [jax.ShapeDtypeStruct((d, units), BF)] * 2
        + grads,
        compiler_params=params("feed"),
        cost_estimate=cost(2 * 4 * rows * d * units, 16e6, rows * units),
        name="feed",
    )(place, n2, cot, small, *[a for a, _ in ups], *[a for a, _ in downs], *gots)


def turn_kernel(_, mid_ref, cot_ref, table_ref, *refs):
    pre, ups = refs[0:4], refs[4:8]
    gmid_ref, grows_ref, gain_sum, shift_sum, bias_sum = refs[-5:]
    start_sums(gain_sum, shift_sum, bias_sum)
    grad = None
    for g, w in zip(pre, ups):
        term = dot_nt(g[...], w[...])
        grad = term if grad is None else grad + term
    unit, spread = unit_rows(mid_ref[...])
    add_sum(gain_sum, grad * unit)
    add_sum(shift_sum, grad)
    back = norm_back(grad, unit, spread, table_ref[GAIN_MLP])
    grad_middle = cot_ref[...].astype(F32) + back
    gmid_ref[...] = grad_middle
    rows = grad_middle.astype(BF)
    grows_ref[...] = rows
    add_sum(bias_sum, rows.astype(F32))


def turn_call(place, middle, cot, table, pre, ups):
    rows, d = middle.shape
    units = ups[0].shape[1]
    tile = 256
    by_rows = pl.BlockSpec((tile, d), lambda i: (i, 0))
    kept = pl.BlockSpec((d, units), lambda i: (0, 0), pipeline_mode=pl.Buffered(1))
    total = jax.ShapeDtypeStruct((1, d), F32)
    return pl.pallas_call(
        turn_kernel,
        grid=(rows // tile,),
        in_specs=[pl.BlockSpec(memory_space=pltpu.SMEM), by_rows, by_rows, whole(table.shape)]
        + [pl.BlockSpec((tile, units), lambda i: (i, 0))] * 4
        + [kept] * 4,
        out_specs=[by_rows] * 2 + [whole((1, d))] * 3,
        out_shape=[
            jax.ShapeDtypeStruct((rows, d), F32),
            jax.ShapeDtypeStruct((rows, d), BF),
            total,
            total,
            total,
        ],
        compiler_params=params("turn"),
        cost_estimate=cost(2 * 4 * rows * d * units, 20e6),
        name="turn",
    )(place, middle, cot, table, *pre, *ups)


def output_kernel(_, mid_ref, table_ref, *refs):
    hidden, downs, out_ref = refs[0:4], refs[4:8], refs[-1]
    mlp = table_ref[BIAS_DOWN]
    for h, w in zip(hidden, downs):
        mlp = mlp + dot_nt(h[...], w[...])
    out_ref[...] = (mid_ref[...] + mlp).astype(BF)


def output_call(place, middle, table, hidden, downs):
    rows, d = middle.shape
    units = downs[0].shape[1]
    tile = 256
    by_rows = pl.BlockSpec((tile, d), lambda i: (i, 0))
    kept = pl.BlockSpec((d, units), lambda i: (0, 0), pipeline_mode=pl.Buffered(1))
    return pl.pallas_call(
        output_kernel,
        grid=(rows // tile,),
        in_specs=[pl.BlockSpec(memory_space=pltpu.SMEM), by_rows, whole(table.shape)]
        + [pl.BlockSpec((tile, units), lambda i: (i, 0))] * 4
        + [kept] * 4,
        out_specs=by_rows,
        out_shape=jax.ShapeDtypeStruct((rows, d), BF),
        compiler_params=params("output"),
        cost_estimate=cost(2 * 4 * rows * d * units, 16e6),
        name="output",
    )(place, middle, table, *hidden, *downs)


def attend_back_kernel(count, has_got, place_ref, lse_ref, grows_hbm, w_hbm, proj_hbm, n1_hbm, mixed_hbm, *refs):
    got_hbm = refs[0] if has_got else None
    gproj_hbm, sum_ref, *grad_refs = refs[has_got : has_got + 3 + has_got]
    grows, w, projs, n1, mixed, got, gproj_all, sems, out_sems = refs[has_got + 3 + has_got :]
    seqs = lse_ref.shape[0]

    def of_seq(seq):
        return pl.ds(pl.multiple_of(seq * SEQ_LEN, SEQ_LEN), SEQ_LEN)

    def seq_copies(seq):
        return [
            pltpu.make_async_copy(hbm.at[of_seq(seq)], ref.at[of_seq(seq)], sems.at[i, seq])
            for i, (hbm, ref) in enumerate(((grows_hbm, grows), (proj_hbm, projs)))
        ]

    def out_copy(seq):
        return pltpu.make_async_copy(gproj_all.at[of_seq(seq)], gproj_hbm.at[of_seq(seq)], out_sems.at[seq])

    w_copy = pltpu.make_async_copy(w_hbm.at[:, 512:768], w, sems.at[2, 0])
    late = [
        pltpu.make_async_copy(n1_hbm, n1, sems.at[3, 0]),
        pltpu.make_async_copy(mixed_hbm, mixed, sems.at[4, 0]),
    ]
    if has_got:
        late.append(pltpu.make_async_copy(got_hbm, got, sems.at[5, 0]))
    w_copy.start()
    for seq in range(seqs):
        for copy in seq_copies(seq):
            copy.start()
    for copy in late:
        copy.start()
    w_copy.wait()

    @pl.loop(0, seqs)
    def _(seq):
        for copy in seq_copies(seq):
            copy.wait()
        projected = projs[of_seq(seq)]
        grad_mixed = dot(grows[of_seq(seq)], w[...]).astype(BF)
        out = gproj_all.at[of_seq(seq)]
        parts = {}
        early = lax.broadcasted_iota(jnp.int32, (HALF, HALF), 0) <= lax.broadcasted_iota(jnp.int32, (HALF, HALF), 1)
        jobs = []
        for head, (qt, kt, vt, qk_lane, v_lane) in enumerate(HEAD_PLACES):
            mt = 0 if head == 2 else 1
            query = lane_keep(projected[:, qt * 128 : qt * 128 + 128], qk_lane) * BF(0.125)
            keys = projected[:, kt * 128 : kt * 128 + 128]
            values = projected[:, vt * 128 : vt * 128 + 128]
            grads = lane_keep(grad_mixed[:, mt * 128 : mt * 128 + 128], v_lane)
            parts["k", head] = [None, None]
            parts["v", head] = [None, None]
            for block in range(2):
                rows = slice(block * HALF, block * HALF + HALF)
                jobs.append((head, block, qk_lane, query[rows], keys, values, grads[rows]))

        def first_stage(job):
            head, block, _, qb, keys, values, gb = job
            last = block * HALF + HALF
            return dot_nt(keys[0:last], qb), dot_nt(values[0:last], gb)

        def last_stage(job, scores, gprobs):
            head, block, qk_lane, qb, keys, values, gb = job
            last = block * HALF + HALF
            lse = lse_ref[seq, head : head + 1, last - HALF : last]
            probs = jnp.exp(scores - lse)
            corner = jnp.where(early, probs[last - HALF :], 0.0)
            probs = jnp.concatenate([probs[: last - HALF], corner], axis=0) if block else corner
            both = probs * gprobs
            delta = jnp.sum(both, axis=0, keepdims=True)
            gscores = (both - probs * delta).astype(BF)
            gq = dot_tn(keys[0:last], gscores) * 0.125
            parts["q", head, block] = gq[qk_lane : qk_lane + HEAD_DIM]
            gk = dot(gscores, qb)
            gv = dot(probs.astype(BF), gb)
            for name, got in (("k", gk), ("v", gv)):
                held = parts[name, head]
                for b in range(block + 1):
                    part = got[b * HALF : b * HALF + HALF]
                    held[b] = part if held[b] is None else held[b] + part

        waiting = None
        for job in jobs + [None]:
            ahead = None if job is None else (job, *first_stage(job))
            if waiting is not None:
                last_stage(*waiting)
            waiting = ahead
        for block in range(2):
            rows = slice(block * HALF, block * HALF + HALF)
            pair = jnp.concatenate([parts["q", 0, block], parts["q", 1, block]], axis=0).T
            lone = parts["q", 2, block]
            lone = jnp.concatenate([lone, jnp.zeros_like(lone)], axis=0).T
            out[rows, 0:128] = pair.astype(BF)
            out[rows, 128:256] = (parts["k", 0][block] + parts["k", 1][block]).astype(BF)
            out[rows, 256:384] = (parts["v", 0][block] + parts["v", 1][block]).astype(BF)
            out[rows, 384:512] = (lone + parts["v", 2][block]).astype(BF)
            out[rows, 512:640] = parts["k", 2][block].astype(BF)
        out_copy(seq).start()

    gproj = gproj_all[...]
    sum_ref[...] = jnp.sum(gproj.astype(F32), axis=0, keepdims=True)
    for copy in late:
        copy.wait()
    grad_a = dot_tn(n1[...], gproj)
    grad_b = dot_tn(grows[...], mixed[...])
    grad = jnp.concatenate(
        [grad_a[:, 0:512], grad_a[:, 512:640] + grad_b[:, 0:128], grad_b[:, 128:256]], axis=1
    )
    if has_got:
        store_split(*grad_refs, got, (), place_ref, grad, count)
    else:
        store_all(*grad_refs, (), place_ref, grad, count)
    for seq in range(seqs):
        out_copy(seq).wait()


def attend_back_call(place, count, grows, n1, w, proj, mixed, lse, got=None):
    rows, d = grows.shape
    seqs = rows // SEQ_LEN
    shard = d // (2 * count)
    gots = () if got is None else (got,)
    both = (2 * count, shard, 768)
    grads = [both] if got is None else [(count, shard, 768)] * 2
    hbm = pl.BlockSpec(memory_space=pl.ANY)
    return pl.pallas_call(
        functools.partial(attend_back_kernel, count, len(gots)),
        grid=(1,),
        in_specs=[pl.BlockSpec(memory_space=pltpu.SMEM), whole(lse.shape)] + [hbm] * (5 + len(gots)),
        out_specs=[hbm, whole((1, 640))] + [whole(g) for g in grads],
        out_shape=[jax.ShapeDtypeStruct((rows, 640), BF), jax.ShapeDtypeStruct((1, 640), F32)]
        + [jax.ShapeDtypeStruct(g, BF) for g in grads],
        scratch_shapes=[
            pltpu.VMEM((rows, d), BF),
            pltpu.VMEM((d, 256), BF),
            pltpu.VMEM((rows, 640), BF),
            pltpu.VMEM((rows, d), BF),
            pltpu.VMEM((rows, 256), BF),
            pltpu.VMEM(both if got is not None else (8, 16, 128), BF),
            pltpu.VMEM((rows, 640), BF),
            pltpu.SemaphoreType.DMA((6, seqs)),
            pltpu.SemaphoreType.DMA((seqs,)),
        ],
        compiler_params=params("attend_back"),
        cost_estimate=cost(10e9, 12e6),
        name="attend_back",
    )(place, lse, grows, w, proj, n1, mixed, *gots)


def finish_kernel(_, x_ref, gmid_ref, table_ref, *refs):
    gproj, weights, known, sum_proj, sum_up = refs[0:4], refs[4:8], refs[8:12], refs[12:16], refs[16:20]
    out_ref, keep_ref, away_ref, gain_sum, shift_sum = refs[20:]
    start_sums(gain_sum, shift_sum)
    grad = None
    for g, w in zip(gproj, weights):
        term = dot_nt(g[...], w[...])
        grad = term if grad is None else grad + term
    unit, spread = unit_rows(x_ref[...].astype(F32))
    add_sum(gain_sum, grad * unit)
    add_sum(shift_sum, grad)
    back = norm_back(grad, unit, spread, table_ref[GAIN_ATTN])
    out_ref[...] = (gmid_ref[...] + back).astype(BF)

    @pl.when(pl.program_id(0) == pl.num_programs(0) - 1)
    def _():
        shared = jnp.concatenate(
            [r[...] for r in known] + [gain_sum[...], shift_sum[...]], axis=1
        )
        for dy in range(2):
            for dc, ref in enumerate((keep_ref, away_ref)):
                row = jnp.concatenate([shared, sum_proj[2 * dy + dc][...], sum_up[2 * dy + dc][...]], axis=1)
                ref[dy : dy + 1] = row


def finish_call(place, x, gmid, table, gproj, weights, known, sum_proj, sum_up):
    rows, d = x.shape
    tile = 256
    by_rows = pl.BlockSpec((tile, d), lambda i: (i, 0))
    width = 6 * d + sum_proj[0].shape[1] + sum_up[0].shape[1]
    return pl.pallas_call(
        finish_kernel,
        grid=(rows // tile,),
        in_specs=[pl.BlockSpec(memory_space=pltpu.SMEM), by_rows, by_rows, whole(table.shape)]
        + [pl.BlockSpec((tile, 640), lambda i: (i, 0))] * 4
        + [pl.BlockSpec((d, 640), lambda i: (0, 0))] * 4
        + [whole(v.shape) for v in (*known, *sum_proj, *sum_up)],
        out_specs=[by_rows, whole((2, width)), whole((2, width))],
        out_shape=[jax.ShapeDtypeStruct((rows, d), BF)] + [jax.ShapeDtypeStruct((2, width), F32)] * 2,
        scratch_shapes=[pltpu.VMEM((1, d), F32)] * 2,
        compiler_params=params("finish"),
        cost_estimate=cost(2 * 4 * rows * d * 640, 16e6),
        name="finish",
    )(place, x, gmid, table, *gproj, *weights, *known, *sum_proj, *sum_up)


class Links:
    def __init__(self, mesh):
        self.count = mesh.shape["fsdp"] // 2
        places = [
            (z, x, y, c)
            for z in range(self.count)
            for x in range(2)
            for y in range(2)
            for c in range(2)
        ]

        def index(z, x, y, c):
            return ((z * 2 + x) * 2 + y) * 2 + c

        def pairs(move):
            return [(index(*p), index(*move(*p))) for p in places]

        self.core = pairs(lambda z, x, y, c: (z, x, y, 1 - c))
        self.y = pairs(lambda z, x, y, c: (z, x, 1 - y, c))
        self.x = pairs(lambda z, x, y, c: (z, 1 - x, y, c))
        self.ring = pairs(lambda z, x, y, c: ((z + 1) % self.count, x, y, c))
        self.far = [
            pairs(lambda z, x, y, c, k=k: ((z + k) % self.count, x, y, c)) for k in range(self.count)
        ]
        self.back = [
            pairs(lambda z, x, y, c, k=k: ((z - k) % self.count, x, y, c)) for k in range(self.count)
        ]
        self.xy = pairs(lambda z, x, y, c: (z, 1 - x, 1 - y, c))
        self.trees = []
        step = 1
        while step < self.count:
            size = 4 if step * 4 <= self.count else 2
            self.trees.append(
                [pairs(lambda z, x, y, c, b=step * k: (z ^ b, x, y, c)) for k in range(1, size)]
            )
            step *= size

    @staticmethod
    def send(value, pairs):
        return lax.ppermute(value, AXES, pairs)


def plus(*terms, kind=BF):
    total = terms[0].astype(F32)
    for term in terms[1:]:
        total = total + term.astype(F32)
    return total.astype(kind)


def tie(value, *others):
    return lax.optimization_barrier((value, others))[0]


def ring_from(links, first):
    held = [first]
    for _ in range(links.count - 1):
        held.append(links.send(held[-1], links.ring))
    return held


def gather_and_attend(links, place, attn, up, down, n1, smalls, layer_input, table):
    n = links.count
    half = n // 2
    small_y = links.send(smalls, links.y)

    near = [jnp.stack([attn, down])]
    done = (n1,)
    for k in range(1, n):
        now = near[-1] if k == 1 else tie(near[-1], *done)
        near.append(links.send(now, links.ring))
        if k == 3:
            steps.append(links.send(tie(steps[0], near[2]), links.ring))
        done = (near[-1],)
        if k == 1:
            pair = jnp.stack([up, links.send(up, links.x)])
            done += (pair, n1, smalls)
        if k == 2:
            steps = [jnp.stack([pair, links.send(tie(pair, near[1]), links.y)])]
            done += (steps[0], small_y)
        if k == half:
            lines = [jnp.stack([v[0] for v in near[:half]])]
            others = [links.send(lines[0], links.x)]
            done += (others[0],)
        if k == half + 1:
            quads = [links.send(tie(jnp.stack([lines[0], others[0]]), *near[half:-1]), links.y)]
            smalls = [smalls, links.send(smalls, links.core), small_y, links.send(small_y, links.core)]
            done += (smalls[1], smalls[3], quads[0])

    lines.append(tie(jnp.stack([v[0] for v in near[half:]]), *done))
    others.append(links.send(lines[1], links.x))
    line = jnp.stack([v[1] for v in near])
    beyond = [links.send(tie(line, *done), links.y)]
    steps.append(links.send(tie(steps[-1], *done), links.ring))
    core = lambda values: [links.send(v, links.core) for v in values]

    def from_lines(*pair):
        return [(v[k // half], (k % half,)) for v in pair for k in range(n)]

    def from_quads(quads):
        return [(quads[k // half], (dx, k % half)) for dx in range(2) for k in range(n)]

    quads.append(links.send(jnp.stack([lines[1], others[1]]), links.y))
    far = links.send(tie(line, others[1]), links.x)

    attn_w, proj, mixed, lse = [], [], [], []

    def attend(pieces, *before):
        j = len(proj)
        w, p, m, s = attend_call(tie(place, *before) if before else place, n1, pieces, smalls[j])
        attn_w.append(w)
        proj.append(p)
        mixed.append(m)
        lse.append(s)

    attend(from_lines(lines, others))
    attend(from_lines(core(lines), core(others)), mixed[0])
    quads_core = core([quads[0], tie(quads[1], mixed[1])])
    beyond.append(links.send(tie(beyond[0], far), links.x))
    for _ in range(3, n):
        steps.append(links.send(tie(steps[-1], mixed[1]), links.ring))
    attend(from_quads(quads), mixed[1], quads[1], far, steps[2])
    attend(from_quads(quads_core), mixed[2])
    middle, n2 = middle_call(layer_input, table, mixed, attn_w)

    steps[-1] = tie(steps[-1], mixed[3])
    up_core = core(steps)
    up_w = [[(v, (dy, dx)) for dx in range(2) for v in vs] for dy in range(2) for vs in (steps, up_core)]
    down_w = [
        [(v, (k,)) for v in vs for k in range(n)]
        for pair in ((line, far), beyond)
        for vs in (pair, core(pair))
    ]
    return attn_w, up_w, down_w, proj, mixed, lse, smalls, middle, n2


def spread_sum(links, home):
    got = [links.send(home[k], links.far[k]) for k in range(1, links.count)]
    return plus(home[0], *got, kind=F32)


def sum_near(links, keep, away):
    rows = keep + links.send(away, links.core)
    near, far = rows[0:1], rows[1:2]
    return (near + links.send(near, links.x)) + (
        links.send(far, links.y) + links.send(far, links.xy)
    )


def sum_far(links, total):
    for pairs in links.trees:
        got = [total] + [links.send(total, p) for p in pairs]
        while len(got) > 1:
            got = [got[i] + got[i + 1] for i in range(0, len(got), 2)]
        total = got[0]
    return total


def pack_attn(w_qkv, w_out):
    q, k, v, o = w_qkv[:, 0], w_qkv[:, 1], w_qkv[:, 2], w_out.T
    return jnp.concatenate(
        [q[:, :128], k[:, :128], v[:, :128], q[:, 128:], v[:, 128:], k[:, 128:], o[:, 128:], o[:, :128]],
        axis=1,
    )


def unpack_attn(g):
    q = jnp.concatenate([g[:, 0:128], g[:, 384:448]], axis=1)
    k = jnp.concatenate([g[:, 128:256], g[:, 512:576]], axis=1)
    v = jnp.concatenate([g[:, 256:384], g[:, 448:512]], axis=1)
    o = jnp.concatenate([g[:, 640:768], g[:, 576:640]], axis=1)
    return jnp.stack([q, k, v], axis=1), o.T


def body(
    links,
    layer_input,
    w_qkv,
    bias_qv,
    w_out,
    bias_out,
    gain_attn,
    shift_attn,
    gain_mlp,
    shift_mlp,
    w_up,
    bias_up,
    w_down,
    bias_down,
    cotangent,
):
    fsdp = lax.axis_index("fsdp")
    place = jnp.stack([fsdp // 2, fsdp % 2]).astype(jnp.int32)
    count = links.count
    n1, sum_down, small, table = start_call(
        layer_input,
        cotangent,
        bias_qv,
        bias_up,
        (bias_out, gain_attn, shift_attn, gain_mlp, shift_mlp, bias_down),
    )
    attn_w, up_w, down_w, proj, mixed, lse, smalls, middle, n2 = gather_and_attend(
        links, place, pack_attn(w_qkv, w_out), w_up, w_down.T, n1, small, layer_input, table
    )

    hidden, pre, sum_up = [None] * 4, [None] * 4, [None] * 4
    up_home, up_away, down_sum = [None] * 2, [None] * 2, [None] * 2
    gots = [None] * 4
    for j in (1, 3, 0, 2):
        out = feed_call(
            place, count, n2, cotangent, up_w[j], down_w[j], smalls[j], gots[j]
        )
        hidden[j], pre[j], sum_up[j], up_w[j], down_w[j] = out[0:5]
        if j % 2:
            gots[j - 1] = links.send(out[5], links.core)
        else:
            up_home[j // 2], up_away[j // 2], down_sum[j // 2] = out[5:8]

    got_x0 = links.send(up_away[0], links.x)
    got_x1 = links.send(up_away[1], links.x)
    got_down = links.send(down_sum[1], links.y)
    gmid, grows, gain_two, shift_two, sum_out = turn_call(
        place, middle, cotangent, table, pre, up_w
    )

    gproj, sum_proj = [None] * 4, [None] * 4
    attn_home, attn_away = [None] * 2, [None] * 2

    def back(j, got, *before):
        out = attend_back_call(
            tie(place, *before) if before else place,
            count,
            grows,
            n1,
            attn_w[j],
            proj[j],
            mixed[j],
            lse[j],
            got,
        )
        gproj[j], sum_proj[j] = out[0:2]
        if j % 2:
            return links.send(out[2], links.core)
        attn_home[j // 2], attn_away[j // 2] = out[2:4]

    got_three = back(3, None, got_x0)
    up_beyond = plus(up_home[1], got_x1)
    got_up = links.send(up_beyond, links.y)
    got_one = back(1, None, up_beyond)
    down_away = plus(down_sum[0][count:], got_down[count:])
    got_x = links.send(down_away, links.x)
    back(2, got_three, down_away)
    got_a1 = links.send(attn_away[1], links.x)
    up_all = plus(up_home[0], got_x0, got_up)
    down_all = plus(down_sum[0][:count], got_down[:count], got_x)
    back(0, got_one, up_all, down_all, sum_proj[2])
    grad_up = spread_sum(links, up_all)
    grad_down = spread_sum(links, down_all)
    got_a0 = links.send(attn_away[0], links.x)
    attn_beyond = plus(attn_home[1], got_a1)
    got_attn = links.send(attn_beyond, links.y)
    grad_input, keep, away = finish_call(
        tie(place, attn_beyond, grad_up),
        layer_input,
        gmid,
        table,
        gproj,
        attn_w,
        (sum_out, sum_down, gain_two, shift_two),
        sum_proj,
        sum_up,
    )
    attn_all = plus(tie(attn_home[0], keep), got_a0, got_attn)
    parts = [attn_all[0]] + [links.send(attn_all[k], links.far[k]) for k in range(1, count)]
    total = sum_near(links, keep, tie(away, attn_all))
    before = (total, attn_all, grad_up, grad_down)
    layer_output = output_call(tie(place, *before), middle, table, hidden, down_w)
    sums = sum_far(links, tie(total, layer_output, parts[1]))
    grad_attn = plus(*parts, kind=F32)

    d = layer_input.shape[1]
    heads = bias_qv.shape[1]
    vec = sums[0]
    total_out, total_down, gain_two, shift_two, gain_one, shift_one = (
        vec[i * d : (i + 1) * d] for i in range(6)
    )
    own = vec[6 * d :]
    total_qv = jnp.stack(
        [
            jnp.concatenate([own[0:128], own[384:448]]),
            jnp.concatenate([own[256:384], own[448:512]]),
        ]
    )
    total_up = own[640:]

    shard_qkv, shard_out = unpack_attn(grad_attn)
    return (
        layer_output,
        grad_input,
        shard_qkv,
        total_qv,
        shard_out,
        total_out,
        gain_one,
        shift_one,
        gain_two,
        shift_two,
        grad_up,
        total_up,
        grad_down.T,
        total_down,
    )


def solution(mesh):
    tokens = P(("fsdp", "tp"), None)
    placed = (
        tokens,
        P("fsdp", None, "tp"),
        P(None, "tp"),
        P("tp", "fsdp"),
        P(),
        P(),
        P(),
        P(),
        P(),
        P("fsdp", "tp"),
        P("tp"),
        P("tp", "fsdp"),
        P(),
        tokens,
    )
    return jax.shard_map(
        functools.partial(body, Links(mesh)),
        mesh=mesh,
        in_specs=placed,
        out_specs=(
            tokens,
            tokens,
            P("fsdp", None, "tp"),
            P(None, "tp"),
            P("tp", "fsdp"),
            P(),
            P(),
            P(),
            P(),
            P(),
            P("fsdp", "tp"),
            P("tp"),
            P("tp", "fsdp"),
            P(),
        ),
        check_vma=False,
    )
```

```python
import functools

import jax
import jax.numpy as jnp
from jax import lax
from jax.experimental import pallas as pl
from jax.experimental.pallas import tpu as pltpu
from jax.sharding import PartitionSpec as P

HEAD_DIM = 64
SEQ_LEN = 512
HALF = 256
EPS = 1e-05
AXES = ("fsdp", "tp")
BF = jnp.bfloat16
F32 = jnp.float32
MB = 1 << 20
SHARE = 0.32
BIAS_OUT, GAIN_ATTN, SHIFT_ATTN, GAIN_MLP, SHIFT_MLP, BIAS_DOWN = (slice(i, i + 1) for i in range(6))
VMEM_MB = {"start": 60, "feed": 60, "attend_back": 60, "turn": 60, "finish": 60, "output": 60}
SMALL_ATTN = 768


def dot(left, right):
    return lax.dot_general(left, right, (((1,), (0,)), ((), ())), preferred_element_type=F32)


def dot_nt(left, right):
    return lax.dot_general(left, right, (((1,), (1,)), ((), ())), preferred_element_type=F32)


def dot_tn(left, right):
    return lax.dot_general(left, right, (((0,), (0,)), ((), ())), preferred_element_type=F32)


def whole(shape):
    zeros = (0,) * len(shape)
    return pl.BlockSpec(shape, lambda *_: zeros)


def params(kernel):
    return pltpu.CompilerParams(vmem_limit_bytes=VMEM_MB.get(kernel, 36) * MB)


def cost(flops, nbytes, trans=0):
    return pl.CostEstimate(
        flops=int(flops * SHARE), bytes_accessed=int(nbytes * SHARE), transcendentals=int(trans * SHARE)
    )


def unit_rows(rows):
    centre = rows - jnp.mean(rows, axis=-1, keepdims=True)
    spread = lax.rsqrt(jnp.mean(centre * centre, axis=-1, keepdims=True) + EPS)
    return centre * spread, spread


def norm_back(grad_out, unit, spread, gain):
    scaled = grad_out * gain
    inner = jnp.mean(scaled * unit, axis=-1, keepdims=True)
    return spread * (scaled - jnp.mean(scaled, axis=-1, keepdims=True) - unit * inner)


def start_sums(*refs):
    @pl.when(pl.program_id(0) == 0)
    def _():
        for ref in refs:
            ref[...] = jnp.zeros_like(ref)


def add_sum(ref, value):
    ref[...] += jnp.sum(value, axis=0, keepdims=True)


def start_kernel(x_ref, cot_ref, qv_ref, up_ref, *refs):
    vectors, (n1_ref, sum_ref, small_ref, table_ref) = refs[:6], refs[6:]
    start_sums(sum_ref)

    @pl.when(pl.program_id(0) == 0)
    def _():
        for i, ref in enumerate(vectors):
            table_ref[i : i + 1] = ref[...].astype(F32).reshape(1, -1)
        small_ref[...] = jnp.zeros_like(small_ref)
        for c in range(2):
            pair, lone = (0, 384) if c == 0 else (256, 448)
            row = qv_ref[c : c + 1].astype(F32)
            small_ref[:, pair : pair + 128] = row[:, 0:128]
            small_ref[:, lone : lone + HEAD_DIM] = row[:, 128:192]
        small_ref[:, SMALL_ATTN:] = up_ref[...].astype(F32).reshape(1, -1)

    unit, _ = unit_rows(x_ref[...].astype(F32))
    normed = unit * table_ref[GAIN_ATTN] + table_ref[SHIFT_ATTN]
    n1_ref[...] = normed.astype(BF)
    add_sum(sum_ref, cot_ref[...].astype(F32))


def start_call(x, cot, bias_qv, bias_up, vectors):
    rows, d = x.shape
    units = bias_up.shape[0]
    tile = 256
    by_rows = pl.BlockSpec((tile, d), lambda i: (i, 0))
    return pl.pallas_call(
        start_kernel,
        grid=(rows // tile,),
        in_specs=[by_rows, by_rows, whole(bias_qv.shape), whole(bias_up.shape)]
        + [whole(v.shape) for v in vectors],
        out_specs=[by_rows]
        + [whole((1, d)), whole((1, SMALL_ATTN + units)), whole((8, d))],
        out_shape=[
            jax.ShapeDtypeStruct((rows, d), BF),
            jax.ShapeDtypeStruct((1, d), F32),
            jax.ShapeDtypeStruct((1, SMALL_ATTN + units), F32),
            jax.ShapeDtypeStruct((8, d), F32),
        ],
        compiler_params=params("start"),
        cost_estimate=cost(0, 10 * rows * d),
        name="start",
    )(x, cot, bias_qv, bias_up, *vectors)


def piece_specs(pieces, cols, index):
    rows = pieces[0][0].shape[-2]
    return [
        pl.BlockSpec((1,) * len(lead) + (rows, cols), lambda i, lead=lead: lead + (0, index(i)))
        for _, lead in pieces
    ]


def place_pieces(place_ref, pieces, out_ref):
    count = len(pieces) // 2
    z, x = place_ref[0], place_ref[1]
    for k in range(count):
        for dx in range(2):
            piece = pieces[dx * count + k]
            size, cols = piece.shape[-2:]
            slot = lax.rem(z - k + count, count) * 2 + lax.rem(x + dx, 2)
            out_ref[pl.ds(pl.multiple_of(slot * size, size), size)] = piece[...].reshape(size, cols)


HEAD_PLACES = ((0, 1, 2, 0, 0), (0, 1, 2, 64, 64), (3, 4, 3, 0, 64))


def lane_keep(tile, first):
    lanes = lax.broadcasted_iota(jnp.int32, tile.shape, 1)
    keep = (lanes >= first) & (lanes < first + HEAD_DIM)
    return jnp.where(keep, tile, jnp.zeros_like(tile))


def attend_kernel(place_ref, n1_ref, bias_ref, *refs):
    pieces, (w_ref, proj_ref, mixed_ref, lse_ref) = refs[:-4], refs[-4:]

    @pl.when(pl.program_id(0) == 0)
    def _():
        place_pieces(place_ref, pieces, w_ref)

    projected = (dot(n1_ref[...], w_ref[:, 0:640]) + bias_ref[...].astype(F32)).astype(BF)
    proj_ref[...] = projected
    lse_ref[...] = jnp.zeros_like(lse_ref)
    outs = {}
    early = lax.broadcasted_iota(jnp.int32, (HALF, HALF), 0) <= lax.broadcasted_iota(jnp.int32, (HALF, HALF), 1)
    jobs = []
    for head, (qt, kt, vt, qk_lane, v_lane) in enumerate(HEAD_PLACES):
        query = lane_keep(projected[:, qt * 128 : qt * 128 + 128], qk_lane) * BF(0.125)
        keys = projected[:, kt * 128 : kt * 128 + 128]
        values = projected[:, vt * 128 : vt * 128 + 128]
        for block in range(2):
            first, last = block * HALF, block * HALF + HALF
            jobs.append((head, first, last, query[first:last], keys[0:last], values[0:last], v_lane))

    def last_stage(job, scores):
        head, first, last, _, _, values, v_lane = job
        corner = jnp.where(early, scores[first:], -1e30)
        scores = jnp.concatenate([scores[:first], corner], axis=0) if first else corner
        top = jnp.max(scores, axis=0, keepdims=True)
        weight = jnp.exp(scores - top)
        total = jnp.sum(weight, axis=0, keepdims=True)
        mixed = dot_tn(values, weight.astype(BF)) * (1.0 / total)
        outs[head, first // HALF] = mixed[v_lane : v_lane + HEAD_DIM]
        lse_ref[0, head : head + 1, first:last] = top + jnp.log(total)

    waiting = None
    for job in jobs + [None]:
        ahead = None if job is None else (job, dot_nt(job[4], job[3]))
        if waiting is not None:
            last_stage(*waiting)
        waiting = ahead
    for block in range(2):
        first = block * HALF
        rows = slice(first, first + HALF)
        single = jnp.concatenate([jnp.zeros_like(outs[2, block]), outs[2, block]], axis=0)
        pair = jnp.concatenate([outs[0, block], outs[1, block]], axis=0)
        mixed_ref[rows, 0:128] = single.T.astype(BF)
        mixed_ref[rows, 128:256] = pair.T.astype(BF)


def attend_call(place, n1, pieces, bias):
    rows, d = n1.shape
    seqs = rows // SEQ_LEN
    return pl.pallas_call(
        attend_kernel,
        grid=(seqs,),
        in_specs=[
            pl.BlockSpec(memory_space=pltpu.SMEM),
            pl.BlockSpec((SEQ_LEN, d), lambda i: (i, 0)),
            pl.BlockSpec((1, 640), lambda i: (0, 0)),
        ]
        + piece_specs(pieces, 768, lambda i: 0),
        out_specs=[
            whole((d, 768)),
            pl.BlockSpec((SEQ_LEN, 640), lambda i: (i, 0)),
            pl.BlockSpec((SEQ_LEN, 256), lambda i: (i, 0)),
            pl.BlockSpec((1, 8, SEQ_LEN), lambda i: (i, 0, 0)),
        ],
        out_shape=[
            jax.ShapeDtypeStruct((d, 768), BF),
            pltpu.HBM((rows, 640), BF),
            jax.ShapeDtypeStruct((rows, 256), BF),
            pltpu.HBM((seqs, 8, SEQ_LEN), F32),
        ],
        compiler_params=params("attend"),
        cost_estimate=cost(6e9, 8e6),
        name="attend",
    )(place, n1, bias, *[array for array, _ in pieces])


def middle_kernel(x_ref, table_ref, *refs):
    mixed, weights, (mid_ref, n2_ref) = refs[0:4], refs[4:8], refs[8:]
    attended = table_ref[BIAS_OUT]
    for m, w in zip(mixed, weights):
        attended = attended + dot_nt(m[...], w[...])
    middle = x_ref[...].astype(F32) + attended
    mid_ref[...] = middle
    unit, _ = unit_rows(middle)
    normed = unit * table_ref[GAIN_MLP] + table_ref[SHIFT_MLP]
    n2_ref[...] = normed.astype(BF)


def middle_call(x, table, mixed, weights):
    rows, d = x.shape
    tile = 256
    by_rows = pl.BlockSpec((tile, d), lambda i: (i, 0))
    return pl.pallas_call(
        middle_kernel,
        grid=(rows // tile,),
        in_specs=[by_rows, whole(table.shape)]
        + [pl.BlockSpec((tile, 256), lambda i: (i, 0))] * 4
        + [pl.BlockSpec((d, 256), lambda i: (0, 2))] * 4,
        out_specs=[by_rows, by_rows],
        out_shape=[pltpu.HBM((rows, d), F32), pltpu.HBM((rows, d), BF)],
        compiler_params=params("middle"),
        cost_estimate=cost(2 * rows * d * 1024, 16e6),
        name="middle",
    )(x, table, *mixed, *weights)


def gelu_both(value):
    cumulative = 0.5 + 0.5 * lax.erf(value * 2.0**-0.5)
    bell = jnp.exp(-0.5 * value * value)
    return value * cumulative, cumulative + value * bell * (2.0 * 3.141592653589793) ** -0.5


def store_all(ref, lead, place_ref, value, count, got_ref=None, got_lead=()):
    z, x = place_ref[0], place_ref[1]
    size = value.shape[0] // (2 * count)
    for block in range(2 * count):
        slot = lax.rem(x + block % 2, 2) * count + lax.rem(block // 2 - z + count, count)
        part = value[block * size : (block + 1) * size]
        if got_ref is not None:
            part = part + got_ref[got_lead + (slot,)].astype(F32)
        ref[lead + (slot,)] = part.astype(BF)


def store_split(home_ref, away_ref, got_ref, lead, place_ref, value, count):
    z, x = place_ref[0], place_ref[1]
    size = value.shape[0] // (2 * count)
    for pair in range(count):
        slot = lax.rem(pair - z + count, count)
        first = value[2 * pair * size : (2 * pair + 1) * size]
        second = value[(2 * pair + 1) * size : (2 * pair + 2) * size]
        home = jnp.where(x == 0, first, second) + got_ref[lead + (slot,)].astype(F32)
        away = jnp.where(x == 0, second, first) + got_ref[lead + (count + slot,)].astype(F32)
        home_ref[slot] = home.astype(BF)
        away_ref[slot] = away.astype(BF)


def feed_kernel(count, tokens, has_got, place_ref, n2_ref, cot_ref, bias_ref, *refs):
    ups, downs, refs = refs[: 2 * count], refs[2 * count : 4 * count], refs[4 * count :]
    got_ref = refs[0] if has_got else None
    hidden_ref, pre_ref, sum_ref, up_ref, down_ref, *outs = refs[has_got:]
    place_pieces(place_ref, ups, up_ref)
    place_pieces(place_ref, downs, down_ref)
    rows = n2_ref.shape[0]
    up, down, bias = up_ref[...], down_ref[...], bias_ref[...].astype(F32)
    total = jnp.zeros_like(bias)
    for first in range(0, rows, tokens):
        here = slice(first, first + tokens)
        pre = dot(n2_ref[here], up) + bias
        grad_hidden = dot(cot_ref[here], down)
        hidden, slope = gelu_both(pre)
        hidden_ref[here] = hidden.astype(BF)
        grad_pre = (grad_hidden * slope).astype(BF)
        pre_ref[here] = grad_pre
        total = total + jnp.sum(grad_pre.astype(F32), axis=0, keepdims=True)
    sum_ref[...] = total
    grads = (dot_tn(n2_ref[...], pre_ref[...]), dot_tn(cot_ref[...], hidden_ref[...]))
    if has_got:
        store_split(outs[0], outs[1], got_ref, (0,), place_ref, grads[0], count)
        store_all(outs[2], (), place_ref, grads[1], count, got_ref, (1,))
    else:
        store_all(outs[0], (0,), place_ref, grads[0], count)
        store_all(outs[0], (1,), place_ref, grads[1], count)


def feed_call(place, count, n2, cot, ups, downs, small, got=None):
    rows, d = n2.shape
    units = ups[0][0].shape[-1]
    tile = 256
    shard = d // (2 * count)
    cols = lambda n: pl.BlockSpec((n, tile), lambda i: (0, i))
    hid = jax.ShapeDtypeStruct((rows, units), BF)
    both_spec = pl.BlockSpec((2, 2 * count, shard, tile), lambda i: (0, 0, 0, i))
    if got is None:
        grad_specs = [both_spec]
        grads = [jax.ShapeDtypeStruct((2, 2 * count, shard, units), BF)]
    else:
        grad_specs = [pl.BlockSpec((n, shard, tile), lambda i: (0, 0, i)) for n in (count, count, 2 * count)]
        grads = [jax.ShapeDtypeStruct((n, shard, units), BF) for n in (count, count, 2 * count)]
    gots = () if got is None else (got,)
    return pl.pallas_call(
        functools.partial(feed_kernel, count, 512, len(gots)),
        grid=(units // tile,),
        in_specs=[
            pl.BlockSpec(memory_space=pltpu.SMEM),
            whole((rows, d)),
            whole((rows, d)),
            pl.BlockSpec((1, tile), lambda i: (0, SMALL_ATTN // tile + i)),
        ]
        + piece_specs(ups, tile, lambda i: i)
        + piece_specs(downs, tile, lambda i: i)
        + [both_spec] * len(gots),
        out_specs=[cols(rows)] * 2 + [cols(1)] + [cols(d)] * 2 + grad_specs,
        out_shape=[hid] * 2
        + [jax.ShapeDtypeStruct((1, units), F32)]
        + [jax.ShapeDtypeStruct((d, units), BF)] * 2
        + grads,
        compiler_params=params("feed"),
        cost_estimate=cost(2 * 4 * rows * d * units, 16e6, rows * units),
        name="feed",
    )(place, n2, cot, small, *[a for a, _ in ups], *[a for a, _ in downs], *gots)


def turn_kernel(_, mid_ref, cot_ref, table_ref, *refs):
    pre, ups = refs[0:4], refs[4:8]
    gmid_ref, grows_ref, gain_sum, shift_sum, bias_sum = refs[-5:]
    start_sums(gain_sum, shift_sum, bias_sum)
    grad = None
    for g, w in zip(pre, ups):
        term = dot_nt(g[...], w[...])
        grad = term if grad is None else grad + term
    unit, spread = unit_rows(mid_ref[...])
    add_sum(gain_sum, grad * unit)
    add_sum(shift_sum, grad)
    back = norm_back(grad, unit, spread, table_ref[GAIN_MLP])
    grad_middle = cot_ref[...].astype(F32) + back
    gmid_ref[...] = grad_middle
    rows = grad_middle.astype(BF)
    grows_ref[...] = rows
    add_sum(bias_sum, rows.astype(F32))


def turn_call(place, middle, cot, table, pre, ups):
    rows, d = middle.shape
    units = ups[0].shape[1]
    tile = 256
    by_rows = pl.BlockSpec((tile, d), lambda i: (i, 0))
    kept = pl.BlockSpec((d, units), lambda i: (0, 0), pipeline_mode=pl.Buffered(1))
    total = jax.ShapeDtypeStruct((1, d), F32)
    return pl.pallas_call(
        turn_kernel,
        grid=(rows // tile,),
        in_specs=[pl.BlockSpec(memory_space=pltpu.SMEM), by_rows, by_rows, whole(table.shape)]
        + [pl.BlockSpec((tile, units), lambda i: (i, 0))] * 4
        + [kept] * 4,
        out_specs=[by_rows] * 2 + [whole((1, d))] * 3,
        out_shape=[
            jax.ShapeDtypeStruct((rows, d), F32),
            jax.ShapeDtypeStruct((rows, d), BF),
            total,
            total,
            total,
        ],
        compiler_params=params("turn"),
        cost_estimate=cost(2 * 4 * rows * d * units, 20e6),
        name="turn",
    )(place, middle, cot, table, *pre, *ups)


def output_kernel(_, mid_ref, table_ref, *refs):
    hidden, downs, out_ref = refs[0:4], refs[4:8], refs[-1]
    mlp = table_ref[BIAS_DOWN]
    for h, w in zip(hidden, downs):
        mlp = mlp + dot_nt(h[...], w[...])
    out_ref[...] = (mid_ref[...] + mlp).astype(BF)


def output_call(place, middle, table, hidden, downs):
    rows, d = middle.shape
    units = downs[0].shape[1]
    tile = 256
    by_rows = pl.BlockSpec((tile, d), lambda i: (i, 0))
    kept = pl.BlockSpec((d, units), lambda i: (0, 0), pipeline_mode=pl.Buffered(1))
    return pl.pallas_call(
        output_kernel,
        grid=(rows // tile,),
        in_specs=[pl.BlockSpec(memory_space=pltpu.SMEM), by_rows, whole(table.shape)]
        + [pl.BlockSpec((tile, units), lambda i: (i, 0))] * 4
        + [kept] * 4,
        out_specs=by_rows,
        out_shape=jax.ShapeDtypeStruct((rows, d), BF),
        compiler_params=params("output"),
        cost_estimate=cost(2 * 4 * rows * d * units, 16e6),
        name="output",
    )(place, middle, table, *hidden, *downs)


def attend_back_kernel(count, has_got, place_ref, lse_ref, grows_hbm, w_hbm, proj_hbm, n1_hbm, mixed_hbm, *refs):
    got_hbm = refs[0] if has_got else None
    gproj_hbm, sum_ref, *grad_refs = refs[has_got : has_got + 3 + has_got]
    grows, w, projs, n1, mixed, got, gproj_all, sems, out_sems = refs[has_got + 3 + has_got :]
    seqs = lse_ref.shape[0]

    def of_seq(seq):
        return pl.ds(pl.multiple_of(seq * SEQ_LEN, SEQ_LEN), SEQ_LEN)

    def seq_copies(seq):
        return [
            pltpu.make_async_copy(hbm.at[of_seq(seq)], ref.at[of_seq(seq)], sems.at[i, seq])
            for i, (hbm, ref) in enumerate(((grows_hbm, grows), (proj_hbm, projs)))
        ]

    def out_copy(seq):
        return pltpu.make_async_copy(gproj_all.at[of_seq(seq)], gproj_hbm.at[of_seq(seq)], out_sems.at[seq])

    w_copy = pltpu.make_async_copy(w_hbm.at[:, 512:768], w, sems.at[2, 0])
    late = [
        pltpu.make_async_copy(n1_hbm, n1, sems.at[3, 0]),
        pltpu.make_async_copy(mixed_hbm, mixed, sems.at[4, 0]),
    ]
    if has_got:
        late.append(pltpu.make_async_copy(got_hbm, got, sems.at[5, 0]))
    w_copy.start()
    for seq in range(seqs):
        for copy in seq_copies(seq):
            copy.start()
    for copy in late:
        copy.start()
    w_copy.wait()

    @pl.loop(0, seqs)
    def _(seq):
        for copy in seq_copies(seq):
            copy.wait()
        projected = projs[of_seq(seq)]
        grad_mixed = dot(grows[of_seq(seq)], w[...]).astype(BF)
        out = gproj_all.at[of_seq(seq)]
        parts = {}
        early = lax.broadcasted_iota(jnp.int32, (HALF, HALF), 0) <= lax.broadcasted_iota(jnp.int32, (HALF, HALF), 1)
        jobs = []
        for head, (qt, kt, vt, qk_lane, v_lane) in enumerate(HEAD_PLACES):
            mt = 0 if head == 2 else 1
            query = lane_keep(projected[:, qt * 128 : qt * 128 + 128], qk_lane) * BF(0.125)
            keys = projected[:, kt * 128 : kt * 128 + 128]
            values = projected[:, vt * 128 : vt * 128 + 128]
            grads = lane_keep(grad_mixed[:, mt * 128 : mt * 128 + 128], v_lane)
            parts["k", head] = [None, None]
            parts["v", head] = [None, None]
            for block in range(2):
                rows = slice(block * HALF, block * HALF + HALF)
                jobs.append((head, block, qk_lane, query[rows], keys, values, grads[rows]))

        def first_stage(job):
            head, block, _, qb, keys, values, gb = job
            last = block * HALF + HALF
            return dot_nt(keys[0:last], qb), dot_nt(values[0:last], gb)

        def last_stage(job, scores, gprobs):
            head, block, qk_lane, qb, keys, values, gb = job
            last = block * HALF + HALF
            lse = lse_ref[seq, head : head + 1, last - HALF : last]
            probs = jnp.exp(scores - lse)
            corner = jnp.where(early, probs[last - HALF :], 0.0)
            probs = jnp.concatenate([probs[: last - HALF], corner], axis=0) if block else corner
            both = probs * gprobs
            delta = jnp.sum(both, axis=0, keepdims=True)
            gscores = (both - probs * delta).astype(BF)
            gq = dot_tn(keys[0:last], gscores) * 0.125
            parts["q", head, block] = gq[qk_lane : qk_lane + HEAD_DIM]
            gk = dot(gscores, qb)
            gv = dot(probs.astype(BF), gb)
            for name, got in (("k", gk), ("v", gv)):
                held = parts[name, head]
                for b in range(block + 1):
                    part = got[b * HALF : b * HALF + HALF]
                    held[b] = part if held[b] is None else held[b] + part

        waiting = None
        for job in jobs + [None]:
            ahead = None if job is None else (job, *first_stage(job))
            if waiting is not None:
                last_stage(*waiting)
            waiting = ahead
        for block in range(2):
            rows = slice(block * HALF, block * HALF + HALF)
            pair = jnp.concatenate([parts["q", 0, block], parts["q", 1, block]], axis=0).T
            lone = parts["q", 2, block]
            lone = jnp.concatenate([lone, jnp.zeros_like(lone)], axis=0).T
            out[rows, 0:128] = pair.astype(BF)
            out[rows, 128:256] = (parts["k", 0][block] + parts["k", 1][block]).astype(BF)
            out[rows, 256:384] = (parts["v", 0][block] + parts["v", 1][block]).astype(BF)
            out[rows, 384:512] = (lone + parts["v", 2][block]).astype(BF)
            out[rows, 512:640] = parts["k", 2][block].astype(BF)
        out_copy(seq).start()

    gproj = gproj_all[...]
    sum_ref[...] = jnp.sum(gproj.astype(F32), axis=0, keepdims=True)
    for copy in late:
        copy.wait()
    grad_a = dot_tn(n1[...], gproj)
    grad_b = dot_tn(grows[...], mixed[...])
    grad = jnp.concatenate(
        [grad_a[:, 0:512], grad_a[:, 512:640] + grad_b[:, 0:128], grad_b[:, 128:256]], axis=1
    )
    if has_got:
        store_split(*grad_refs, got, (), place_ref, grad, count)
    else:
        store_all(*grad_refs, (), place_ref, grad, count)
    for seq in range(seqs):
        out_copy(seq).wait()


def attend_back_call(place, count, grows, n1, w, proj, mixed, lse, got=None):
    rows, d = grows.shape
    seqs = rows // SEQ_LEN
    shard = d // (2 * count)
    gots = () if got is None else (got,)
    both = (2 * count, shard, 768)
    grads = [both] if got is None else [(count, shard, 768)] * 2
    hbm = pl.BlockSpec(memory_space=pl.ANY)
    return pl.pallas_call(
        functools.partial(attend_back_kernel, count, len(gots)),
        grid=(1,),
        in_specs=[pl.BlockSpec(memory_space=pltpu.SMEM), whole(lse.shape)] + [hbm] * (5 + len(gots)),
        out_specs=[hbm, whole((1, 640))] + [whole(g) for g in grads],
        out_shape=[jax.ShapeDtypeStruct((rows, 640), BF), jax.ShapeDtypeStruct((1, 640), F32)]
        + [jax.ShapeDtypeStruct(g, BF) for g in grads],
        scratch_shapes=[
            pltpu.VMEM((rows, d), BF),
            pltpu.VMEM((d, 256), BF),
            pltpu.VMEM((rows, 640), BF),
            pltpu.VMEM((rows, d), BF),
            pltpu.VMEM((rows, 256), BF),
            pltpu.VMEM(both if got is not None else (8, 16, 128), BF),
            pltpu.VMEM((rows, 640), BF),
            pltpu.SemaphoreType.DMA((6, seqs)),
            pltpu.SemaphoreType.DMA((seqs,)),
        ],
        compiler_params=params("attend_back"),
        cost_estimate=cost(10e9, 12e6),
        name="attend_back",
    )(place, lse, grows, w, proj, n1, mixed, *gots)


def finish_kernel(_, x_ref, gmid_ref, table_ref, *refs):
    gproj, weights, known, sum_proj, sum_up = refs[0:4], refs[4:8], refs[8:12], refs[12:16], refs[16:20]
    out_ref, keep_ref, away_ref, gain_sum, shift_sum = refs[20:]
    start_sums(gain_sum, shift_sum)
    grad = None
    for g, w in zip(gproj, weights):
        term = dot_nt(g[...], w[...])
        grad = term if grad is None else grad + term
    unit, spread = unit_rows(x_ref[...].astype(F32))
    add_sum(gain_sum, grad * unit)
    add_sum(shift_sum, grad)
    back = norm_back(grad, unit, spread, table_ref[GAIN_ATTN])
    out_ref[...] = (gmid_ref[...] + back).astype(BF)

    @pl.when(pl.program_id(0) == pl.num_programs(0) - 1)
    def _():
        shared = jnp.concatenate(
            [r[...] for r in known] + [gain_sum[...], shift_sum[...]], axis=1
        )
        for dy in range(2):
            for dc, ref in enumerate((keep_ref, away_ref)):
                row = jnp.concatenate([shared, sum_proj[2 * dy + dc][...], sum_up[2 * dy + dc][...]], axis=1)
                ref[dy : dy + 1] = row


def finish_call(place, x, gmid, table, gproj, weights, known, sum_proj, sum_up):
    rows, d = x.shape
    tile = 256
    by_rows = pl.BlockSpec((tile, d), lambda i: (i, 0))
    width = 6 * d + sum_proj[0].shape[1] + sum_up[0].shape[1]
    return pl.pallas_call(
        finish_kernel,
        grid=(rows // tile,),
        in_specs=[pl.BlockSpec(memory_space=pltpu.SMEM), by_rows, by_rows, whole(table.shape)]
        + [pl.BlockSpec((tile, 640), lambda i: (i, 0))] * 4
        + [pl.BlockSpec((d, 640), lambda i: (0, 0))] * 4
        + [whole(v.shape) for v in (*known, *sum_proj, *sum_up)],
        out_specs=[by_rows, whole((2, width)), whole((2, width))],
        out_shape=[jax.ShapeDtypeStruct((rows, d), BF)] + [jax.ShapeDtypeStruct((2, width), F32)] * 2,
        scratch_shapes=[pltpu.VMEM((1, d), F32)] * 2,
        compiler_params=params("finish"),
        cost_estimate=cost(2 * 4 * rows * d * 640, 16e6),
        name="finish",
    )(place, x, gmid, table, *gproj, *weights, *known, *sum_proj, *sum_up)


class Links:
    def __init__(self, mesh):
        self.count = mesh.shape["fsdp"] // 2
        places = [
            (z, x, y, c)
            for z in range(self.count)
            for x in range(2)
            for y in range(2)
            for c in range(2)
        ]

        def index(z, x, y, c):
            return ((z * 2 + x) * 2 + y) * 2 + c

        def pairs(move):
            return [(index(*p), index(*move(*p))) for p in places]

        self.core = pairs(lambda z, x, y, c: (z, x, y, 1 - c))
        self.y = pairs(lambda z, x, y, c: (z, x, 1 - y, c))
        self.x = pairs(lambda z, x, y, c: (z, 1 - x, y, c))
        self.ring = pairs(lambda z, x, y, c: ((z + 1) % self.count, x, y, c))
        self.far = [
            pairs(lambda z, x, y, c, k=k: ((z + k) % self.count, x, y, c)) for k in range(self.count)
        ]
        self.back = [
            pairs(lambda z, x, y, c, k=k: ((z - k) % self.count, x, y, c)) for k in range(self.count)
        ]
        self.xy = pairs(lambda z, x, y, c: (z, 1 - x, 1 - y, c))
        self.trees = []
        step = 1
        while step < self.count:
            size = 4 if step * 4 <= self.count else 2
            self.trees.append(
                [pairs(lambda z, x, y, c, b=step * k: (z ^ b, x, y, c)) for k in range(1, size)]
            )
            step *= size

    @staticmethod
    def send(value, pairs):
        return lax.ppermute(value, AXES, pairs)


def plus(*terms, kind=BF):
    total = terms[0].astype(F32)
    for term in terms[1:]:
        total = total + term.astype(F32)
    return total.astype(kind)


def tie(value, *others):
    return lax.optimization_barrier((value, others))[0]


def ring_from(links, first):
    held = [first]
    for _ in range(links.count - 1):
        held.append(links.send(held[-1], links.ring))
    return held


def gather_and_attend(links, place, attn, up, down, n1, smalls, layer_input, table):
    n = links.count
    half = n // 2
    small_y = links.send(smalls, links.y)

    near = [jnp.stack([attn, down])]
    done = (n1,)
    for k in range(1, n):
        now = near[-1] if k == 1 else tie(near[-1], *done)
        near.append(links.send(now, links.ring))
        if k == 3:
            steps.append(links.send(tie(steps[0], near[2]), links.ring))
        done = (near[-1],)
        if k == 1:
            pair = jnp.stack([up, links.send(up, links.x)])
            done += (pair, n1, smalls)
        if k == 2:
            steps = [jnp.stack([pair, links.send(pair, links.y)])]
            done += (steps[0], small_y)
        if k == half:
            lines = [jnp.stack([v[0] for v in near[:half]])]
            others = [links.send(lines[0], links.x)]
            done += (others[0],)
        if k == half + 1:
            quads = [links.send(tie(jnp.stack([lines[0], others[0]]), *near[half:-1]), links.y)]
            smalls = [smalls, links.send(smalls, links.core), small_y, links.send(small_y, links.core)]
            done += (smalls[1], smalls[3], quads[0])

    lines.append(tie(jnp.stack([v[0] for v in near[half:]]), *done))
    others.append(links.send(lines[1], links.x))
    line = jnp.stack([v[1] for v in near])
    beyond = [links.send(tie(line, *done), links.y)]
    steps.append(links.send(tie(steps[-1], *done), links.ring))
    core = lambda values: [links.send(v, links.core) for v in values]

    def from_lines(*pair):
        return [(v[k // half], (k % half,)) for v in pair for k in range(n)]

    def from_quads(quads):
        return [(quads[k // half], (dx, k % half)) for dx in range(2) for k in range(n)]

    quads.append(links.send(jnp.stack([lines[1], others[1]]), links.y))
    far = links.send(tie(line, others[1]), links.x)

    attn_w, proj, mixed, lse = [], [], [], []

    def attend(pieces, *before):
        j = len(proj)
        w, p, m, s = attend_call(tie(place, *before) if before else place, n1, pieces, smalls[j])
        attn_w.append(w)
        proj.append(p)
        mixed.append(m)
        lse.append(s)

    attend(from_lines(lines, others))
    attend(from_lines(core(lines), core(others)), mixed[0])
    quads_core = core([quads[0], tie(quads[1], mixed[1])])
    beyond.append(links.send(tie(beyond[0], far), links.x))
    for _ in range(3, n):
        steps.append(links.send(tie(steps[-1], mixed[1]), links.ring))
    attend(from_quads(quads), mixed[1], quads[1], far, steps[2])
    attend(from_quads(quads_core), mixed[2])
    middle, n2 = middle_call(layer_input, table, mixed, attn_w)

    steps[-1] = tie(steps[-1], mixed[3])
    up_core = core(steps)
    up_w = [[(v, (dy, dx)) for dx in range(2) for v in vs] for dy in range(2) for vs in (steps, up_core)]
    down_w = [
        [(v, (k,)) for v in vs for k in range(n)]
        for pair in ((line, far), beyond)
        for vs in (pair, core(pair))
    ]
    return attn_w, up_w, down_w, proj, mixed, lse, smalls, middle, n2


def spread_sum(links, home):
    got = [links.send(home[k], links.far[k]) for k in range(1, links.count)]
    return plus(home[0], *got, kind=F32)


def sum_near(links, keep, away):
    rows = keep + links.send(away, links.core)
    near, far = rows[0:1], rows[1:2]
    return (near + links.send(near, links.x)) + (
        links.send(far, links.y) + links.send(far, links.xy)
    )


def sum_far(links, total):
    for pairs in links.trees:
        got = [total] + [links.send(total, p) for p in pairs]
        while len(got) > 1:
            got = [got[i] + got[i + 1] for i in range(0, len(got), 2)]
        total = got[0]
    return total


def pack_attn(w_qkv, w_out):
    q, k, v, o = w_qkv[:, 0], w_qkv[:, 1], w_qkv[:, 2], w_out.T
    return jnp.concatenate(
        [q[:, :128], k[:, :128], v[:, :128], q[:, 128:], v[:, 128:], k[:, 128:], o[:, 128:], o[:, :128]],
        axis=1,
    )


def unpack_attn(g):
    q = jnp.concatenate([g[:, 0:128], g[:, 384:448]], axis=1)
    k = jnp.concatenate([g[:, 128:256], g[:, 512:576]], axis=1)
    v = jnp.concatenate([g[:, 256:384], g[:, 448:512]], axis=1)
    o = jnp.concatenate([g[:, 640:768], g[:, 576:640]], axis=1)
    return jnp.stack([q, k, v], axis=1), o.T


def body(
    links,
    layer_input,
    w_qkv,
    bias_qv,
    w_out,
    bias_out,
    gain_attn,
    shift_attn,
    gain_mlp,
    shift_mlp,
    w_up,
    bias_up,
    w_down,
    bias_down,
    cotangent,
):
    fsdp = lax.axis_index("fsdp")
    place = jnp.stack([fsdp // 2, fsdp % 2]).astype(jnp.int32)
    count = links.count
    n1, sum_down, small, table = start_call(
        layer_input,
        cotangent,
        bias_qv,
        bias_up,
        (bias_out, gain_attn, shift_attn, gain_mlp, shift_mlp, bias_down),
    )
    attn_w, up_w, down_w, proj, mixed, lse, smalls, middle, n2 = gather_and_attend(
        links, place, pack_attn(w_qkv, w_out), w_up, w_down.T, n1, small, layer_input, table
    )

    hidden, pre, sum_up = [None] * 4, [None] * 4, [None] * 4
    up_home, up_away, down_sum = [None] * 2, [None] * 2, [None] * 2
    gots = [None] * 4
    for j in (1, 3, 0, 2):
        out = feed_call(
            place, count, n2, cotangent, up_w[j], down_w[j], smalls[j], gots[j]
        )
        hidden[j], pre[j], sum_up[j], up_w[j], down_w[j] = out[0:5]
        if j % 2:
            gots[j - 1] = links.send(out[5], links.core)
        else:
            up_home[j // 2], up_away[j // 2], down_sum[j // 2] = out[5:8]

    got_x0 = links.send(up_away[0], links.x)
    got_x1 = links.send(up_away[1], links.x)
    got_down = links.send(down_sum[1], links.y)
    gmid, grows, gain_two, shift_two, sum_out = turn_call(
        place, middle, cotangent, table, pre, up_w
    )

    gproj, sum_proj = [None] * 4, [None] * 4
    attn_home, attn_away = [None] * 2, [None] * 2

    def back(j, got, *before):
        out = attend_back_call(
            tie(place, *before) if before else place,
            count,
            grows,
            n1,
            attn_w[j],
            proj[j],
            mixed[j],
            lse[j],
            got,
        )
        gproj[j], sum_proj[j] = out[0:2]
        if j % 2:
            return links.send(out[2], links.core)
        attn_home[j // 2], attn_away[j // 2] = out[2:4]

    got_three = back(3, None, got_x0)
    up_beyond = plus(up_home[1], got_x1)
    got_up = links.send(up_beyond, links.y)
    got_one = back(1, None, up_beyond)
    down_away = plus(down_sum[0][count:], got_down[count:])
    got_x = links.send(down_away, links.x)
    back(2, got_three, down_away)
    got_a1 = links.send(attn_away[1], links.x)
    up_all = plus(up_home[0], got_x0, got_up)
    down_all = plus(down_sum[0][:count], got_down[:count], got_x)
    back(0, got_one, up_all, down_all, sum_proj[2])
    grad_up = spread_sum(links, up_all)
    grad_down = spread_sum(links, down_all)
    got_a0 = links.send(attn_away[0], links.x)
    attn_beyond = plus(attn_home[1], got_a1)
    got_attn = links.send(attn_beyond, links.y)
    grad_input, keep, away = finish_call(
        tie(place, attn_beyond, grad_up),
        layer_input,
        gmid,
        table,
        gproj,
        attn_w,
        (sum_out, sum_down, gain_two, shift_two),
        sum_proj,
        sum_up,
    )
    attn_all = plus(tie(attn_home[0], keep), got_a0, got_attn)
    parts = [attn_all[0]] + [links.send(attn_all[k], links.far[k]) for k in range(1, count)]
    total = sum_near(links, keep, tie(away, attn_all))
    before = (total, attn_all, grad_up, grad_down)
    layer_output = output_call(tie(place, *before), middle, table, hidden, down_w)
    sums = sum_far(links, tie(total, layer_output, parts[1]))
    grad_attn = plus(*parts, kind=F32)

    d = layer_input.shape[1]
    heads = bias_qv.shape[1]
    vec = sums[0]
    total_out, total_down, gain_two, shift_two, gain_one, shift_one = (
        vec[i * d : (i + 1) * d] for i in range(6)
    )
    own = vec[6 * d :]
    total_qv = jnp.stack(
        [
            jnp.concatenate([own[0:128], own[384:448]]),
            jnp.concatenate([own[256:384], own[448:512]]),
        ]
    )
    total_up = own[640:]

    shard_qkv, shard_out = unpack_attn(grad_attn)
    return (
        layer_output,
        grad_input,
        shard_qkv,
        total_qv,
        shard_out,
        total_out,
        gain_one,
        shift_one,
        gain_two,
        shift_two,
        grad_up,
        total_up,
        grad_down.T,
        total_down,
    )


def solution(mesh):
    tokens = P(("fsdp", "tp"), None)
    placed = (
        tokens,
        P("fsdp", None, "tp"),
        P(None, "tp"),
        P("tp", "fsdp"),
        P(),
        P(),
        P(),
        P(),
        P(),
        P("fsdp", "tp"),
        P("tp"),
        P("tp", "fsdp"),
        P(),
        tokens,
    )
    return jax.shard_map(
        functools.partial(body, Links(mesh)),
        mesh=mesh,
        in_specs=placed,
        out_specs=(
            tokens,
            tokens,
            P("fsdp", None, "tp"),
            P(None, "tp"),
            P("tp", "fsdp"),
            P(),
            P(),
            P(),
            P(),
            P(),
            P("fsdp", "tp"),
            P("tp"),
            P("tp", "fsdp"),
            P(),
        ),
        check_vma=False,
    )
```
